128 devices in a mesh: frame: 16 (over y, x), head: 4 (over z), fsdp: 2 (over core).
Axes of the slice: x: 4, y: 4, z: 4, core: 2. Of those that a mesh axis runs over, the one named last changes fastest.
Arguments:
- history: bfloat16 [64, 16, 8, 256], P('frame'), may hold values from -6 to 6
- section: bfloat16 [2048, 64], P('frame'), may hold values from -6 to 6
- slab_kernel: int32 [16], replicated, may hold values from 0 to 2, as said below
- patch_fine: bfloat16 [64, 3072], P(None, ('head', 'fsdp')), may hold values from -0.75 to 0.75
- patch_mid: bfloat16 [512, 3072], P(None, ('head', 'fsdp')), may hold values from -0.25 to 0.25
- patch_coarse: bfloat16 [4096, 3072], P(None, ('head', 'fsdp')), may hold values from -0.09375 to 0.09375
- modulation: float32 [2, 3072], replicated, may hold values from -3 to 3
- w_qkv: bfloat16 [3, 3072, 3072], P(None, None, ('head', 'fsdp')), may hold values from -0.109375 to 0.109375
Outputs:
- attended: bfloat16 [2048, 3072], P('frame', ('head', 'fsdp'))
The draws below stay inside these ranges and needn't reach their ends.
Inputs may be any that keep to these rules, and one draw needn't show every extreme that they name: `slab_kernel`: exactly one slab takes kernel 0, exactly 8 slabs take kernel 2, the others take kernel 1.
All inputs are finite; a program needn't handle non-finite values.
Results may differ from the reference program's by a relative error of at most 0.0034.
Values may be sent and summed in bfloat16 or wider, within the bound.
No kernel may reach another device: no remote copies, remote signals or barrier semaphores. Data moves between devices by JAX's collectives and lax.ppermute only.
A program may use at most 192 MiB of HBM per device.

```python
import jax
import jax.numpy as jnp
import numpy as np
from jax import lax

D = 3072
HEADS = 24
HEAD_DIM = 128
CHANNELS = 16
ROPE_T = 16
ROPE_H = 56
ROPE_W = 56
LH = 8
LW = 256
SLAB_LEN = 4
SLABS = 16
HIST_FRAMES = 64
SEC_TOK = 2048


def draw_slab_kernel(key, part):
    key = jax.random.fold_in(key, 7)
    draw_order = jax.random.permutation(key, SLABS)
    coarse_end = 1 + SLABS // 2
    return jnp.where(draw_order == 0, 0, jnp.where(draw_order < coarse_end, 2, 1)).astype(jnp.int32)


def levels(own_key, shape, cuts, smallest, high):
    def one(position, shards_of):
        steps = jax.random.uniform(jax.random.fold_in(jax.random.fold_in(own_key, 6), position), (shards_of,), jnp.float32, smallest / len(cuts), high / len(cuts))
        return jnp.repeat(jnp.exp(steps), shape[position] // shards_of).reshape((-1,) + (1,) * (len(shape) - position - 1))

    gain = one(*cuts[0])
    for cut in cuts[1:]:
        gain = gain * one(*cut)
    return gain


def gaussian(own_key, shape, scale, limit, shards=(), kind=jnp.bfloat16):
    factor_of = levels(own_key, shape, shards, -0.22, 0.18) if shards else 1.0
    values = jax.random.normal(own_key, shape, jnp.float32) * scale * factor_of
    return jnp.minimum(jnp.maximum(values, -limit), limit).astype(kind)


def setup_inputs(seed: int = 0) -> dict:
    streams_of = jax.random.split(jax.random.key(seed), 9)
    history = gaussian(streams_of[0], (HIST_FRAMES, CHANNELS, LH, LW), 1.0, 6.0, ((0, 16),))
    section = gaussian(streams_of[1], (SEC_TOK, CHANNELS * 4), 1.0, 6.0, ((0, 16),))
    slab_kernel = draw_slab_kernel(jax.random.fold_in(streams_of[8], 71), 0)
    patch_fine = gaussian(streams_of[3], (CHANNELS * 4, D), (CHANNELS * 4) ** -0.5, 0.75, ((1, 8),))
    patch_mid = gaussian(streams_of[4], (CHANNELS * 32, D), (CHANNELS * 32) ** -0.5, 0.25, ((1, 8),))
    patch_coarse = gaussian(streams_of[5], (CHANNELS * 256, D), (CHANNELS * 256) ** -0.5, 0.09375, ((1, 8),))
    modulation = gaussian(streams_of[6], (2, D), 0.5, 3.0, (), jnp.float32)
    w_qkv = gaussian(streams_of[7], (3, D, D), D ** -0.5, 0.109375, ((2, 8),))
    return dict(history=history, section=section, slab_kernel=slab_kernel, patch_fine=patch_fine, patch_mid=patch_mid, patch_coarse=patch_coarse, modulation=modulation, w_qkv=w_qkv)


THETA = 256.0
EPS = 1e-06

def rotary_tables():
    widths = (ROPE_T, ROPE_H, ROPE_W)
    axis_list, freq_list, partner_list, sign_list = ([], [], [], [])
    offset = 0
    for axis_id, part_width in enumerate(widths):
        half_width = part_width // 2
        for column in range(part_width):
            pair_id = column % half_width
            axis_list.append(axis_id)
            freq_list.append(THETA ** (-2.0 * pair_id / part_width))
            if column < half_width:
                partner_list.append(offset + column + half_width)
                sign_list.append(-1.0)
            else:
                partner_list.append(offset + column - half_width)
                sign_list.append(1.0)
        offset += part_width
    return (np.array(axis_list, np.int32), np.array(freq_list, np.float32), np.array(partner_list, np.int32), np.array(sign_list, np.float32))

def rotate(vectors, positions):
    axis_of, frequency, partner, sign_of = rotary_tables()
    angles = jnp.take(positions, axis_of, axis=1) * frequency
    cosine = jnp.cos(angles)[:, None, :]
    sine_part = (jnp.sin(angles) * sign_of)[:, None, :]
    return vectors * cosine + jnp.take(vectors, partner, axis=2) * sine_part

def rms_norm(vectors):
    return vectors * lax.rsqrt(lax.optimization_barrier(jnp.mean(vectors * vectors, axis=-1, keepdims=True)) + EPS)

def patchify(slab_cells, step_t, step_h, step_w):
    frames_in, channel_count, rows_in, cols_in = slab_cells.shape
    blocks = slab_cells.reshape(frames_in // step_t, step_t, channel_count, rows_in // step_h, step_h, cols_in // step_w, step_w)
    blocks = blocks.transpose(0, 3, 5, 2, 1, 4, 6)
    return blocks.reshape(frames_in // step_t * (rows_in // step_h) * (cols_in // step_w), channel_count * step_t * step_h * step_w)

def slab_features(slab_cells, kernel_index, weights, capacity):

    def make_branch(stride, weight):

        def branch(cells):
            tokens = patchify(cells, stride, 2 * stride, 2 * stride)
            product = jnp.dot(tokens, weight, preferred_element_type=jnp.float32)
            product = jnp.pad(product, ((0, capacity - product.shape[0]), (0, 0)))
            return product.astype(jnp.bfloat16)
        return branch
    return lax.switch(kernel_index, [make_branch(1, weights[0]), make_branch(2, weights[1]), make_branch(4, weights[2])], slab_cells)

def stride_of(kernel_index):
    return jnp.where(kernel_index == 0, 1, jnp.where(kernel_index == 1, 2, 4)).astype(jnp.int32)

def live_count(kernel_index, height, breadth):
    stride = stride_of(kernel_index)
    return SLAB_LEN // stride * (height // (2 * stride)) * (breadth // (2 * stride))

def slab_positions(slab_index, kernel_index, height, breadth, capacity):
    stride = stride_of(kernel_index)
    grid_h = height // (2 * stride)
    grid_w = breadth // (2 * stride)
    row_ids = jnp.arange(capacity, dtype=jnp.int32)
    frame_at = (row_ids // (grid_h * grid_w)).astype(jnp.float32)
    row_at = (row_ids // grid_w % grid_h).astype(jnp.float32)
    col_at = (row_ids % grid_w).astype(jnp.float32)
    factor = stride.astype(jnp.float32)
    pos_t = SLAB_LEN * slab_index.astype(jnp.float32) + factor * frame_at + (factor - 1.0) / 2.0
    pos_h = 2.0 * factor * row_at + factor - 0.5
    pos_w = 2.0 * factor * col_at + factor - 0.5
    return jnp.stack([pos_t, pos_h, pos_w], axis=1)

def section_positions(first_row, row_count, height, breadth, history_frames):
    row_ids = first_row + jnp.arange(row_count, dtype=jnp.int32)
    grid_h = height // 2
    grid_w = breadth // 2
    frame_at = (row_ids // (grid_h * grid_w)).astype(jnp.float32)
    row_at = (row_ids // grid_w % grid_h).astype(jnp.float32)
    col_at = (row_ids % grid_w).astype(jnp.float32)
    pos_t = history_frames + frame_at
    return jnp.stack([pos_t, 2.0 * row_at + 0.5, 2.0 * col_at + 0.5], axis=1)

def modulate(features, modulation):
    values32 = features.astype(jnp.float32)
    centered = values32 - lax.optimization_barrier(jnp.mean(values32, axis=-1, keepdims=True))
    variance = lax.optimization_barrier(jnp.mean(centered * centered, axis=-1, keepdims=True))
    normed = centered * lax.rsqrt(variance + EPS)
    return (normed * (1.0 + modulation[1]) + modulation[0]).astype(jnp.bfloat16)

def reference(history, section, slab_kernel, patch_fine, patch_mid, patch_coarse, modulation, w_qkv):
    capacity = LH * LW
    slabs = history.reshape(SLABS, SLAB_LEN, CHANNELS, LH, LW)
    weights = (patch_fine, patch_mid, patch_coarse)

    def slab_one(pair):
        cells, kernel_index = pair
        return slab_features(cells, kernel_index, weights, capacity)
    hist_feat = lax.map(slab_one, (slabs, slab_kernel)).reshape(SLABS * capacity, D)
    section_feat = jnp.dot(section, patch_fine, preferred_element_type=jnp.float32).astype(jnp.bfloat16)
    features = jnp.concatenate([hist_feat, section_feat], axis=0)
    slab_ids = jnp.arange(SLABS, dtype=jnp.int32)
    lives = live_count(slab_kernel, LH, LW)
    hist_mask = (jnp.arange(capacity, dtype=jnp.int32)[None, :] < lives[:, None]).reshape(-1)
    key_mask = jnp.concatenate([hist_mask, jnp.ones((SEC_TOK,), bool)])
    hist_pos = jax.vmap(lambda slab_index, kernel_index: slab_positions(slab_index, kernel_index, LH, LW, capacity))(slab_ids, slab_kernel).reshape(-1, 3)
    sec_pos = section_positions(jnp.int32(0), SEC_TOK, LH, LW, float(HIST_FRAMES))
    positions = jnp.concatenate([hist_pos, sec_pos], axis=0)
    modulated = modulate(features, modulation)
    total_rows = features.shape[0]
    query_raw = jnp.dot(modulated[SLABS * capacity:], w_qkv[0], preferred_element_type=jnp.float32)
    queries = rotate(rms_norm(query_raw.reshape(SEC_TOK, HEADS, HEAD_DIM)), sec_pos).astype(jnp.bfloat16)
    key_raw = jnp.dot(modulated, w_qkv[1], preferred_element_type=jnp.float32)
    key_rows = rotate(rms_norm(key_raw.reshape(total_rows, HEADS, HEAD_DIM)), positions).astype(jnp.bfloat16)
    values = jnp.dot(modulated, w_qkv[2], preferred_element_type=jnp.float32).astype(jnp.bfloat16)
    values = values.reshape(total_rows, HEADS, HEAD_DIM)
    score_scale = HEAD_DIM ** (-0.5)

    def per_head(triple):
        query_head, key_head, value_head = triple
        scores = jnp.dot(query_head, key_head.T, preferred_element_type=jnp.float32) * score_scale
        weights_full = jnp.where(key_mask[None, :], jnp.exp(scores), 0.0)
        denominator = lax.optimization_barrier(jnp.sum(weights_full, axis=1))
        numerator = jnp.dot(weights_full.astype(jnp.bfloat16), value_head, preferred_element_type=jnp.float32)
        return numerator / denominator[:, None]
    attended = lax.map(per_head, (queries.transpose(1, 0, 2), key_rows.transpose(1, 0, 2), values.transpose(1, 0, 2)))
    return attended.transpose(1, 0, 2).reshape(SEC_TOK, D).astype(jnp.bfloat16)
```

```python
import functools

import jax
import jax.numpy as jnp
import numpy as np
from jax import lax
from jax.experimental import pallas as pl
from jax.experimental.pallas import tpu as pltpu
from jax.sharding import PartitionSpec as P

HEAD_DIM = 128
PARTS = (16, 56, 56)
THETA = 256.0
EPS = 1e-06
QUERY_SCALE = float(np.log2(np.e) * HEAD_DIM**-0.5)
BF = jnp.bfloat16
F32 = jnp.float32
VMEM = pl.BlockSpec(memory_space=pltpu.VMEM)
SMEM = pl.BlockSpec(memory_space=pltpu.SMEM)


def params(mib=48):
    return pltpu.CompilerParams(vmem_limit_bytes=mib * 2**20)


def cost(flops, bytes_accessed, transcendentals=0):
    return pl.CostEstimate(
        flops=int(flops), bytes_accessed=int(bytes_accessed), transcendentals=int(transcendentals)
    )


def pair_tables():
    freqs = np.zeros((3, 64), np.float64)
    first, second = [], []
    pair, offset = 0, 0
    for axis, width in enumerate(PARTS):
        half = width // 2
        for i in range(half):
            freqs[axis, pair] = THETA ** (-2.0 * i / width)
            first.append(offset + i)
            second.append(offset + i + half)
            pair += 1
        offset += width
    return freqs, np.array(first + second)


def section_tables(frames, per_frame):
    freqs, _ = pair_tables()
    rows = np.arange(frames * per_frame)
    pos = np.stack(
        [4.0 * frames + rows // 512, 2.0 * (rows // 128 % 4) + 0.5, 2.0 * (rows % 128) + 0.5]
    )
    angles = freqs.T @ pos
    return np.cos(angles).astype(np.float32), np.sin(angles).astype(np.float32)


def head_permutation():
    _, order = pair_tables()
    perm = np.zeros((HEAD_DIM, HEAD_DIM), np.float32)
    perm[order, np.arange(HEAD_DIM)] = 1.0
    return perm


def lane_frequencies():
    freqs, _ = pair_tables()
    table = np.zeros((8, HEAD_DIM), np.float32)
    table[:3] = np.concatenate([freqs, freqs], axis=1)
    table[3] = np.concatenate([-np.ones(64), np.ones(64)])
    return table


def dot(a, b, dims=((1,), (0,))):
    return lax.dot_general(a, b, (dims, ((), ())), preferred_element_type=F32)


def select_columns(rows, columns, source):
    j = lax.broadcasted_iota(jnp.int32, (8, columns), 1)[0:1]
    i = lax.broadcasted_iota(jnp.int32, (rows, columns), 0)
    return jnp.where(i == source(j), 1.0, 0.0).astype(BF)


def select_rows(rows, columns, source):
    j = lax.broadcasted_iota(jnp.int32, (rows, columns), 1)
    i = lax.broadcasted_iota(jnp.int32, (rows, 128), 0)[:, 0:1]
    return jnp.where(j == source(i), 1.0, 0.0).astype(BF)


def split(value):
    high = value.astype(BF)
    return high, (value - high.astype(F32)).astype(BF)


def prepare_kernel(kinds_ref, hist_ref, sec_ref, out_ref):
    kind = kinds_ref[lax.axis_index("frame")]
    cells = hist_ref[...]

    own = select_rows(64, 64, lambda i: (i & 31) * 2 + (i >> 5))
    section = dot(own, sec_ref[...], ((1,), (1,))).astype(BF)
    for d in range(16):
        out_ref[d, 64:128, :] = section

    @pl.when(kind == 0)
    def _():
        cols = select_columns(256, 256, lambda j: (j & 127) * 2 + (j >> 7))
        rows = select_rows(
            512,
            512,
            lambda i: (i >> 7) * 128 + ((i >> 1) & 15) * 8 + ((i >> 5) & 3) * 2 + (i & 1),
        )
        out = dot(rows, dot(cells, cols).astype(BF)).astype(BF)
        for d in range(16):
            for w in range(2):
                out_ref[d, 32 * w : 32 * w + 32, :] = out[
                    32 * d : 32 * d + 32, 128 * w : 128 * w + 128
                ]

    @pl.when(kind == 1)
    def _():
        cols = select_columns(256, 256, lambda j: (j & 63) * 4 + (j >> 6))
        lanes = select_columns(
            512,
            512,
            lambda j: ((j >> 8) * 2 + ((j >> 2) & 1)) * 128
            + ((j >> 3) & 15) * 8
            + ((j >> 7) & 1) * 4
            + (j & 3),
        )
        out = dot(dot(cells, cols).astype(BF), lanes, ((0,), (0,))).astype(BF)
        for d in range(16):
            g, q = d // 4, d % 4
            for w in range(4):
                out_ref[d, 16 * w : 16 * w + 16, :] = out[
                    64 * w + 16 * q : 64 * w + 16 * q + 16, 128 * g : 128 * g + 128
                ]

    @pl.when(kind == 2)
    def _():
        lanes = select_columns(
            512, 512, lambda j: ((j >> 3) & 3) * 128 + (j >> 5) * 8 + (j & 7)
        )
        out = dot(cells, lanes, ((0,), (0,))).astype(BF)
        for d in range(16):
            for g in range(4):
                out_ref[d, 16 * g : 16 * g + 16, :] = out[
                    16 * d : 16 * d + 16, 128 * g : 128 * g + 128
                ]


def prepare(kinds, history, section):
    return pl.pallas_call(
        prepare_kernel,
        out_shape=jax.ShapeDtypeStruct((16, 128, 128), BF),
        in_specs=[SMEM, VMEM, VMEM],
        out_specs=VMEM,
        compiler_params=params(),
        cost_estimate=cost(1e9, 1e6),
        name="prepare",
    )(kinds, history.reshape(512, 256), section)


def embed_kernel(kinds_ref, recv_ref, mid_ref, coarse_ref, out_ref, mid_buf, coarse_buf):
    mid_count = jnp.int32(0)
    coarse_count = jnp.int32(0)
    for s in range(16):
        kind = kinds_ref[s]
        block = recv_ref[s, 0:64, :]
        mid_buf[jnp.where(kind == 1, jnp.minimum(mid_count, 6), 7)] = block
        coarse_buf[jnp.where(kind == 2, jnp.minimum(coarse_count, 7), 8)] = block
        mid_count += jnp.where(kind == 1, 1, 0)
        coarse_count += jnp.where(kind == 2, 1, 0)
    tokens = jnp.concatenate(
        [mid_buf[0:7, 16 * w : 16 * w + 16, :].reshape(112, 128) for w in range(4)], axis=1
    )
    order = select_columns(512, 512, lambda j: (j & 3) * 128 + (j >> 2))
    tokens = dot(tokens, order).astype(BF)
    out_ref[0:112, :] = dot(tokens, mid_ref[...]).astype(BF)
    cells = coarse_buf[0:8].reshape(512, 128)
    order = select_rows(
        512,
        512,
        lambda i: ((i >> 1) & 7) * 64 + (i >> 7) * 16 + (i & 1) * 8 + ((i >> 4) & 7),
    )
    cells = dot(order, cells).astype(BF)
    tokens = jnp.concatenate(
        [
            jnp.concatenate(
                [cells[128 * g + 16 * w : 128 * g + 16 * w + 16] for w in range(8)], axis=1
            )
            for g in range(4)
        ],
        axis=0,
    )
    order = select_columns(1024, 1024, lambda j: (j & 7) * 128 + (j >> 3))
    tokens = dot(tokens, order).astype(BF)
    total = jnp.zeros((16, out_ref.shape[1]), F32)
    for g in range(4):
        total += dot(tokens[16 * g : 16 * g + 16], coarse_ref[1024 * g : 1024 * g + 1024, :])
    out_ref[112:128, :] = total.astype(BF)


def embed(kinds, received, patch_mid, patch_coarse):
    return pl.pallas_call(
        embed_kernel,
        out_shape=jax.ShapeDtypeStruct((128, patch_mid.shape[1]), BF),
        in_specs=[SMEM, VMEM, VMEM, VMEM],
        out_specs=VMEM,
        scratch_shapes=[pltpu.VMEM((8, 64, 128), BF), pltpu.VMEM((9, 64, 128), BF)],
        compiler_params=params(),
        cost_estimate=cost(2e9, 5e6),
        name="embed",
    )(kinds, received, patch_mid, patch_coarse)


def gather_columns(block):
    rings = [block] + [
        lax.ppermute(block, "head", [(i, (i + d) % 4) for i in range(4)]) for d in (1, 3, 2)
    ]
    same = jnp.stack([rings[0], rings[1], rings[3], rings[2]])
    other = lax.ppermute(same, "fsdp", [(0, 1), (1, 0)])
    return same, other


def place_columns(same_ref, other_ref, full_ref):
    z, core = lax.axis_index("head"), lax.axis_index("fsdp")
    width = same_ref.shape[2]
    for d in range(4):
        at = ((z + 4 - d) & 3) * 2
        for ref, column in ((same_ref, at + core), (other_ref, at + 1 - core)):
            full_ref[:, pl.ds(pl.multiple_of(column * width, 128), width)] = ref[d]


def fold_kernel(same_ref, other_ref, mod_ref, w_ref, perm_ref, fold_ref, gram_ref, full_ref):
    place_columns(same_ref, other_ref, full_ref)
    order = select_rows(64, 64, lambda i: (i & 31) * 2 + (i >> 5))
    raw = full_ref[...]
    width = raw.shape[1]
    weight = dot(order, raw)
    low = weight.astype(BF)
    mean = jnp.sum(weight, axis=1, keepdims=True) / width
    mean_row = dot(jnp.ones((8, width), BF), low, ((1,), (1,)))[0:1] / width
    gram_ref[...] = dot(low, low, ((1,), (1,))) / width - mean * mean_row
    scaled = (weight - mean) * (1.0 + mod_ref[1:2, :])
    shift_high, shift_low = split(mod_ref[0:1, :])
    pad = jnp.zeros((14, width), BF)
    high, rest = split(scaled)
    left = jnp.concatenate(
        [high, rest, jnp.concatenate([shift_high, shift_low, pad], axis=0)], axis=0
    )
    for part in range(3):
        product = dot(left, w_ref[part])
        matrix = product[0:64] + product[64:128]
        bias = product[128:129] + product[129:130]
        columns = matrix.shape[1]
        high, rest = split(matrix)
        bias_high, bias_low = split(bias)
        rows = jnp.concatenate(
            [
                high.astype(F32),
                rest.astype(F32),
                bias_high.astype(F32),
                bias_high.astype(F32),
                bias_low.astype(F32),
                jnp.zeros((13, columns), F32),
            ],
            axis=0,
        ).astype(BF)
        if part < 2:
            rows = jnp.concatenate(
                [
                    dot(rows[:, HEAD_DIM * h : HEAD_DIM * (h + 1)], perm_ref[...]).astype(BF)
                    for h in range(columns // HEAD_DIM)
                ],
                axis=1,
            )
        fold_ref[part] = rows


def fold(same, other, modulation, w_qkv, perm):
    width, columns = w_qkv.shape[1], w_qkv.shape[2]
    return pl.pallas_call(
        fold_kernel,
        out_shape=(
            jax.ShapeDtypeStruct((3, 144, columns), BF),
            jax.ShapeDtypeStruct((64, 64), F32),
        ),
        in_specs=[VMEM] * 5,
        out_specs=(VMEM, VMEM),
        scratch_shapes=[pltpu.VMEM((64, width), BF)],
        compiler_params=params(),
        cost_estimate=cost(2e9, 8e6),
        name="fold",
    )(same, other, modulation, w_qkv, perm)


def turn_rows(keys, cosine, sine):
    return keys * cosine + pltpu.roll(keys, 64, 1) * sine


def row_angles(kinds_ref, freq_ref):
    me = lax.axis_index("frame")
    row = lax.broadcasted_iota(jnp.int32, (128, 128), 0)
    slot = row >> 4
    slab = jnp.zeros((128, 128), F32)
    mid_count = jnp.int32(0)
    coarse_count = jnp.int32(0)
    fine_slab = jnp.int32(0)
    coarse_slot = jnp.where(slot == 7, (row >> 1) & 7, -1)
    for s in range(16):
        kind = kinds_ref[s]
        is_mid, is_coarse = kind == 1, kind == 2
        slab = jnp.where(slot == jnp.where(is_mid, mid_count, 99), float(s), slab)
        slab = jnp.where(coarse_slot == jnp.where(is_coarse, coarse_count, 99), float(s), slab)
        mid_count += jnp.where(is_mid, 1, 0)
        coarse_count += jnp.where(is_coarse, 1, 0)
        fine_slab += jnp.where(kind == 0, s, 0)
    coarse = slot == 7
    whole = me.astype(F32)
    block = (me >> 2).astype(F32)
    quarter = (me & 3).astype(F32)
    frame_half = (me >> 3).astype(F32)
    row_half = ((me >> 2) & 1).astype(F32)
    at = (row & 15).astype(F32)
    t = 4.0 * slab + jnp.where(coarse, 1.5, 2.0 * frame_half + 0.5)
    h = jnp.where(coarse, 3.5, 4.0 * row_half + 1.5)
    w = jnp.where(
        coarse,
        8.0 * (2.0 * whole + (row & 1).astype(F32)) + 3.5,
        4.0 * (16.0 * quarter + at) + 1.5,
    )
    freq_t, freq_h, freq_w, sign = (freq_ref[i : i + 1, :] for i in range(4))
    angles = t * freq_t + h * freq_h + w * freq_w
    fine_t = 4.0 * fine_slab.astype(F32) + block
    fine_angles = (
        fine_t * freq_t
        + (2.0 * quarter + 0.5) * freq_h
        + (2.0 * row.astype(F32) + 0.5) * freq_w
    )
    return (
        (jnp.cos(angles), jnp.sin(angles) * sign),
        (jnp.cos(fine_angles), jnp.sin(fine_angles) * sign),
        fine_slab,
    )


def query_kernel(
    kinds_ref,
    recv_ref,
    fold_ref,
    gram_ref,
    cos_ref,
    sin_ref,
    freq_ref,
    query_ref,
    own_ref,
    key_ref,
    value_ref,
    table_ref,
    patch_ref,
    scale_ref,
):
    (cos_far, sin_far), (cos_fine, sin_fine), fine_slab = row_angles(kinds_ref, freq_ref)
    table_ref[0] = cos_far
    table_ref[1] = sin_far
    count = query_ref.shape[1]
    heads = query_ref.shape[0] // HEAD_DIM
    patches = jnp.concatenate(
        [recv_ref[f, 64:128, :] for f in range(16)] + [recv_ref[fine_slab, 0:64, :]], axis=1
    )
    one, rest = split(gram_ref[...])
    two, three = split(gram_ref[...] - one.astype(F32))
    gram = jnp.concatenate([one, two, three], axis=1)
    spread = dot(gram, jnp.concatenate([patches, patches, patches], axis=0))
    variance = jnp.sum(spread * patches.astype(F32), axis=0, keepdims=True)
    variance = jnp.maximum(variance, 0.0) + EPS
    deviation = jnp.sqrt(variance)
    dev_high, dev_low = split(deviation)
    rows = lax.broadcasted_iota(jnp.int32, (16, patches.shape[1]), 0)
    extra = jnp.where(
        rows == 1,
        dev_low.astype(F32),
        jnp.where((rows == 0) | (rows == 2), dev_high.astype(F32), 0.0),
    ).astype(BF)
    patches = jnp.concatenate([patches, patches, extra], axis=0)
    patch_ref[...] = patches[:, 0:count]
    scale_ref[0:1, :] = variance[:, 0:count]
    scale_ref[1:2, :] = lax.rsqrt(variance[:, 0:count])
    for h in range(heads):
        at = slice(HEAD_DIM * h, HEAD_DIM * (h + 1))
        raw = dot(fold_ref[0][:, at], patches[:, 0:count], ((0,), (0,)))
        square = jnp.sum(raw * raw, axis=0, keepdims=True) / HEAD_DIM
        factor = lax.rsqrt(square + EPS * variance[:, 0:count]) * QUERY_SCALE
        a, b = raw[0:64] * factor, raw[64:128] * factor
        cosine, sine = cos_ref[...], sin_ref[...]
        turned = jnp.concatenate([a * cosine - b * sine, b * cosine + a * sine], axis=0)
        query_ref[at, :] = turned.astype(BF)
        me = lax.axis_index("frame")
        own_ref[at, :] = query_ref[at, pl.ds(pl.multiple_of(me * 128, 128), 128)]
    fine = patches[:, count:]
    fine_variance = jnp.transpose(jnp.broadcast_to(variance[:, count:], (128, 128)))
    value_ref[...] = (
        dot(fine, fold_ref[2], ((0,), (0,)))
        * jnp.concatenate([lax.rsqrt(fine_variance)] * heads, axis=1)
    ).astype(BF)
    for h in range(heads):
        at = slice(HEAD_DIM * h, HEAD_DIM * (h + 1))
        raw = dot(fine, fold_ref[1][:, at], ((0,), (0,)))
        square = jnp.sum(raw * raw, axis=1, keepdims=True) / HEAD_DIM
        raw = raw * lax.rsqrt(square + EPS * fine_variance)
        key_ref[:, at] = turn_rows(raw, cos_fine, sin_fine).astype(BF)


def make_queries(kinds, received, folded, gram, cosine, sine, freqs):
    columns = folded.shape[2]
    count = cosine.shape[1]
    return pl.pallas_call(
        query_kernel,
        out_shape=(
            jax.ShapeDtypeStruct((columns, count), BF),
            jax.ShapeDtypeStruct((columns, 128), BF),
            jax.ShapeDtypeStruct((128, columns), BF),
            jax.ShapeDtypeStruct((128, columns), BF),
            jax.ShapeDtypeStruct((2, 128, 128), F32),
            jax.ShapeDtypeStruct((144, count), BF),
            jax.ShapeDtypeStruct((8, count), F32),
        ),
        in_specs=[SMEM] + [VMEM] * 6,
        out_specs=tuple([VMEM] * 7),
        compiler_params=params(),
        cost_estimate=cost(2e9, 8e6),
        name="queries",
    )(kinds, received, folded, gram, cosine, sine, freqs)


def history_kernel(
    same_ref,
    other_ref,
    mod_ref,
    w_ref,
    perm_ref,
    table_ref,
    query_ref,
    key_ref,
    value_ref,
    out_ref,
    full_ref,
):
    place_columns(same_ref, other_ref, full_ref)
    heads = query_ref.shape[0] // HEAD_DIM
    count = query_ref.shape[1]
    x = full_ref[...].astype(F32)
    x = x - jnp.mean(x, axis=1, keepdims=True)
    x = x * lax.rsqrt(jnp.mean(x * x, axis=1, keepdims=True) + EPS)
    x = (x * (1.0 + mod_ref[1:2, :]) + mod_ref[0:1, :]).astype(BF)
    raw_keys = dot(x, w_ref[1])
    values = dot(x, w_ref[2])
    chunk = 512
    sums = []
    for h in range(heads):
        at = slice(HEAD_DIM * h, HEAD_DIM * (h + 1))
        raw = raw_keys[:, at]
        raw = raw * lax.rsqrt(jnp.mean(raw * raw, axis=1, keepdims=True) + EPS)
        high, rest = split(raw)
        raw = dot(high, perm_ref[...]) + dot(rest, perm_ref[...])
        keys = jnp.concatenate(
            [turn_rows(raw, table_ref[0], table_ref[1]).astype(BF), key_ref[:, at]], axis=0
        )
        value_rows = jnp.concatenate([values[:, at], value_ref[:, at].astype(F32)], axis=0)
        value_columns = jnp.transpose(value_rows).astype(BF)
        row_sums = []
        for c in range(count // chunk):
            scores = dot(keys, query_ref[at, chunk * c : chunk * (c + 1)])
            weights = jnp.exp2(scores)
            row_sums.append(jnp.sum(weights, axis=0, keepdims=True))
            part = dot(value_columns, weights.astype(BF)).astype(BF)
            for d in range(chunk // 128):
                out_ref[c * (chunk // 128) + d, at, :] = part[:, 128 * d : 128 * d + 128]
        sums.append(jnp.concatenate(row_sums, axis=1))
    rows = lax.broadcasted_iota(jnp.int32, (16, count), 0)
    tail = jnp.zeros((16, count), F32)
    for h in range(heads):
        high, rest = split(sums[h])
        tail = jnp.where(rows == h, high.astype(F32), tail)
        tail = jnp.where(rows == heads + h, rest.astype(F32), tail)
    tail = tail.astype(BF)
    for d in range(count // 128):
        out_ref[d, HEAD_DIM * heads :, :] = tail[:, 128 * d : 128 * d + 128]


def attend_history(same, other, modulation, w_qkv, perm, table, queries, keys, values):
    columns, count = queries.shape
    return pl.pallas_call(
        history_kernel,
        out_shape=jax.ShapeDtypeStruct((count // 128, columns + 16, 128), BF),
        in_specs=[VMEM] * 9,
        out_specs=VMEM,
        scratch_shapes=[pltpu.VMEM((128, w_qkv.shape[1]), BF)],
        compiler_params=params(),
        cost_estimate=cost(4e9, 1e7, 2e6),
        name="history",
    )(same, other, modulation, w_qkv, perm, table, queries, keys, values)


def section_kernel(patch_ref, scale_ref, fold_ref, own_ref, cos_ref, sin_ref, num_ref, den_ref):
    heads = own_ref.shape[0] // HEAD_DIM
    variance = scale_ref[0:1, :]
    inverse = scale_ref[1:2, :]
    ones = jnp.ones((8, patch_ref.shape[1]), BF)
    for h in range(heads):
        at = slice(HEAD_DIM * h, HEAD_DIM * (h + 1))
        raw = dot(fold_ref[1][:, at], patch_ref[...], ((0,), (0,)))
        square = jnp.sum(raw * raw, axis=0, keepdims=True) / HEAD_DIM
        factor = lax.rsqrt(square + EPS * variance)
        a, b = raw[0:64] * factor, raw[64:128] * factor
        cosine, sine = cos_ref[...], sin_ref[...]
        keys = jnp.concatenate([a * cosine - b * sine, b * cosine + a * sine], axis=0).astype(BF)
        values = (dot(fold_ref[2][:, at], patch_ref[...], ((0,), (0,))) * inverse).astype(BF)
        weights = jnp.exp2(dot(own_ref[at, :], keys, ((0,), (0,)))).astype(BF)
        num_ref[at, :] = dot(values, weights, ((1,), (1,)))
        den_ref[8 * h : 8 * h + 8, :] = dot(ones, weights, ((1,), (1,)))


def attend_section(patches, scales, folded, own, cosine, sine):
    columns = own.shape[0]
    return pl.pallas_call(
        section_kernel,
        out_shape=(
            jax.ShapeDtypeStruct((columns, 128), F32),
            jax.ShapeDtypeStruct((8 * columns // HEAD_DIM, 128), F32),
        ),
        in_specs=[VMEM] * 6,
        out_specs=(VMEM, VMEM),
        compiler_params=params(),
        cost_estimate=cost(4e9, 1e7, 2e6),
        name="section",
    )(patches, scales, folded, own, cosine, sine)


def combine_kernel(part_ref, num_ref, den_ref, out_ref):
    columns = num_ref.shape[0]
    heads = columns // HEAD_DIM
    total = num_ref[...]
    tail = jnp.zeros((16, 128), F32)
    for f in range(part_ref.shape[0]):
        total += part_ref[f, 0:columns, :].astype(F32)
        tail += part_ref[f, columns:, :].astype(F32)
    for h in range(heads):
        at = slice(HEAD_DIM * h, HEAD_DIM * (h + 1))
        denominator = den_ref[8 * h : 8 * h + 1] + tail[h : h + 1] + tail[heads + h : heads + h + 1]
        out_ref[:, at] = jnp.transpose(total[at] / denominator).astype(BF)


def combine(parts, numerator, denominator):
    columns = numerator.shape[0]
    return pl.pallas_call(
        combine_kernel,
        out_shape=jax.ShapeDtypeStruct((128, columns), BF),
        in_specs=[VMEM] * 3,
        out_specs=VMEM,
        compiler_params=params(),
        cost_estimate=cost(1e7, 2e6),
        name="combine",
    )(parts, numerator, denominator)


def per_device(
    history, section, slab_kernel, patch_fine, patch_mid, patch_coarse, modulation, w_qkv
):
    frames = lax.axis_size("frame")
    cos_table, sin_table = section_tables(frames, section.shape[0])
    cosine, sine = jnp.asarray(cos_table), jnp.asarray(sin_table)
    perm = jnp.asarray(head_permutation(), BF)
    freqs = jnp.asarray(lane_frequencies())

    sent = prepare(slab_kernel, history, section)
    received = lax.all_to_all(sent, "frame", 0, 0, tiled=True)
    fine_same, fine_other = gather_columns(patch_fine)
    folded, gram = fold(fine_same, fine_other, modulation, w_qkv, perm)
    features = embed(slab_kernel, received, patch_mid, patch_coarse)
    same, other = gather_columns(features)
    queries, own, keys, values, table, patches, scales = make_queries(
        slab_kernel, received, folded, gram, cosine, sine, freqs
    )
    parts = attend_history(same, other, modulation, w_qkv, perm, table, queries, keys, values)
    parts = lax.all_to_all(parts, "frame", 0, 0, tiled=True)
    numerator, denominator = attend_section(patches, scales, folded, own, cosine, sine)
    return combine(parts, numerator, denominator)


def solution(mesh):
    in_specs = (
        P("frame", None, None, None),
        P("frame", None),
        P(),
        P(None, ("head", "fsdp")),
        P(None, ("head", "fsdp")),
        P(None, ("head", "fsdp")),
        P(),
        P(None, None, ("head", "fsdp")),
    )
    out_specs = P("frame", ("head", "fsdp"))
    return jax.shard_map(
        per_device, mesh=mesh, in_specs=in_specs, out_specs=out_specs, check_vma=False
    )
```

```python
import functools

import jax
import jax.numpy as jnp
import numpy as np
from jax import lax
from jax.experimental import pallas as pl
from jax.experimental.pallas import tpu as pltpu
from jax.sharding import PartitionSpec as P

HEAD_DIM = 128
PARTS = (16, 56, 56)
THETA = 256.0
EPS = 1e-06
QUERY_SCALE = float(np.log2(np.e) * HEAD_DIM**-0.5)
EMBED = 50
BF = jnp.bfloat16
F32 = jnp.float32
VMEM = pl.BlockSpec(memory_space=pltpu.VMEM)
ANY = pl.BlockSpec(memory_space=pl.ANY)
SMEM = pl.BlockSpec(memory_space=pltpu.SMEM)


def params(mib=10):
    return pltpu.CompilerParams(vmem_limit_bytes=mib * 2**20)


def cost(flops, bytes_accessed, transcendentals=0):
    return pl.CostEstimate(
        flops=int(flops), bytes_accessed=int(bytes_accessed), transcendentals=int(transcendentals)
    )


def pair_tables():
    freqs = np.zeros((3, 64), np.float64)
    first, second = [], []
    pair, offset = 0, 0
    for axis, width in enumerate(PARTS):
        half = width // 2
        for i in range(half):
            freqs[axis, pair] = THETA ** (-2.0 * i / width)
            first.append(offset + i)
            second.append(offset + i + half)
            pair += 1
        offset += width
    return freqs, np.array(first + second)


def section_tables(frames, per_frame):
    freqs, _ = pair_tables()
    rows = np.arange(frames * per_frame)
    pos = np.stack(
        [4.0 * frames + rows // 512, 2.0 * (rows // 128 % 4) + 0.5, 2.0 * (rows % 128) + 0.5]
    )
    angles = freqs.T @ pos
    return np.cos(angles).astype(np.float32), np.sin(angles).astype(np.float32)


def head_permutation():
    _, order = pair_tables()
    perm = np.zeros((HEAD_DIM, HEAD_DIM), np.float32)
    perm[order, np.arange(HEAD_DIM)] = 1.0
    return perm


def lane_frequencies():
    freqs, _ = pair_tables()
    table = np.zeros((8, HEAD_DIM), np.float32)
    table[:3] = np.concatenate([freqs, freqs], axis=1)
    table[3] = np.concatenate([-np.ones(64), np.ones(64)])
    return table


def dot(a, b, dims=((1,), (0,))):
    return lax.dot_general(a, b, (dims, ((), ())), preferred_element_type=F32)


def select_columns(rows, columns, source):
    j = lax.broadcasted_iota(jnp.int32, (8, columns), 1)[0:1]
    i = lax.broadcasted_iota(jnp.int32, (rows, columns), 0)
    return jnp.where(i == source(j), 1.0, 0.0).astype(BF)


def select_rows(rows, columns, source):
    j = lax.broadcasted_iota(jnp.int32, (rows, columns), 1)
    i = lax.broadcasted_iota(jnp.int32, (rows, 128), 0)[:, 0:1]
    return jnp.where(j == source(i), 1.0, 0.0).astype(BF)


def split(value):
    high = value.astype(BF)
    return high, (value - high.astype(F32)).astype(BF)


def prepare_kernel(
    kinds_hbm,
    hist_hbm,
    sec_hbm,
    fine_hbm,
    out_ref,
    fine_ref,
    kinds_ref,
    hist_ref,
    sec_ref,
    kinds_sem,
    hist_sem,
    sec_sem,
    fine_sem,
):
    staged = [pltpu.make_async_copy(fine_hbm, fine_ref, fine_sem)]
    copies = [
        pltpu.make_async_copy(kinds_hbm, kinds_ref, kinds_sem),
        pltpu.make_async_copy(sec_hbm, sec_ref, sec_sem),
        pltpu.make_async_copy(hist_hbm, hist_ref, hist_sem),
    ]
    for copy in copies + staged:
        copy.start()
    for copy in copies:
        copy.wait()
    kind = kinds_ref[lax.axis_index("frame")]
    cells = hist_ref[...]

    own = select_rows(64, 64, lambda i: (i & 31) * 2 + (i >> 5))
    section = dot(own, sec_ref[...]).astype(BF)
    for d in range(16):
        out_ref[d, 64:128, :] = section

    @pl.when(kind == 0)
    def _():
        z, core = lax.axis_index("head"), lax.axis_index("fsdp")
        cols = select_columns(256, 128, lambda j: (64 * core + (j & 63)) * 2 + (j >> 6))
        rows = select_rows(
            128, 512, lambda i: (i >> 5) * 128 + ((i >> 1) & 15) * 8 + z * 2 + (i & 1)
        )
        out = dot(rows, dot(cells, cols).astype(BF)).astype(BF)
        blank = jnp.zeros((32, 128), BF)
        for d in range(16):
            t = d // 4
            out_ref[d, 0:64, :] = jnp.concatenate([out[32 * t : 32 * t + 32], blank], axis=0)

    @pl.when(kind == 1)
    def _():
        cols = select_columns(256, 256, lambda j: (j & 63) * 4 + (j >> 6))
        lanes = select_columns(
            512,
            512,
            lambda j: ((j >> 8) * 2 + ((j >> 2) & 1)) * 128
            + ((j >> 3) & 15) * 8
            + ((j >> 7) & 1) * 4
            + (j & 3),
        )
        out = dot(dot(cells, cols).astype(BF), lanes, ((0,), (0,))).astype(BF)
        for d in range(16):
            g, q = d // 4, d % 4
            for w in range(4):
                out_ref[d, 16 * w : 16 * w + 16, :] = out[
                    64 * w + 16 * q : 64 * w + 16 * q + 16, 128 * g : 128 * g + 128
                ]

    @pl.when(kind == 2)
    def _():
        lanes = select_columns(
            512, 512, lambda j: ((j >> 3) & 3) * 128 + (j >> 5) * 8 + (j & 7)
        )
        out = dot(cells, lanes, ((0,), (0,))).astype(BF)
        for d in range(16):
            for g in range(4):
                out_ref[d, 16 * g : 16 * g + 16, :] = out[
                    16 * d : 16 * d + 16, 128 * g : 128 * g + 128
                ]

    for copy in staged:
        copy.wait()


def prepare(kinds, history, section, patch_fine):
    return pl.pallas_call(
        prepare_kernel,
        out_shape=(
            jax.ShapeDtypeStruct((16, 128, 128), BF),
            jax.ShapeDtypeStruct(patch_fine.shape, BF),
        ),
        in_specs=[ANY] * 4,
        out_specs=(VMEM,) * 2,
        scratch_shapes=[
            pltpu.SMEM((16,), jnp.int32),
            pltpu.VMEM((512, 256), BF),
            pltpu.VMEM((64, 128), BF),
        ]
        + [pltpu.SemaphoreType.DMA] * 4,
        compiler_params=params(60),
        cost_estimate=cost(2e10, 1e6),
        name="prepare",
    )(kinds, history.reshape(512, 256), section.T, patch_fine)


def embed_kernel(
    kinds_ref,
    recv_ref,
    mid_hbm,
    coarse_hbm,
    other_ref,
    out_ref,
    mid_ref,
    coarse_ref,
    mid_buf,
    coarse_buf,
    mid_sem,
    coarse_sem,
):
    del other_ref
    mid_copy = pltpu.make_async_copy(mid_hbm, mid_ref, mid_sem)
    coarse_copy = pltpu.make_async_copy(coarse_hbm, coarse_ref, coarse_sem)
    mid_copy.start()
    coarse_copy.start()
    mid_count = jnp.int32(0)
    coarse_count = jnp.int32(0)
    for s in range(16):
        kind = kinds_ref[s]
        block = recv_ref[s, 0:64, :]
        mid_buf[jnp.where(kind == 1, jnp.minimum(mid_count, 6), 7)] = block
        coarse_buf[jnp.where(kind == 2, jnp.minimum(coarse_count, 7), 8)] = block
        mid_count += jnp.where(kind == 1, 1, 0)
        coarse_count += jnp.where(kind == 2, 1, 0)

        @pl.when(kind == 0)
        def _(block=block):
            blank = jnp.zeros((16, out_ref.shape[1] - 256), BF)
            out_ref[128:144, :] = jnp.concatenate([block[0:16], block[16:32], blank], axis=1)

    tokens = jnp.concatenate(
        [mid_buf[0:7, 16 * w : 16 * w + 16, :].reshape(112, 128) for w in range(4)], axis=1
    )
    order = select_columns(512, 512, lambda j: (j & 3) * 128 + (j >> 2))
    tokens = dot(tokens, order).astype(BF)
    mid_copy.wait()
    out_ref[0:112, :] = dot(tokens, mid_ref[...]).astype(BF)
    cells = coarse_buf[0:8].reshape(512, 128)
    order = select_rows(
        512,
        512,
        lambda i: ((i >> 1) & 7) * 64 + (i >> 7) * 16 + (i & 1) * 8 + ((i >> 4) & 7),
    )
    cells = dot(order, cells).astype(BF)
    tokens = jnp.concatenate(
        [
            jnp.concatenate(
                [cells[128 * g + 16 * w : 128 * g + 16 * w + 16] for w in range(8)], axis=1
            )
            for g in range(4)
        ],
        axis=0,
    )
    order = select_columns(1024, 1024, lambda j: (j & 7) * 128 + (j >> 3))
    tokens = dot(tokens, order).astype(BF)
    total = jnp.zeros((16, out_ref.shape[1]), F32)
    coarse_copy.wait()
    for g in range(4):
        total += dot(tokens[16 * g : 16 * g + 16], coarse_ref[1024 * g : 1024 * g + 1024, :])
    out_ref[112:128, :] = total.astype(BF)


def embed(kinds, received, patch_mid, patch_coarse, fine_other):
    return pl.pallas_call(
        embed_kernel,
        out_shape=jax.ShapeDtypeStruct((144, patch_mid.shape[1]), BF),
        in_specs=[SMEM, VMEM, ANY, ANY, ANY],
        out_specs=VMEM,
        scratch_shapes=[
            pltpu.VMEM(patch_mid.shape, BF),
            pltpu.VMEM(patch_coarse.shape, BF),
            pltpu.VMEM((8, 64, 128), BF),
            pltpu.VMEM((9, 64, 128), BF),
        ]
        + [pltpu.SemaphoreType.DMA] * 2,
        compiler_params=params(EMBED),
        cost_estimate=cost(2e9, 5e6),
        name="embed",
    )(kinds, received, patch_mid, patch_coarse, fine_other)


def stack_kernel(*refs):
    for d, ref in enumerate(refs[:-1]):
        refs[-1][d] = ref[...]


def stack(blocks, estimate):
    return pl.pallas_call(
        stack_kernel,
        out_shape=jax.ShapeDtypeStruct((len(blocks), *blocks[0].shape), BF),
        in_specs=[VMEM] * len(blocks),
        out_specs=VMEM,
        compiler_params=params(),
        cost_estimate=estimate,
        name="stack",
    )(*blocks)


def gather_columns(block, estimate):
    ring1, ring3, ring2 = (
        lax.ppermute(block, "head", [(i, (i + d) % 4) for i in range(4)]) for d in (1, 3, 2)
    )
    swap = [(0, 1), (1, 0)]
    twin = lax.ppermute(block, "fsdp", swap)
    same = stack((ring1, ring2, ring3), estimate)
    return block, twin, same, lax.ppermute(same, "fsdp", swap)


def pairs(own_ref, twin_ref, same_ref, other_ref):
    yield 0, own_ref, twin_ref
    for d in range(3):
        yield d + 1, same_ref.at[d], other_ref.at[d]


def place_columns(gathered, full_ref):
    z, core = lax.axis_index("head"), lax.axis_index("fsdp")
    rows = full_ref.shape[0]
    for d, mine, theirs in pairs(*gathered):
        at = ((z + 4 - d) & 3) * 2
        width = mine.shape[1]
        for ref, column in ((mine, at + core), (theirs, at + 1 - core)):
            full_ref[:, pl.ds(pl.multiple_of(column * width, 128), width)] = ref[0:rows]


def fold_kernel(
    own_ref,
    twin_ref,
    same_ref,
    other_ref,
    mod_ref,
    w_ref,
    perm_ref,
    far_ref,
    fold_ref,
    gram_ref,
    full_ref,
):
    del far_ref
    place_columns((own_ref, twin_ref, same_ref, other_ref), full_ref)
    order = select_rows(64, 64, lambda i: (i & 31) * 2 + (i >> 5))
    raw = full_ref[...]
    width = raw.shape[1]
    weight = dot(order, raw)
    low = weight.astype(BF)
    mean = jnp.sum(weight, axis=1, keepdims=True) / width
    mean_row = dot(jnp.ones((8, width), BF), low, ((1,), (1,)))[0:1] / width
    gram_ref[...] = dot(low, low, ((1,), (1,))) / width - mean * mean_row
    scaled = (weight - mean) * (1.0 + mod_ref[1:2, :])
    shift_high, shift_low = split(mod_ref[0:1, :])
    pad = jnp.zeros((14, width), BF)
    high, rest = split(scaled)
    left = jnp.concatenate(
        [high, rest, jnp.concatenate([shift_high, shift_low, pad], axis=0)], axis=0
    )
    for part in range(3):
        product = dot(left, w_ref[part])
        matrix = product[0:64] + product[64:128]
        bias = product[128:129] + product[129:130]
        columns = matrix.shape[1]
        high, rest = split(matrix)
        bias_high, bias_low = split(bias)
        rows = jnp.concatenate(
            [
                high.astype(F32),
                rest.astype(F32),
                bias_high.astype(F32),
                bias_high.astype(F32),
                bias_low.astype(F32),
                jnp.zeros((13, columns), F32),
            ],
            axis=0,
        ).astype(BF)
        if part < 2:
            rows = jnp.concatenate(
                [
                    dot(rows[:, HEAD_DIM * h : HEAD_DIM * (h + 1)], perm_ref[...]).astype(BF)
                    for h in range(columns // HEAD_DIM)
                ],
                axis=1,
            )
        fold_ref[part] = rows


def fold(gathered, modulation, w_qkv, perm, far):
    width, columns = w_qkv.shape[1], w_qkv.shape[2]
    return pl.pallas_call(
        fold_kernel,
        out_shape=(
            jax.ShapeDtypeStruct((3, 144, columns), BF),
            jax.ShapeDtypeStruct((64, 64), F32),
        ),
        in_specs=[VMEM] * 7 + [ANY],
        out_specs=(VMEM, VMEM),
        scratch_shapes=[pltpu.VMEM((64, width), BF)],
        compiler_params=params(),
        cost_estimate=cost(1e6, 1e4),
        name="fold",
    )(*gathered, modulation, w_qkv, perm, far)


def along_x(value, d):
    return lax.ppermute(value, "frame", [(i, i // 4 * 4 + (i + d) % 4) for i in range(16)])


def along_y(value, d):
    return lax.ppermute(value, "frame", [(i, (i + 4 * d) % 16) for i in range(16)])


def spread_of(patches, gram):
    one, rest = split(gram)
    two, three = split(gram - one.astype(F32))
    parts = jnp.concatenate([one, two, three], axis=1)
    spread = dot(parts, jnp.concatenate([patches, patches, patches], axis=0))
    variance = jnp.sum(spread * patches.astype(F32), axis=0, keepdims=True)
    return jnp.maximum(variance, 0.0) + EPS


def extended(patches, variance):
    high, low = split(jnp.sqrt(variance))
    rows = lax.broadcasted_iota(jnp.int32, (16, patches.shape[1]), 0)
    extra = jnp.where(
        rows == 1,
        low.astype(F32),
        jnp.where((rows == 0) | (rows == 2), high.astype(F32), 0.0),
    ).astype(BF)
    return jnp.concatenate([patches, patches, extra], axis=0)


def turned_columns(raw, variance, cosine, sine, scale):
    square = jnp.sum(raw * raw, axis=0, keepdims=True) / HEAD_DIM
    factor = lax.rsqrt(square + EPS * variance) * scale
    a, b = raw[0:64] * factor, raw[64:128] * factor
    return jnp.concatenate([a * cosine - b * sine, b * cosine + a * sine], axis=0).astype(BF)


def token_kernel(
    kinds_ref,
    recv_ref,
    own_ref,
    twin_ref,
    same_ref,
    other_ref,
    fold_ref,
    gram_ref,
    cos_ref,
    sin_ref,
    time_ref,
    query_ref,
    key_ref,
    value_ref,
    fine_buf,
):
    me = lax.axis_index("frame")
    x, y = me & 3, me >> 2
    heads = query_ref.shape[0] // HEAD_DIM
    columns = [((y + d) & 3) * 4 + x for d in range(4)]

    def block(ref, f):
        return ref[:, pl.ds(pl.multiple_of(f * 128, 128), 128)]

    z, core = lax.axis_index("head"), lax.axis_index("fsdp")
    for d, mine, theirs in pairs(own_ref, twin_ref, same_ref, other_ref):
        mine, theirs = (
            jnp.concatenate([ref[128:144, 0:128], ref[128:144, 128:256]], axis=0).astype(F32)
            for ref in (mine, theirs)
        )
        first, second = jnp.where(core == 0, mine, theirs), jnp.where(core == 0, theirs, mine)
        fine_buf[:, pl.ds(pl.multiple_of(((z + 4 - d) & 3) * 128, 128), 128)] = jnp.concatenate(
            [
                jnp.concatenate([first[:, 0:64], second[:, 0:64]], axis=1),
                jnp.concatenate([first[:, 64:128], second[:, 64:128]], axis=1),
            ],
            axis=0,
        ).astype(BF)
    patches = jnp.concatenate(
        [recv_ref[f, 64:128, :] for f in columns]
        + [recv_ref[4 * y + i, 64:128, :] for i in range(4)]
        + [fine_buf[...]],
        axis=1,
    )
    variance = spread_of(patches, gram_ref[...])
    inverse = lax.rsqrt(variance)
    patches = extended(patches, variance)
    cosine = jnp.concatenate([block(cos_ref, f) for f in columns], axis=1)
    sine = jnp.concatenate([block(sin_ref, f) for f in columns], axis=1)
    row = pl.ds(pl.multiple_of(y * 512, 128), 512)
    key_cos, key_sin = cos_ref[:, row], sin_ref[:, row]
    slab = jnp.int32(0)
    for s in range(16):
        slab += jnp.where(kinds_ref[s] == 0, s, 0)
    angles = time_ref[...] * (4 * slab + y).astype(F32)
    fine_cos = jnp.concatenate([jnp.concatenate([jnp.cos(angles)] * 4, axis=1), key_cos[8:]], axis=0)
    fine_sin = jnp.concatenate([jnp.concatenate([jnp.sin(angles)] * 4, axis=1), key_sin[8:]], axis=0)
    key_cos = jnp.concatenate([key_cos, fine_cos], axis=1)
    key_sin = jnp.concatenate([key_sin, fine_sin], axis=1)
    for h in range(heads):
        at = slice(HEAD_DIM * h, HEAD_DIM * (h + 1))
        raw = dot(fold_ref[0][:, at], patches[:, 0:512], ((0,), (0,)))
        query_ref[at, :] = turned_columns(raw, variance[:, 0:512], cosine, sine, QUERY_SCALE)
        raw = dot(fold_ref[1][:, at], patches[:, 512:], ((0,), (0,)))
        key_ref[at, :] = turned_columns(raw, variance[:, 512:], key_cos, key_sin, 1.0)
        raw = dot(fold_ref[2][:, at], patches[:, 512:], ((0,), (0,)))
        value_ref[at, :] = (raw * inverse[:, 512:]).astype(BF)


def make_tokens(kinds, received, gathered, folded, gram, cosine, sine, times):
    columns = folded.shape[2]
    return pl.pallas_call(
        token_kernel,
        out_shape=(
            jax.ShapeDtypeStruct((columns, 512), BF),
            jax.ShapeDtypeStruct((columns, 1024), BF),
            jax.ShapeDtypeStruct((columns, 1024), BF),
        ),
        in_specs=[SMEM] + [VMEM] * 10,
        out_specs=tuple([VMEM] * 3),
        scratch_shapes=[pltpu.VMEM((64, 512), BF)],
        compiler_params=params(),
        cost_estimate=cost(2e9, 8e6),
        name="tokens",
    )(kinds, received, *gathered, folded, gram, cosine, sine, times)


def near_kernel(query_ref, key_ref, value_ref, num_ref, den_ref):
    heads = query_ref.shape[0] // HEAD_DIM
    for h in range(heads):
        at = slice(HEAD_DIM * h, HEAD_DIM * (h + 1))
        weights = jnp.exp2(dot(key_ref[at, :], query_ref[at, :], ((0,), (0,))))
        den_ref[h : h + 1, :] = jnp.sum(weights, axis=0, keepdims=True)
        num_ref[at, :] = dot(value_ref[at, :], weights.astype(BF))


def attend_near(queries, keys, values):
    columns, count = queries.shape
    return pl.pallas_call(
        near_kernel,
        out_shape=(
            jax.ShapeDtypeStruct((columns, count), F32),
            jax.ShapeDtypeStruct((8, count), F32),
        ),
        in_specs=[VMEM] * 3,
        out_specs=(VMEM, VMEM),
        compiler_params=params(),
        cost_estimate=cost(4e9, 1e7, 2e6),
        name="near",
    )(queries, keys, values)


def row_angles(kinds_ref, freq_ref):
    me = lax.axis_index("frame")
    row = lax.broadcasted_iota(jnp.int32, (128, 128), 0)
    slot = row >> 4
    slab = jnp.zeros((128, 128), F32)
    mid_count = jnp.int32(0)
    coarse_count = jnp.int32(0)
    coarse_slot = jnp.where(slot == 7, (row >> 1) & 7, -1)
    for s in range(16):
        kind = kinds_ref[s]
        is_mid, is_coarse = kind == 1, kind == 2
        slab = jnp.where(slot == jnp.where(is_mid, mid_count, 99), float(s), slab)
        slab = jnp.where(coarse_slot == jnp.where(is_coarse, coarse_count, 99), float(s), slab)
        mid_count += jnp.where(is_mid, 1, 0)
        coarse_count += jnp.where(is_coarse, 1, 0)
    coarse = slot == 7
    whole = me.astype(F32)
    quarter = (me & 3).astype(F32)
    frame_half = (me >> 3).astype(F32)
    row_half = ((me >> 2) & 1).astype(F32)
    t = 4.0 * slab + jnp.where(coarse, 1.5, 2.0 * frame_half + 0.5)
    h = jnp.where(coarse, 3.5, 4.0 * row_half + 1.5)
    w = jnp.where(
        coarse,
        8.0 * (2.0 * whole + (row & 1).astype(F32)) + 3.5,
        4.0 * (16.0 * quarter + (row & 15).astype(F32)) + 1.5,
    )
    freq_t, freq_h, freq_w, sign = (freq_ref[i : i + 1, :] for i in range(4))
    angles = t * freq_t + h * freq_h + w * freq_w
    return jnp.cos(angles), jnp.sin(angles) * sign


def far_kernel(
    kinds_ref,
    own_ref,
    twin_ref,
    same_ref,
    other_ref,
    mod_ref,
    w_ref,
    perm_ref,
    freq_ref,
    out_ref,
    full_ref,
):
    place_columns((own_ref, twin_ref, same_ref, other_ref), full_ref)
    heads = out_ref.shape[2] // HEAD_DIM
    x = full_ref[...].astype(F32)
    x = x - jnp.mean(x, axis=1, keepdims=True)
    x = x * lax.rsqrt(jnp.mean(x * x, axis=1, keepdims=True) + EPS)
    x = (x * (1.0 + mod_ref[1:2, :]) + mod_ref[0:1, :]).astype(BF)
    raw_keys = dot(x, w_ref[1])
    out_ref[1] = dot(x, w_ref[2]).astype(BF)
    cosine, sine = row_angles(kinds_ref, freq_ref)
    for h in range(heads):
        at = slice(HEAD_DIM * h, HEAD_DIM * (h + 1))
        raw = raw_keys[:, at]
        raw = raw * lax.rsqrt(jnp.mean(raw * raw, axis=1, keepdims=True) + EPS)
        high, rest = split(raw)
        raw = dot(high, perm_ref[...]) + dot(rest, perm_ref[...])
        out_ref[0, :, at] = (raw * cosine + pltpu.roll(raw, 64, 1) * sine).astype(BF)


def make_far(kinds, gathered, modulation, w_qkv, perm, freqs):
    columns = w_qkv.shape[2]
    return pl.pallas_call(
        far_kernel,
        out_shape=jax.ShapeDtypeStruct((2, 128, columns), BF),
        in_specs=[SMEM] + [VMEM] * 8,
        out_specs=VMEM,
        scratch_shapes=[pltpu.VMEM((128, w_qkv.shape[1]), BF)],
        compiler_params=params(),
        cost_estimate=cost(2e9, 1e7),
        name="far",
    )(kinds, *gathered, modulation, w_qkv, perm, freqs)


def history_kernel(far0, far1, far3, key2, value2, query_ref, num_ref, den_ref, out0, out1, out2, out3):
    heads = query_ref.shape[0] // HEAD_DIM
    count = query_ref.shape[1]
    outs = (out0, out1, out2, out3)
    rows = lax.broadcasted_iota(jnp.int32, (16, count), 0)
    tail = jnp.zeros((16, count), F32)
    for h in range(heads):
        at = slice(HEAD_DIM * h, HEAD_DIM * (h + 1))
        fars = (far0, far1, far3)
        keys = jnp.concatenate([far[0, :, at] for far in fars] + [key2[:, at]], axis=0)
        values = jnp.concatenate([far[1, :, at] for far in fars] + [value2[:, at]], axis=0)
        weights = jnp.exp2(dot(keys, query_ref[at, :]))
        high, rest = split(den_ref[h : h + 1, :] + jnp.sum(weights, axis=0, keepdims=True))
        tail = jnp.where(rows == h, high.astype(F32), tail)
        tail = jnp.where(rows == heads + h, rest.astype(F32), tail)
        part = num_ref[at, :] + dot(values, weights.astype(BF), ((0,), (0,)))
        for d, out in enumerate(outs):
            out[at, :] = part[:, 128 * d : 128 * d + 128].astype(out.dtype)
    for d, out in enumerate(outs):
        out[HEAD_DIM * heads :, :] = tail[:, 128 * d : 128 * d + 128].astype(out.dtype)


def attend_history(fars, queries, numerator, denominator):
    columns = queries.shape[0]
    return pl.pallas_call(
        history_kernel,
        out_shape=tuple(jax.ShapeDtypeStruct((columns + 16, 128), t) for t in (F32, BF, BF, BF)),
        in_specs=[VMEM] * 8,
        out_specs=tuple([VMEM] * 4),
        compiler_params=params(),
        cost_estimate=cost(2e9, 4e6, 1e6),
        name="history",
    )(*fars, queries, numerator, denominator)


def combine_kernel(part0, part1, part2, part3, out_ref):
    columns = out_ref.shape[1]
    heads = columns // HEAD_DIM
    total = sum(part[...].astype(F32) for part in (part0, part1, part2, part3))
    for h in range(heads):
        at = slice(HEAD_DIM * h, HEAD_DIM * (h + 1))
        low = columns + heads + h
        denominator = total[columns + h : columns + h + 1] + total[low : low + 1]
        out_ref[:, at] = jnp.transpose(total[at] / denominator).astype(BF)


def combine(parts):
    return pl.pallas_call(
        combine_kernel,
        out_shape=jax.ShapeDtypeStruct((128, parts[0].shape[0] - 16), BF),
        in_specs=[VMEM] * 4,
        out_specs=VMEM,
        compiler_params=params(),
        cost_estimate=cost(1e7, 2e6),
        name="combine",
    )(*parts)


def per_device(
    history, section, slab_kernel, patch_fine, patch_mid, patch_coarse, modulation, w_qkv
):
    frames = lax.axis_size("frame")
    cos_table, sin_table = section_tables(frames, section.shape[0])
    cosine, sine = jnp.asarray(cos_table), jnp.asarray(sin_table)
    perm = jnp.asarray(head_permutation(), BF)
    lane_table = lane_frequencies()
    freqs = jnp.asarray(lane_table)
    times = jnp.asarray(np.repeat(lane_table[0, 0:8, None], 128, axis=1))

    sent, patch_fine = prepare(slab_kernel, history, section, patch_fine)
    received = lax.all_to_all(sent, "frame", 0, 0, tiled=True)
    fine = gather_columns(patch_fine, cost(1e6, 4e5))
    features = embed(slab_kernel, received, patch_mid, patch_coarse, fine[3])
    gathered = gather_columns(features, cost(2e10, 1e6))
    far = make_far(slab_kernel, gathered, modulation, w_qkv, perm, freqs)
    far1, far3 = along_x(far, 1), along_x(far, 3)
    far2 = along_x(far1[0], 1), along_x(far3[1], 3)
    folded, gram = fold(fine, modulation, w_qkv, perm, far)
    queries, keys, values = make_tokens(
        slab_kernel, received, gathered, folded, gram, cosine, sine, times
    )
    numerator, denominator = attend_near(queries, keys, values)
    fars = [far, far1, far3, *far2]
    parts = attend_history(fars, queries, numerator, denominator)
    part2 = along_y(parts[2], 2)
    return combine([parts[0], along_y(parts[1], 1), part2, along_y(parts[3], 3)])


def solution(mesh):
    in_specs = (
        P("frame", None, None, None),
        P("frame", None),
        P(),
        P(None, ("head", "fsdp")),
        P(None, ("head", "fsdp")),
        P(None, ("head", "fsdp")),
        P(),
        P(None, None, ("head", "fsdp")),
    )
    out_specs = P("frame", ("head", "fsdp"))
    return jax.shard_map(
        per_device, mesh=mesh, in_specs=in_specs, out_specs=out_specs, check_vma=False
    )
```

```python
import functools

import jax
import jax.numpy as jnp
import numpy as np
from jax import lax
from jax.experimental import pallas as pl
from jax.experimental.pallas import tpu as pltpu
from jax.sharding import PartitionSpec as P

HEAD_DIM = 128
PARTS = (16, 56, 56)
THETA = 256.0
EPS = 1e-06
QUERY_SCALE = float(np.log2(np.e) * HEAD_DIM**-0.5)
EMBED = 50
BF = jnp.bfloat16
F32 = jnp.float32
VMEM = pl.BlockSpec(memory_space=pltpu.VMEM)
ANY = pl.BlockSpec(memory_space=pl.ANY)
SMEM = pl.BlockSpec(memory_space=pltpu.SMEM)


def params(mib=10):
    return pltpu.CompilerParams(vmem_limit_bytes=mib * 2**20)


def cost(flops, bytes_accessed, transcendentals=0):
    return pl.CostEstimate(
        flops=int(flops), bytes_accessed=int(bytes_accessed), transcendentals=int(transcendentals)
    )


def pair_tables():
    freqs = np.zeros((3, 64), np.float64)
    first, second = [], []
    pair, offset = 0, 0
    for axis, width in enumerate(PARTS):
        half = width // 2
        for i in range(half):
            freqs[axis, pair] = THETA ** (-2.0 * i / width)
            first.append(offset + i)
            second.append(offset + i + half)
            pair += 1
        offset += width
    return freqs, np.array(first + second)


def section_tables(frames, per_frame):
    freqs, _ = pair_tables()
    rows = np.arange(frames * per_frame)
    pos = np.stack(
        [4.0 * frames + rows // 512, 2.0 * (rows // 128 % 4) + 0.5, 2.0 * (rows % 128) + 0.5]
    )
    angles = freqs.T @ pos
    return np.cos(angles).astype(np.float32), np.sin(angles).astype(np.float32)


def head_permutation():
    _, order = pair_tables()
    perm = np.zeros((HEAD_DIM, HEAD_DIM), np.float32)
    perm[order, np.arange(HEAD_DIM)] = 1.0
    return perm


def lane_frequencies():
    freqs, _ = pair_tables()
    table = np.zeros((8, HEAD_DIM), np.float32)
    table[:3] = np.concatenate([freqs, freqs], axis=1)
    table[3] = np.concatenate([-np.ones(64), np.ones(64)])
    return table


def dot(a, b, dims=((1,), (0,))):
    return lax.dot_general(a, b, (dims, ((), ())), preferred_element_type=F32)


def select_columns(rows, columns, source):
    j = lax.broadcasted_iota(jnp.int32, (8, columns), 1)[0:1]
    i = lax.broadcasted_iota(jnp.int32, (rows, columns), 0)
    return jnp.where(i == source(j), 1.0, 0.0).astype(BF)


def select_rows(rows, columns, source):
    j = lax.broadcasted_iota(jnp.int32, (rows, columns), 1)
    i = lax.broadcasted_iota(jnp.int32, (rows, 128), 0)[:, 0:1]
    return jnp.where(j == source(i), 1.0, 0.0).astype(BF)


def split(value):
    high = value.astype(BF)
    return high, (value - high.astype(F32)).astype(BF)


def prepare_kernel(
    kinds_hbm,
    hist_hbm,
    sec_hbm,
    fine_hbm,
    out_ref,
    fine_ref,
    kinds_ref,
    hist_ref,
    sec_ref,
    kinds_sem,
    hist_sem,
    sec_sem,
    fine_sem,
):
    staged = [pltpu.make_async_copy(fine_hbm, fine_ref, fine_sem)]
    copies = [
        pltpu.make_async_copy(kinds_hbm, kinds_ref, kinds_sem),
        pltpu.make_async_copy(sec_hbm, sec_ref, sec_sem),
        pltpu.make_async_copy(hist_hbm, hist_ref, hist_sem),
    ]
    for copy in copies + staged:
        copy.start()
    kinds_copy, sec_copy, hist_copy = copies
    own = select_rows(64, 64, lambda i: (i & 31) * 2 + (i >> 5))
    kinds_copy.wait()
    kind = kinds_ref[lax.axis_index("frame")]
    sec_copy.wait()
    section = dot(own, sec_ref[...]).astype(BF)
    for d in range(16):
        out_ref[d, 64:128, :] = section

    @pl.when(kind == 0)
    def _():
        z, core = lax.axis_index("head"), lax.axis_index("fsdp")
        cols = select_columns(256, 128, lambda j: (64 * core + (j & 63)) * 2 + (j >> 6))
        rows = select_rows(
            128, 512, lambda i: (i >> 5) * 128 + ((i >> 1) & 15) * 8 + z * 2 + (i & 1)
        )
        hist_copy.wait()
        out = dot(rows, dot(hist_ref[...], cols).astype(BF)).astype(BF)
        blank = jnp.zeros((32, 128), BF)
        for d in range(16):
            t = d // 4
            out_ref[d, 0:64, :] = jnp.concatenate([out[32 * t : 32 * t + 32], blank], axis=0)

    @pl.when(kind == 1)
    def _():
        cols = select_columns(256, 256, lambda j: (j & 63) * 4 + (j >> 6))
        lanes = select_columns(
            512,
            512,
            lambda j: ((j >> 8) * 2 + ((j >> 2) & 1)) * 128
            + ((j >> 3) & 15) * 8
            + ((j >> 7) & 1) * 4
            + (j & 3),
        )
        hist_copy.wait()
        out = dot(dot(hist_ref[...], cols).astype(BF), lanes, ((0,), (0,))).astype(BF)
        for d in range(16):
            g, q = d // 4, d % 4
            for w in range(4):
                out_ref[d, 16 * w : 16 * w + 16, :] = out[
                    64 * w + 16 * q : 64 * w + 16 * q + 16, 128 * g : 128 * g + 128
                ]

    @pl.when(kind == 2)
    def _():
        lanes = select_columns(
            512, 512, lambda j: ((j >> 3) & 3) * 128 + (j >> 5) * 8 + (j & 7)
        )
        hist_copy.wait()
        out = dot(hist_ref[...], lanes, ((0,), (0,))).astype(BF)
        for d in range(16):
            for g in range(4):
                out_ref[d, 16 * g : 16 * g + 16, :] = out[
                    16 * d : 16 * d + 16, 128 * g : 128 * g + 128
                ]

    for copy in staged:
        copy.wait()


def prepare(kinds, history, section, patch_fine):
    return pl.pallas_call(
        prepare_kernel,
        out_shape=(
            jax.ShapeDtypeStruct((16, 128, 128), BF),
            jax.ShapeDtypeStruct(patch_fine.shape, BF),
        ),
        in_specs=[ANY] * 4,
        out_specs=(VMEM,) * 2,
        scratch_shapes=[
            pltpu.SMEM((16,), jnp.int32),
            pltpu.VMEM((512, 256), BF),
            pltpu.VMEM((64, 128), BF),
        ]
        + [pltpu.SemaphoreType.DMA] * 4,
        compiler_params=params(60),
        cost_estimate=cost(2e10, 1e6),
        name="prepare",
    )(kinds, history.reshape(512, 256), section.T, patch_fine)


def embed_kernel(
    kinds_ref,
    recv_ref,
    mid_hbm,
    coarse_hbm,
    fine_ref,
    out_ref,
    mid_ref,
    coarse_ref,
    mid_buf,
    coarse_buf,
    mid_sem,
    coarse_sem,
):
    del fine_ref
    mid_copy = pltpu.make_async_copy(mid_hbm, mid_ref, mid_sem)
    coarse_copy = pltpu.make_async_copy(coarse_hbm, coarse_ref, coarse_sem)
    mid_copy.start()
    coarse_copy.start()
    mid_count = jnp.int32(0)
    coarse_count = jnp.int32(0)
    for s in range(16):
        kind = kinds_ref[s]
        block = recv_ref[s, 0:64, :]
        mid_buf[jnp.where(kind == 1, jnp.minimum(mid_count, 6), 7)] = block
        coarse_buf[jnp.where(kind == 2, jnp.minimum(coarse_count, 7), 8)] = block
        mid_count += jnp.where(kind == 1, 1, 0)
        coarse_count += jnp.where(kind == 2, 1, 0)

        @pl.when(kind == 0)
        def _(block=block):
            blank = jnp.zeros((16, out_ref.shape[1] - 256), BF)
            out_ref[128:144, :] = jnp.concatenate([block[0:16], block[16:32], blank], axis=1)

    tokens = jnp.concatenate(
        [mid_buf[0:7, 16 * w : 16 * w + 16, :].reshape(112, 128) for w in range(4)], axis=1
    )
    order = select_columns(512, 512, lambda j: (j & 3) * 128 + (j >> 2))
    tokens = dot(tokens, order).astype(BF)
    mid_copy.wait()
    out_ref[0:112, :] = dot(tokens, mid_ref[...]).astype(BF)
    cells = coarse_buf[0:8].reshape(512, 128)
    order = select_rows(
        512,
        512,
        lambda i: ((i >> 1) & 7) * 64 + (i >> 7) * 16 + (i & 1) * 8 + ((i >> 4) & 7),
    )
    cells = dot(order, cells).astype(BF)
    tokens = jnp.concatenate(
        [
            jnp.concatenate(
                [cells[128 * g + 16 * w : 128 * g + 16 * w + 16] for w in range(8)], axis=1
            )
            for g in range(4)
        ],
        axis=0,
    )
    order = select_columns(1024, 1024, lambda j: (j & 7) * 128 + (j >> 3))
    tokens = dot(tokens, order).astype(BF)
    total = jnp.zeros((16, out_ref.shape[1]), F32)
    coarse_copy.wait()
    for g in range(4):
        total += dot(tokens[16 * g : 16 * g + 16], coarse_ref[1024 * g : 1024 * g + 1024, :])
    out_ref[112:128, :] = total.astype(BF)


def embed(kinds, received, patch_mid, patch_coarse, fine):
    return pl.pallas_call(
        embed_kernel,
        out_shape=jax.ShapeDtypeStruct((144, patch_mid.shape[1]), BF),
        in_specs=[SMEM, VMEM, ANY, ANY, ANY],
        out_specs=VMEM,
        scratch_shapes=[
            pltpu.VMEM(patch_mid.shape, BF),
            pltpu.VMEM(patch_coarse.shape, BF),
            pltpu.VMEM((8, 64, 128), BF),
            pltpu.VMEM((9, 64, 128), BF),
        ]
        + [pltpu.SemaphoreType.DMA] * 2,
        compiler_params=params(EMBED),
        cost_estimate=cost(1e6, 1e4),
        name="embed",
    )(kinds, received, patch_mid, patch_coarse, fine)


def stack_kernel(*refs):
    for d, ref in enumerate(refs[:-1]):
        refs[-1][d] = ref[...]


def stack(blocks, estimate):
    return pl.pallas_call(
        stack_kernel,
        out_shape=jax.ShapeDtypeStruct((len(blocks), *blocks[0].shape), BF),
        in_specs=[VMEM] * len(blocks),
        out_specs=VMEM,
        compiler_params=params(),
        cost_estimate=estimate,
        name="stack",
    )(*blocks)


def gather_columns(block, estimate):
    ring1, ring3, ring2 = (
        lax.ppermute(block, "head", [(i, (i + d) % 4) for i in range(4)]) for d in (1, 3, 2)
    )
    swap = [(0, 1), (1, 0)]
    twin = lax.ppermute(block, "fsdp", swap)
    same = stack((ring3, ring2, ring1), estimate)
    return block, twin, same, lax.ppermute(same, "fsdp", swap)


def pairs(own_ref, twin_ref, same_ref, other_ref):
    yield 0, own_ref, twin_ref
    for d in range(3):
        yield 3 - d, same_ref.at[d], other_ref.at[d]


def place_columns(gathered, full_ref):
    z, core = lax.axis_index("head"), lax.axis_index("fsdp")
    rows = full_ref.shape[0]
    for d, mine, theirs in pairs(*gathered):
        at = ((z + 4 - d) & 3) * 2
        width = mine.shape[1]
        for ref, column in ((mine, at + core), (theirs, at + 1 - core)):
            full_ref[:, pl.ds(pl.multiple_of(column * width, 128), width)] = ref[0:rows]


def fold_kernel(
    own_ref,
    twin_ref,
    same_ref,
    other_ref,
    mod_ref,
    w_ref,
    perm_ref,
    far_ref,
    fold_ref,
    gram_ref,
    full_ref,
):
    del far_ref
    place_columns((own_ref, twin_ref, same_ref, other_ref), full_ref)
    order = select_rows(64, 64, lambda i: (i & 31) * 2 + (i >> 5))
    raw = full_ref[...]
    width = raw.shape[1]
    weight = dot(order, raw)
    low = weight.astype(BF)
    mean = jnp.sum(weight, axis=1, keepdims=True) / width
    mean_row = dot(jnp.ones((8, width), BF), low, ((1,), (1,)))[0:1] / width
    gram_ref[...] = dot(low, low, ((1,), (1,))) / width - mean * mean_row
    scaled = (weight - mean) * (1.0 + mod_ref[1:2, :])
    shift_high, shift_low = split(mod_ref[0:1, :])
    pad = jnp.zeros((14, width), BF)
    high, rest = split(scaled)
    left = jnp.concatenate(
        [high, rest, jnp.concatenate([shift_high, shift_low, pad], axis=0)], axis=0
    )
    for part in range(3):
        product = dot(left, w_ref[part])
        matrix = product[0:64] + product[64:128]
        bias = product[128:129] + product[129:130]
        columns = matrix.shape[1]
        high, rest = split(matrix)
        bias_high, bias_low = split(bias)
        rows = jnp.concatenate(
            [
                high.astype(F32),
                rest.astype(F32),
                bias_high.astype(F32),
                bias_high.astype(F32),
                bias_low.astype(F32),
                jnp.zeros((13, columns), F32),
            ],
            axis=0,
        ).astype(BF)
        if part < 2:
            rows = jnp.concatenate(
                [
                    dot(rows[:, HEAD_DIM * h : HEAD_DIM * (h + 1)], perm_ref[...]).astype(BF)
                    for h in range(columns // HEAD_DIM)
                ],
                axis=1,
            )
        fold_ref[part] = rows


def fold(gathered, modulation, w_qkv, perm, far):
    width, columns = w_qkv.shape[1], w_qkv.shape[2]
    return pl.pallas_call(
        fold_kernel,
        out_shape=(
            jax.ShapeDtypeStruct((3, 144, columns), BF),
            jax.ShapeDtypeStruct((64, 64), F32),
        ),
        in_specs=[VMEM] * 7 + [ANY],
        out_specs=(VMEM, VMEM),
        scratch_shapes=[pltpu.VMEM((64, width), BF)],
        compiler_params=params(),
        cost_estimate=cost(1e6, 1e4),
        name="fold",
    )(*gathered, modulation, w_qkv, perm, far)


def along_x(value, d):
    return lax.ppermute(value, "frame", [(i, i // 4 * 4 + (i + d) % 4) for i in range(16)])


def along_y(value, d):
    return lax.ppermute(value, "frame", [(i, (i + 4 * d) % 16) for i in range(16)])


def spread_of(patches, gram):
    one, rest = split(gram)
    two, three = split(gram - one.astype(F32))
    parts = jnp.concatenate([one, two, three], axis=1)
    spread = dot(parts, jnp.concatenate([patches, patches, patches], axis=0))
    variance = jnp.sum(spread * patches.astype(F32), axis=0, keepdims=True)
    return jnp.maximum(variance, 0.0) + EPS


def extended(patches, variance):
    high, low = split(jnp.sqrt(variance))
    rows = lax.broadcasted_iota(jnp.int32, (16, patches.shape[1]), 0)
    extra = jnp.where(
        rows == 1,
        low.astype(F32),
        jnp.where((rows == 0) | (rows == 2), high.astype(F32), 0.0),
    ).astype(BF)
    return jnp.concatenate([patches, patches, extra], axis=0)


def turned_columns(raw, variance, cosine, sine, scale):
    square = jnp.sum(raw * raw, axis=0, keepdims=True) / HEAD_DIM
    factor = lax.rsqrt(square + EPS * variance) * scale
    a, b = raw[0:64] * factor, raw[64:128] * factor
    return jnp.concatenate([a * cosine - b * sine, b * cosine + a * sine], axis=0).astype(BF)


def token_kernel(
    kinds_ref,
    recv_ref,
    own_ref,
    twin_ref,
    same_ref,
    other_ref,
    fold_ref,
    gram_ref,
    cos_ref,
    sin_ref,
    time_ref,
    query_ref,
    key_ref,
    value_ref,
    fine_buf,
):
    me = lax.axis_index("frame")
    x, y = me & 3, me >> 2
    heads = query_ref.shape[0] // HEAD_DIM
    columns = [((y + d) & 3) * 4 + x for d in range(4)]

    def block(ref, f):
        return ref[:, pl.ds(pl.multiple_of(f * 128, 128), 128)]

    z, core = lax.axis_index("head"), lax.axis_index("fsdp")
    for d, mine, theirs in pairs(own_ref, twin_ref, same_ref, other_ref):
        mine, theirs = (
            jnp.concatenate([ref[128:144, 0:128], ref[128:144, 128:256]], axis=0).astype(F32)
            for ref in (mine, theirs)
        )
        first, second = jnp.where(core == 0, mine, theirs), jnp.where(core == 0, theirs, mine)
        fine_buf[:, pl.ds(pl.multiple_of(((z + 4 - d) & 3) * 128, 128), 128)] = jnp.concatenate(
            [
                jnp.concatenate([first[:, 0:64], second[:, 0:64]], axis=1),
                jnp.concatenate([first[:, 64:128], second[:, 64:128]], axis=1),
            ],
            axis=0,
        ).astype(BF)
    patches = jnp.concatenate(
        [recv_ref[f, 64:128, :] for f in columns]
        + [recv_ref[4 * y + i, 64:128, :] for i in range(4)]
        + [fine_buf[...]],
        axis=1,
    )
    variance = spread_of(patches, gram_ref[...])
    inverse = lax.rsqrt(variance)
    patches = extended(patches, variance)
    cosine = jnp.concatenate([block(cos_ref, f) for f in columns], axis=1)
    sine = jnp.concatenate([block(sin_ref, f) for f in columns], axis=1)
    row = pl.ds(pl.multiple_of(y * 512, 128), 512)
    key_cos, key_sin = cos_ref[:, row], sin_ref[:, row]
    slab = jnp.int32(0)
    for s in range(16):
        slab += jnp.where(kinds_ref[s] == 0, s, 0)
    angles = time_ref[...] * (4 * slab + y).astype(F32)
    fine_cos = jnp.concatenate([jnp.concatenate([jnp.cos(angles)] * 4, axis=1), key_cos[8:]], axis=0)
    fine_sin = jnp.concatenate([jnp.concatenate([jnp.sin(angles)] * 4, axis=1), key_sin[8:]], axis=0)
    key_cos = jnp.concatenate([key_cos, fine_cos], axis=1)
    key_sin = jnp.concatenate([key_sin, fine_sin], axis=1)
    for h in range(heads):
        at = slice(HEAD_DIM * h, HEAD_DIM * (h + 1))
        raw = dot(fold_ref[0][:, at], patches[:, 0:512], ((0,), (0,)))
        query_ref[at, :] = turned_columns(raw, variance[:, 0:512], cosine, sine, QUERY_SCALE)
        raw = dot(fold_ref[1][:, at], patches[:, 512:], ((0,), (0,)))
        key_ref[at, :] = turned_columns(raw, variance[:, 512:], key_cos, key_sin, 1.0)
        raw = dot(fold_ref[2][:, at], patches[:, 512:], ((0,), (0,)))
        value_ref[at, :] = (raw * inverse[:, 512:]).astype(BF)


def make_tokens(kinds, received, gathered, folded, gram, cosine, sine, times):
    columns = folded.shape[2]
    return pl.pallas_call(
        token_kernel,
        out_shape=(
            jax.ShapeDtypeStruct((columns, 512), BF),
            jax.ShapeDtypeStruct((columns, 1024), BF),
            jax.ShapeDtypeStruct((columns, 1024), BF),
        ),
        in_specs=[SMEM] + [VMEM] * 10,
        out_specs=tuple([VMEM] * 3),
        scratch_shapes=[pltpu.VMEM((64, 512), BF)],
        compiler_params=params(),
        cost_estimate=cost(2e9, 8e6),
        name="tokens",
    )(kinds, received, *gathered, folded, gram, cosine, sine, times)


def near_kernel(query_ref, key_ref, value_ref, num_ref, den_ref):
    heads = query_ref.shape[0] // HEAD_DIM
    for h in range(heads):
        at = slice(HEAD_DIM * h, HEAD_DIM * (h + 1))
        weights = jnp.exp2(dot(key_ref[at, :], query_ref[at, :], ((0,), (0,))))
        den_ref[h : h + 1, :] = jnp.sum(weights, axis=0, keepdims=True)
        num_ref[at, :] = dot(value_ref[at, :], weights.astype(BF))


def attend_near(queries, keys, values):
    columns, count = queries.shape
    return pl.pallas_call(
        near_kernel,
        out_shape=(
            jax.ShapeDtypeStruct((columns, count), F32),
            jax.ShapeDtypeStruct((8, count), F32),
        ),
        in_specs=[VMEM] * 3,
        out_specs=(VMEM, VMEM),
        compiler_params=params(),
        cost_estimate=cost(4e9, 1e7, 2e6),
        name="near",
    )(queries, keys, values)


def row_angles(kinds_ref, freq_ref):
    me = lax.axis_index("frame")
    row = lax.broadcasted_iota(jnp.int32, (128, 128), 0)
    slot = row >> 4
    slab = jnp.zeros((128, 128), F32)
    mid_count = jnp.int32(0)
    coarse_count = jnp.int32(0)
    coarse_slot = jnp.where(slot == 7, (row >> 1) & 7, -1)
    for s in range(16):
        kind = kinds_ref[s]
        is_mid, is_coarse = kind == 1, kind == 2
        slab = jnp.where(slot == jnp.where(is_mid, mid_count, 99), float(s), slab)
        slab = jnp.where(coarse_slot == jnp.where(is_coarse, coarse_count, 99), float(s), slab)
        mid_count += jnp.where(is_mid, 1, 0)
        coarse_count += jnp.where(is_coarse, 1, 0)
    coarse = slot == 7
    whole = me.astype(F32)
    quarter = (me & 3).astype(F32)
    frame_half = (me >> 3).astype(F32)
    row_half = ((me >> 2) & 1).astype(F32)
    t = 4.0 * slab + jnp.where(coarse, 1.5, 2.0 * frame_half + 0.5)
    h = jnp.where(coarse, 3.5, 4.0 * row_half + 1.5)
    w = jnp.where(
        coarse,
        8.0 * (2.0 * whole + (row & 1).astype(F32)) + 3.5,
        4.0 * (16.0 * quarter + (row & 15).astype(F32)) + 1.5,
    )
    freq_t, freq_h, freq_w, sign = (freq_ref[i : i + 1, :] for i in range(4))
    angles = t * freq_t + h * freq_h + w * freq_w
    return jnp.cos(angles), jnp.sin(angles) * sign


def far_kernel(
    kinds_ref,
    own_ref,
    twin_ref,
    same_ref,
    other_ref,
    mod_ref,
    w_ref,
    perm_ref,
    freq_ref,
    out_ref,
    full_ref,
):
    place_columns((own_ref, twin_ref, same_ref, other_ref), full_ref)
    heads = out_ref.shape[2] // HEAD_DIM
    x = full_ref[...].astype(F32)
    x = x - jnp.mean(x, axis=1, keepdims=True)
    x = x * lax.rsqrt(jnp.mean(x * x, axis=1, keepdims=True) + EPS)
    x = (x * (1.0 + mod_ref[1:2, :]) + mod_ref[0:1, :]).astype(BF)
    raw_keys = dot(x, w_ref[1])
    out_ref[1] = dot(x, w_ref[2]).astype(BF)
    cosine, sine = row_angles(kinds_ref, freq_ref)
    for h in range(heads):
        at = slice(HEAD_DIM * h, HEAD_DIM * (h + 1))
        raw = raw_keys[:, at]
        raw = raw * lax.rsqrt(jnp.mean(raw * raw, axis=1, keepdims=True) + EPS)
        high, rest = split(raw)
        raw = dot(high, perm_ref[...]) + dot(rest, perm_ref[...])
        out_ref[0, :, at] = (raw * cosine + pltpu.roll(raw, 64, 1) * sine).astype(BF)


def make_far(kinds, gathered, modulation, w_qkv, perm, freqs):
    columns = w_qkv.shape[2]
    return pl.pallas_call(
        far_kernel,
        out_shape=jax.ShapeDtypeStruct((2, 128, columns), BF),
        in_specs=[SMEM] + [VMEM] * 8,
        out_specs=VMEM,
        scratch_shapes=[pltpu.VMEM((128, w_qkv.shape[1]), BF)],
        compiler_params=params(),
        cost_estimate=cost(2e9, 1e7),
        name="far",
    )(kinds, *gathered, modulation, w_qkv, perm, freqs)


def history_kernel(far0, far1, far3, far2, query_ref, num_ref, den_ref, out0, out1, out2, out3):
    heads = query_ref.shape[0] // HEAD_DIM
    count = query_ref.shape[1]
    outs = (out0, out1, out2, out3)
    rows = lax.broadcasted_iota(jnp.int32, (16, count), 0)
    tail = jnp.zeros((16, count), F32)
    for h in range(heads):
        at = slice(HEAD_DIM * h, HEAD_DIM * (h + 1))
        fars = (far0, far1, far3, far2)
        keys = jnp.concatenate([far[0, :, at] for far in fars], axis=0)
        values = jnp.concatenate([far[1, :, at] for far in fars], axis=0)
        weights = jnp.exp2(dot(keys, query_ref[at, :]))
        high, rest = split(den_ref[h : h + 1, :] + jnp.sum(weights, axis=0, keepdims=True))
        tail = jnp.where(rows == h, high.astype(F32), tail)
        tail = jnp.where(rows == heads + h, rest.astype(F32), tail)
        part = num_ref[at, :] + dot(values, weights.astype(BF), ((0,), (0,)))
        for d, out in enumerate(outs):
            out[at, :] = part[:, 128 * d : 128 * d + 128].astype(out.dtype)
    for d, out in enumerate(outs):
        out[HEAD_DIM * heads :, :] = tail[:, 128 * d : 128 * d + 128].astype(out.dtype)


def attend_history(fars, queries, numerator, denominator):
    columns = queries.shape[0]
    return pl.pallas_call(
        history_kernel,
        out_shape=tuple(jax.ShapeDtypeStruct((columns + 16, 128), t) for t in (F32, BF, BF, BF)),
        in_specs=[VMEM] * 7,
        out_specs=tuple([VMEM] * 4),
        compiler_params=params(),
        cost_estimate=cost(2e9, 4e6, 1e6),
        name="history",
    )(*fars, queries, numerator, denominator)


def combine_kernel(part0, part1, part2, part3, out_ref):
    columns = out_ref.shape[1]
    heads = columns // HEAD_DIM
    total = sum(part[...].astype(F32) for part in (part0, part1, part2, part3))
    for h in range(heads):
        at = slice(HEAD_DIM * h, HEAD_DIM * (h + 1))
        low = columns + heads + h
        denominator = total[columns + h : columns + h + 1] + total[low : low + 1]
        out_ref[:, at] = jnp.transpose(total[at] / denominator).astype(BF)


def combine(parts):
    return pl.pallas_call(
        combine_kernel,
        out_shape=jax.ShapeDtypeStruct((128, parts[0].shape[0] - 16), BF),
        in_specs=[VMEM] * 4,
        out_specs=VMEM,
        compiler_params=params(),
        cost_estimate=cost(1e7, 2e6),
        name="combine",
    )(*parts)


def per_device(
    history, section, slab_kernel, patch_fine, patch_mid, patch_coarse, modulation, w_qkv
):
    frames = lax.axis_size("frame")
    cos_table, sin_table = section_tables(frames, section.shape[0])
    cosine, sine = jnp.asarray(cos_table), jnp.asarray(sin_table)
    perm = jnp.asarray(head_permutation(), BF)
    lane_table = lane_frequencies()
    freqs = jnp.asarray(lane_table)
    times = jnp.asarray(np.repeat(lane_table[0, 0:8, None], 128, axis=1))

    sent, patch_fine = prepare(slab_kernel, history, section, patch_fine)
    received = lax.all_to_all(sent, "frame", 0, 0, tiled=True)
    fine = gather_columns(patch_fine, cost(1e6, 1e5))
    features = embed(slab_kernel, received, patch_mid, patch_coarse, fine[2])
    gathered = gather_columns(features, cost(2e10, 1e6))
    far = make_far(slab_kernel, gathered, modulation, w_qkv, perm, freqs)
    far2, far1, far3 = (along_x(far, d) for d in (2, 1, 3))
    folded, gram = fold(fine, modulation, w_qkv, perm, far)
    queries, keys, values = make_tokens(
        slab_kernel, received, gathered, folded, gram, cosine, sine, times
    )
    numerator, denominator = attend_near(queries, keys, values)
    fars = [far, far2, far3, far1]
    parts = attend_history(fars, queries, numerator, denominator)
    part2 = along_y(parts[2], 2)
    return combine([parts[0], along_y(parts[1], 1), part2, along_y(parts[3], 3)])


def solution(mesh):
    in_specs = (
        P("frame", None, None, None),
        P("frame", None),
        P(),
        P(None, ("head", "fsdp")),
        P(None, ("head", "fsdp")),
        P(None, ("head", "fsdp")),
        P(),
        P(None, None, ("head", "fsdp")),
    )
    out_specs = P("frame", ("head", "fsdp"))
    return jax.shard_map(
        per_device, mesh=mesh, in_specs=in_specs, out_specs=out_specs, check_vma=False
    )
```

```python
import functools

import jax
import jax.numpy as jnp
import numpy as np
from jax import lax
from jax.experimental import pallas as pl
from jax.experimental.pallas import tpu as pltpu
from jax.sharding import PartitionSpec as P

HEAD_DIM = 128
PARTS = (16, 56, 56)
THETA = 256.0
EPS = 1e-06
QUERY_SCALE = float(np.log2(np.e) * HEAD_DIM**-0.5)
EMBED = 52
BF = jnp.bfloat16
F32 = jnp.float32
VMEM = pl.BlockSpec(memory_space=pltpu.VMEM)
ANY = pl.BlockSpec(memory_space=pl.ANY)
SMEM = pl.BlockSpec(memory_space=pltpu.SMEM)


def params(mib=10):
    return pltpu.CompilerParams(vmem_limit_bytes=mib * 2**20)


def cost(flops, bytes_accessed, transcendentals=0):
    return pl.CostEstimate(
        flops=int(flops), bytes_accessed=int(bytes_accessed), transcendentals=int(transcendentals)
    )


def pair_tables():
    freqs = np.zeros((3, 64), np.float64)
    first, second = [], []
    pair, offset = 0, 0
    for axis, width in enumerate(PARTS):
        half = width // 2
        for i in range(half):
            freqs[axis, pair] = THETA ** (-2.0 * i / width)
            first.append(offset + i)
            second.append(offset + i + half)
            pair += 1
        offset += width
    return freqs, np.array(first + second)


def section_tables(frames, per_frame):
    freqs, _ = pair_tables()
    rows = np.arange(frames * per_frame)
    pos = np.stack(
        [4.0 * frames + rows // 512, 2.0 * (rows // 128 % 4) + 0.5, 2.0 * (rows % 128) + 0.5]
    )
    angles = freqs.T @ pos
    return np.cos(angles).astype(np.float32), np.sin(angles).astype(np.float32)


def head_permutation():
    _, order = pair_tables()
    perm = np.zeros((HEAD_DIM, HEAD_DIM), np.float32)
    perm[order, np.arange(HEAD_DIM)] = 1.0
    return perm


def lane_frequencies():
    freqs, _ = pair_tables()
    table = np.zeros((8, HEAD_DIM), np.float32)
    table[:3] = np.concatenate([freqs, freqs], axis=1)
    table[3] = np.concatenate([-np.ones(64), np.ones(64)])
    return table


def dot(a, b, dims=((1,), (0,))):
    return lax.dot_general(a, b, (dims, ((), ())), preferred_element_type=F32)


def select_columns(rows, columns, source):
    j = lax.broadcasted_iota(jnp.int32, (8, columns), 1)[0:1]
    i = lax.broadcasted_iota(jnp.int32, (rows, columns), 0)
    return jnp.where(i == source(j), 1.0, 0.0).astype(BF)


def select_rows(rows, columns, source):
    j = lax.broadcasted_iota(jnp.int32, (rows, columns), 1)
    i = lax.broadcasted_iota(jnp.int32, (rows, 128), 0)[:, 0:1]
    return jnp.where(j == source(i), 1.0, 0.0).astype(BF)


def split(value):
    high = value.astype(BF)
    return high, (value - high.astype(F32)).astype(BF)


def prepare_kernel(
    kinds_hbm,
    hist_hbm,
    sec_hbm,
    fine_hbm,
    out_ref,
    fine_ref,
    kinds_ref,
    hist_ref,
    sec_ref,
    kinds_sem,
    hist_sem,
    sec_sem,
    fine_sem,
):
    staged = [pltpu.make_async_copy(fine_hbm, fine_ref, fine_sem)]
    copies = [
        pltpu.make_async_copy(kinds_hbm, kinds_ref, kinds_sem),
        pltpu.make_async_copy(sec_hbm, sec_ref, sec_sem),
        pltpu.make_async_copy(hist_hbm, hist_ref, hist_sem),
    ]
    for copy in copies + staged:
        copy.start()
    kinds_copy, sec_copy, hist_copy = copies
    first = (lax.axis_index("head") * 2 + lax.axis_index("fsdp")) * 8
    own = select_rows(
        16, 64, lambda i: ((first + (i & 7)) & 31) * 2 + ((first + (i & 7)) >> 5)
    )
    kinds_copy.wait()
    kind = kinds_ref[lax.axis_index("frame")]
    sec_copy.wait()
    section = dot(own, sec_ref[...]).astype(BF)
    for d in range(16):
        out_ref[d, 64:80, :] = section

    @pl.when(kind == 0)
    def _():
        z, core = lax.axis_index("head"), lax.axis_index("fsdp")
        cols = select_columns(256, 128, lambda j: (64 * core + (j & 63)) * 2 + (j >> 6))
        rows = select_rows(
            128, 512, lambda i: (i >> 5) * 128 + ((i >> 1) & 15) * 8 + z * 2 + (i & 1)
        )
        hist_copy.wait()
        out = dot(rows, dot(hist_ref[...], cols).astype(BF)).astype(BF)
        blank = jnp.zeros((32, 128), BF)
        for d in range(16):
            t = d // 4
            out_ref[d, 0:64, :] = jnp.concatenate([out[32 * t : 32 * t + 32], blank], axis=0)

    @pl.when(kind == 1)
    def _():
        cols = select_rows(256, 256, lambda i: (i & 63) * 4 + (i >> 6))
        lanes = select_columns(
            512,
            512,
            lambda j: ((j >> 8) * 2 + ((j >> 2) & 1)) * 128
            + ((j >> 3) & 15) * 8
            + ((j >> 7) & 1) * 4
            + (j & 3),
        )
        hist_copy.wait()
        out = dot(dot(cols, hist_ref[...], ((1,), (1,))).astype(BF), lanes).astype(BF)
        for d in range(16):
            g, q = d // 4, d % 4
            for w in range(4):
                out_ref[d, 16 * w : 16 * w + 16, :] = out[
                    64 * w + 16 * q : 64 * w + 16 * q + 16, 128 * g : 128 * g + 128
                ]

    @pl.when(kind == 2)
    def _():
        lanes = select_columns(
            512, 512, lambda j: ((j >> 3) & 3) * 128 + (j >> 5) * 8 + (j & 7)
        )
        cols = select_rows(256, 256, lambda i: i)
        hist_copy.wait()
        out = dot(dot(cols, hist_ref[...], ((1,), (1,))).astype(BF), lanes).astype(BF)
        for d in range(16):
            for g in range(4):
                out_ref[d, 16 * g : 16 * g + 16, :] = out[
                    16 * d : 16 * d + 16, 128 * g : 128 * g + 128
                ]

    for copy in staged:
        copy.wait()


def prepare(kinds, history, section, patch_fine):
    return pl.pallas_call(
        prepare_kernel,
        out_shape=(
            jax.ShapeDtypeStruct((16, 80, 128), BF),
            jax.ShapeDtypeStruct(patch_fine.shape, BF),
        ),
        in_specs=[ANY] * 4,
        out_specs=(VMEM,) * 2,
        scratch_shapes=[
            pltpu.SMEM((16,), jnp.int32),
            pltpu.VMEM((512, 256), BF),
            pltpu.VMEM((64, 128), BF),
        ]
        + [pltpu.SemaphoreType.DMA] * 4,
        compiler_params=params(60),
        cost_estimate=cost(2e10, 1e6),
        name="prepare",
    )(kinds, history.reshape(512, 256), section.T, patch_fine)


def embed_kernel(
    kinds_ref,
    recv_ref,
    mid_hbm,
    coarse_hbm,
    fine1,
    fine2,
    fine3,
    table_ref,
    out_ref,
    mid_ref,
    coarse_ref,
    mid_buf,
    coarse_buf,
    mid_sem,
    coarse_sems,
):
    del fine1, fine2, fine3, table_ref
    mid_copy = pltpu.make_async_copy(mid_hbm, mid_ref, mid_sem)
    mid_copy.start()
    coarse_copies = []
    for g in range(4):
        part = pl.ds(1024 * g, 1024)
        coarse_copies.append(
            pltpu.make_async_copy(coarse_hbm.at[part], coarse_ref.at[part], coarse_sems.at[g])
        )
        coarse_copies[g].start()
    mid_count = jnp.int32(0)
    coarse_count = jnp.int32(0)
    for s in range(16):
        kind = kinds_ref[s]
        block = recv_ref[s, 0:64, :]
        mid_buf[jnp.where(kind == 1, jnp.minimum(mid_count, 6), 7)] = block
        coarse_buf[jnp.where(kind == 2, jnp.minimum(coarse_count, 7), 8)] = block
        mid_count += jnp.where(kind == 1, 1, 0)
        coarse_count += jnp.where(kind == 2, 1, 0)

        @pl.when(kind == 0)
        def _(block=block):
            out_ref[128:144, 0:128] = block[0:16]
            out_ref[128:144, 128:256] = block[16:32]

    me = lax.axis_index("frame")
    x, y = me & 3, me >> 2
    frames = [((y + d) & 3) * 4 + x for d in range(4)] + [4 * y + i for i in range(4)]
    upper = lax.broadcasted_iota(jnp.int32, (16, 128), 0) < 8
    for i, (row, lane) in enumerate(((128, 256), (144, 0), (144, 128), (144, 256))):
        first, second = (
            recv_ref[f, 64:80, :].astype(F32) for f in (frames[2 * i], frames[2 * i + 1])
        )
        out_ref[row : row + 16, lane : lane + 128] = jnp.where(upper, first, second).astype(BF)
    tokens = jnp.concatenate(
        [mid_buf[0:7, 16 * w : 16 * w + 16, :].reshape(112, 128) for w in range(4)], axis=1
    )
    order = select_columns(512, 512, lambda j: (j & 3) * 128 + (j >> 2))
    tokens = dot(tokens, order).astype(BF)
    mid_copy.wait()
    out_ref[0:112, :] = dot(tokens, mid_ref[...]).astype(BF)
    cells = coarse_buf[0:8].reshape(512, 128)
    order = select_rows(
        512,
        512,
        lambda i: ((i >> 1) & 7) * 64 + (i >> 7) * 16 + (i & 1) * 8 + ((i >> 4) & 7),
    )
    cells = dot(order, cells).astype(BF)
    tokens = jnp.concatenate(
        [
            jnp.concatenate(
                [cells[128 * g + 16 * w : 128 * g + 16 * w + 16] for w in range(8)], axis=1
            )
            for g in range(4)
        ],
        axis=0,
    )
    order = select_columns(1024, 1024, lambda j: (j & 7) * 128 + (j >> 3))
    tokens = dot(tokens, order).astype(BF)
    total = jnp.zeros((16, out_ref.shape[1]), F32)
    for g in range(4):
        coarse_copies[g].wait()
        total += dot(tokens[16 * g : 16 * g + 16], coarse_ref[1024 * g : 1024 * g + 1024, :])
    out_ref[112:128, :] = total.astype(BF)


def embed(kinds, received, patch_mid, patch_coarse, fine):
    return pl.pallas_call(
        embed_kernel,
        out_shape=jax.ShapeDtypeStruct((160, patch_mid.shape[1]), BF),
        in_specs=[SMEM, VMEM] + [ANY] * 6,
        out_specs=VMEM,
        scratch_shapes=[
            pltpu.VMEM(patch_mid.shape, BF),
            pltpu.VMEM(patch_coarse.shape, BF),
            pltpu.VMEM((8, 64, 128), BF),
            pltpu.VMEM((9, 64, 128), BF),
            pltpu.SemaphoreType.DMA,
            pltpu.SemaphoreType.DMA((4,)),
        ],
        compiler_params=params(EMBED),
        cost_estimate=cost(2e9, 5e6),
        name="embed",
    )(kinds, received, patch_mid, patch_coarse, *fine)


def along_head(block):
    ring1, ring3, ring2 = (
        lax.ppermute(block, "head", [(i, (i + d) % 4) for i in range(4)]) for d in (1, 3, 2)
    )
    return block, ring1, ring2, ring3


def other_core(block):
    return lax.ppermute(block, "fsdp", [(0, 1), (1, 0)])


def stack_kernel(ref0, ref1, ref2, ref3, after_ref, out_ref):
    del after_ref
    for d, ref in enumerate((ref0, ref1, ref2, ref3)):
        out_ref[d] = ref[...]


def stack(blocks, after):
    return pl.pallas_call(
        stack_kernel,
        out_shape=jax.ShapeDtypeStruct((4, *blocks[0].shape), BF),
        in_specs=[VMEM] * 4 + [ANY],
        out_specs=VMEM,
        compiler_params=params(),
        cost_estimate=cost(2e10, 1e6),
        name="stack",
    )(*blocks, after)


def place_columns(gathered, full_ref):
    z, core = lax.axis_index("head"), lax.axis_index("fsdp")
    rows = full_ref.shape[0]
    for d, (mine, theirs) in enumerate(zip(*gathered)):
        at = ((z + 4 - d) & 3) * 2
        width = mine.shape[1]
        for ref, column in ((mine, at + core), (theirs, at + 1 - core)):
            full_ref[:, pl.ds(pl.multiple_of(column * width, 128), width)] = ref[0:rows]


def fold_kernel(
    same_ref,
    other_ref,
    mod_ref,
    w_ref,
    perm_ref,
    after_ref,
    fold_ref,
    gram_ref,
    full_ref,
):
    del after_ref
    place_columns([[ref.at[d] for d in range(4)] for ref in (same_ref, other_ref)], full_ref)
    order = select_rows(64, 64, lambda i: (i & 31) * 2 + (i >> 5))
    raw = full_ref[...]
    width = raw.shape[1]
    weight = dot(order, raw)
    low = weight.astype(BF)
    mean = jnp.sum(weight, axis=1, keepdims=True) / width
    mean_row = dot(jnp.ones((8, width), BF), low, ((1,), (1,)))[0:1] / width
    gram_ref[...] = dot(low, low, ((1,), (1,))) / width - mean * mean_row
    scaled = (weight - mean) * (1.0 + mod_ref[1:2, :])
    shift_high, shift_low = split(mod_ref[0:1, :])
    pad = jnp.zeros((14, width), BF)
    high, rest = split(scaled)
    left = jnp.concatenate(
        [high, rest, jnp.concatenate([shift_high, shift_low, pad], axis=0)], axis=0
    )
    for part in range(3):
        product = dot(left, w_ref[part])
        matrix = product[0:64] + product[64:128]
        bias = product[128:129] + product[129:130]
        columns = matrix.shape[1]
        high, rest = split(matrix)
        bias_high, bias_low = split(bias)
        rows = jnp.concatenate(
            [
                high.astype(F32),
                rest.astype(F32),
                bias_high.astype(F32),
                bias_high.astype(F32),
                bias_low.astype(F32),
                jnp.zeros((13, columns), F32),
            ],
            axis=0,
        ).astype(BF)
        if part < 2:
            rows = jnp.concatenate(
                [
                    dot(rows[:, HEAD_DIM * h : HEAD_DIM * (h + 1)], perm_ref[...]).astype(BF)
                    for h in range(columns // HEAD_DIM)
                ],
                axis=1,
            )
        fold_ref[part] = rows


def fold(same, other, modulation, w_qkv, perm, after):
    width, columns = w_qkv.shape[1], w_qkv.shape[2]
    return pl.pallas_call(
        fold_kernel,
        out_shape=(
            jax.ShapeDtypeStruct((3, 144, columns), BF),
            jax.ShapeDtypeStruct((64, 64), F32),
        ),
        in_specs=[VMEM] * 5 + [ANY],
        out_specs=(VMEM, VMEM),
        scratch_shapes=[pltpu.VMEM((64, width), BF)],
        compiler_params=params(),
        cost_estimate=cost(1e6, 1e4),
        name="fold",
    )(same, other, modulation, w_qkv, perm, after)


def along_x(value, d):
    return lax.ppermute(value, "frame", [(i, i // 4 * 4 + (i + d) % 4) for i in range(16)])


def along_y(value, d):
    return lax.ppermute(value, "frame", [(i, (i + 4 * d) % 16) for i in range(16)])


def spread_of(patches, gram):
    one, rest = split(gram)
    two, three = split(gram - one.astype(F32))
    parts = jnp.concatenate([one, two, three], axis=1)
    spread = dot(parts, jnp.concatenate([patches, patches, patches], axis=0))
    variance = jnp.sum(spread * patches.astype(F32), axis=0, keepdims=True)
    return jnp.maximum(variance, 0.0) + EPS


def extended(patches, variance):
    high, low = split(jnp.sqrt(variance))
    rows = lax.broadcasted_iota(jnp.int32, (16, patches.shape[1]), 0)
    extra = jnp.where(
        rows == 1,
        low.astype(F32),
        jnp.where((rows == 0) | (rows == 2), high.astype(F32), 0.0),
    ).astype(BF)
    return jnp.concatenate([patches, patches, extra], axis=0)


def turned_columns(raw, variance, cosine, sine, scale):
    square = jnp.sum(raw * raw, axis=0, keepdims=True) / HEAD_DIM
    factor = lax.rsqrt(square + EPS * variance) * scale
    a, b = raw[0:64] * factor, raw[64:128] * factor
    return jnp.concatenate([a * cosine - b * sine, b * cosine + a * sine], axis=0).astype(BF)


def token_kernel(
    kinds_ref,
    mine0,
    mine1,
    mine2,
    mine3,
    theirs0,
    theirs1,
    theirs2,
    theirs3,
    fold_ref,
    gram_ref,
    cos_ref,
    sin_ref,
    time_ref,
    query_ref,
    key_ref,
    value_ref,
    fine_buf,
    sec_buf,
):
    me = lax.axis_index("frame")
    x, y = me & 3, me >> 2
    heads = query_ref.shape[0] // HEAD_DIM
    columns = [((y + d) & 3) * 4 + x for d in range(4)]

    def block(ref, f):
        return ref[:, pl.ds(pl.multiple_of(f * 128, 128), 128)]

    z, core = lax.axis_index("head"), lax.axis_index("fsdp")
    mine_refs, theirs_refs = (mine0, mine1, mine2, mine3), (theirs0, theirs1, theirs2, theirs3)
    for d, (mine_ref, theirs_ref) in enumerate(zip(mine_refs, theirs_refs)):
        at = (z + 4 - d) & 3
        for i, (row, lane) in enumerate(((128, 256), (144, 0), (144, 128), (144, 256))):
            mine, theirs = (
                ref[row : row + 16, lane : lane + 128].astype(F32) for ref in (mine_ref, theirs_ref)
            )
            first, second = jnp.where(core == 0, mine, theirs), jnp.where(core == 0, theirs, mine)
            for k, part in enumerate((slice(0, 8), slice(8, 16))):
                sec_buf[
                    pl.ds(pl.multiple_of(16 * at, 16), 16), 128 * (2 * i + k) : 128 * (2 * i + k + 1)
                ] = jnp.concatenate([first[part], second[part]], axis=0).astype(BF)
        mine, theirs = (
            jnp.concatenate([ref[128:144, 0:128], ref[128:144, 128:256]], axis=0).astype(F32)
            for ref in (mine_ref, theirs_ref)
        )
        first, second = jnp.where(core == 0, mine, theirs), jnp.where(core == 0, theirs, mine)
        fine_buf[:, pl.ds(pl.multiple_of(at * 128, 128), 128)] = jnp.concatenate(
            [
                jnp.concatenate([first[:, 0:64], second[:, 0:64]], axis=1),
                jnp.concatenate([first[:, 64:128], second[:, 64:128]], axis=1),
            ],
            axis=0,
        ).astype(BF)
    patches = jnp.concatenate([sec_buf[...], fine_buf[...]], axis=1)
    variance = spread_of(patches, gram_ref[...])
    inverse = lax.rsqrt(variance)
    patches = extended(patches, variance)
    cosine = jnp.concatenate([block(cos_ref, f) for f in columns], axis=1)
    sine = jnp.concatenate([block(sin_ref, f) for f in columns], axis=1)
    row = pl.ds(pl.multiple_of(y * 512, 128), 512)
    key_cos, key_sin = cos_ref[:, row], sin_ref[:, row]
    slab = jnp.int32(0)
    for s in range(16):
        slab += jnp.where(kinds_ref[s] == 0, s, 0)
    angles = time_ref[...] * (4 * slab + y).astype(F32)
    fine_cos = jnp.concatenate([jnp.concatenate([jnp.cos(angles)] * 4, axis=1), key_cos[8:]], axis=0)
    fine_sin = jnp.concatenate([jnp.concatenate([jnp.sin(angles)] * 4, axis=1), key_sin[8:]], axis=0)
    key_cos = jnp.concatenate([key_cos, fine_cos], axis=1)
    key_sin = jnp.concatenate([key_sin, fine_sin], axis=1)
    for h in range(heads):
        at = slice(HEAD_DIM * h, HEAD_DIM * (h + 1))
        raw = dot(fold_ref[0][:, at], patches[:, 0:512], ((0,), (0,)))
        query_ref[at, :] = turned_columns(raw, variance[:, 0:512], cosine, sine, QUERY_SCALE)
        raw = dot(fold_ref[1][:, at], patches[:, 512:], ((0,), (0,)))
        key_ref[at, :] = turned_columns(raw, variance[:, 512:], key_cos, key_sin, 1.0)
        raw = dot(fold_ref[2][:, at], patches[:, 512:], ((0,), (0,)))
        value_ref[at, :] = (raw * inverse[:, 512:]).astype(BF)


def make_tokens(kinds, gathered, folded, gram, cosine, sine, times):
    columns = folded.shape[2]
    return pl.pallas_call(
        token_kernel,
        out_shape=(
            jax.ShapeDtypeStruct((columns, 512), BF),
            jax.ShapeDtypeStruct((columns, 1024), BF),
            jax.ShapeDtypeStruct((columns, 1024), BF),
        ),
        in_specs=[SMEM] + [VMEM] * 13,
        out_specs=tuple([VMEM] * 3),
        scratch_shapes=[pltpu.VMEM((64, 512), BF), pltpu.VMEM((64, 1024), BF)],
        compiler_params=params(),
        cost_estimate=cost(2e9, 8e6),
        name="tokens",
    )(kinds, *gathered[0], *gathered[1], folded, gram, cosine, sine, times)


def near_kernel(query_ref, key_ref, value_ref, num_ref, den_ref):
    heads = query_ref.shape[0] // HEAD_DIM
    for h in range(heads):
        at = slice(HEAD_DIM * h, HEAD_DIM * (h + 1))
        weights = jnp.exp2(dot(key_ref[at, :], query_ref[at, :], ((0,), (0,))))
        den_ref[h : h + 1, :] = jnp.sum(weights, axis=0, keepdims=True)
        num_ref[at, :] = dot(value_ref[at, :], weights.astype(BF))


def attend_near(queries, keys, values):
    columns, count = queries.shape
    return pl.pallas_call(
        near_kernel,
        out_shape=(
            jax.ShapeDtypeStruct((columns, count), F32),
            jax.ShapeDtypeStruct((8, count), F32),
        ),
        in_specs=[VMEM] * 3,
        out_specs=(VMEM, VMEM),
        compiler_params=params(),
        cost_estimate=cost(4e9, 1e7, 2e6),
        name="near",
    )(queries, keys, values)


def row_angles(kinds_ref, freq_ref):
    me = lax.axis_index("frame")
    row = lax.broadcasted_iota(jnp.int32, (128, 128), 0)
    slot = row >> 4
    slab = jnp.zeros((128, 128), F32)
    mid_count = jnp.int32(0)
    coarse_count = jnp.int32(0)
    coarse_slot = jnp.where(slot == 7, (row >> 1) & 7, -1)
    for s in range(16):
        kind = kinds_ref[s]
        is_mid, is_coarse = kind == 1, kind == 2
        slab = jnp.where(slot == jnp.where(is_mid, mid_count, 99), float(s), slab)
        slab = jnp.where(coarse_slot == jnp.where(is_coarse, coarse_count, 99), float(s), slab)
        mid_count += jnp.where(is_mid, 1, 0)
        coarse_count += jnp.where(is_coarse, 1, 0)
    coarse = slot == 7
    whole = me.astype(F32)
    quarter = (me & 3).astype(F32)
    frame_half = (me >> 3).astype(F32)
    row_half = ((me >> 2) & 1).astype(F32)
    t = 4.0 * slab + jnp.where(coarse, 1.5, 2.0 * frame_half + 0.5)
    h = jnp.where(coarse, 3.5, 4.0 * row_half + 1.5)
    w = jnp.where(
        coarse,
        8.0 * (2.0 * whole + (row & 1).astype(F32)) + 3.5,
        4.0 * (16.0 * quarter + (row & 15).astype(F32)) + 1.5,
    )
    freq_t, freq_h, freq_w, sign = (freq_ref[i : i + 1, :] for i in range(4))
    angles = t * freq_t + h * freq_h + w * freq_w
    return jnp.cos(angles), jnp.sin(angles) * sign


def table_kernel(kinds_ref, freq_ref, after_ref, table_ref):
    del after_ref
    table_ref[0], table_ref[1] = row_angles(kinds_ref, freq_ref)


def make_table(kinds, freqs, after):
    return pl.pallas_call(
        table_kernel,
        out_shape=jax.ShapeDtypeStruct((2, 128, HEAD_DIM), F32),
        in_specs=[SMEM, VMEM, ANY],
        out_specs=VMEM,
        compiler_params=params(),
        cost_estimate=cost(1e5, 1e3),
        name="table",
    )(kinds, freqs, after)


def far_kernel(
    mine0,
    mine1,
    mine2,
    mine3,
    theirs0,
    theirs1,
    theirs2,
    theirs3,
    mod_ref,
    w_ref,
    perm_ref,
    table_ref,
    out_ref,
    full_ref,
):
    place_columns(((mine0, mine1, mine2, mine3), (theirs0, theirs1, theirs2, theirs3)), full_ref)
    heads = out_ref.shape[2] // HEAD_DIM
    x = full_ref[...].astype(F32)
    x = x - jnp.mean(x, axis=1, keepdims=True)
    x = x * lax.rsqrt(jnp.mean(x * x, axis=1, keepdims=True) + EPS)
    x = (x * (1.0 + mod_ref[1:2, :]) + mod_ref[0:1, :]).astype(BF)
    raw_keys = dot(x, w_ref[1])
    out_ref[1] = dot(x, w_ref[2]).astype(BF)
    cosine, sine = table_ref[0], table_ref[1]
    for h in range(heads):
        at = slice(HEAD_DIM * h, HEAD_DIM * (h + 1))
        raw = raw_keys[:, at]
        raw = raw * lax.rsqrt(jnp.mean(raw * raw, axis=1, keepdims=True) + EPS)
        high, rest = split(raw)
        raw = dot(high, perm_ref[...]) + dot(rest, perm_ref[...])
        out_ref[0, :, at] = (raw * cosine + pltpu.roll(raw, 64, 1) * sine).astype(BF)


def make_far(gathered, modulation, w_qkv, perm, table):
    columns = w_qkv.shape[2]
    return pl.pallas_call(
        far_kernel,
        out_shape=jax.ShapeDtypeStruct((2, 128, columns), BF),
        in_specs=[VMEM] * 12,
        out_specs=VMEM,
        scratch_shapes=[pltpu.VMEM((128, w_qkv.shape[1]), BF)],
        compiler_params=params(),
        cost_estimate=cost(2e9, 1e7),
        name="far",
    )(*gathered[0], *gathered[1], modulation, w_qkv, perm, table)


def history_kernel(far0, far1, far3, far2, query_ref, num_ref, den_ref, out0, out1, out2, out3):
    heads = query_ref.shape[0] // HEAD_DIM
    count = query_ref.shape[1]
    outs = (out0, out1, out2, out3)
    rows = lax.broadcasted_iota(jnp.int32, (16, count), 0)
    tail = jnp.zeros((16, count), F32)
    for h in range(heads):
        at = slice(HEAD_DIM * h, HEAD_DIM * (h + 1))
        fars = (far0, far1, far3, far2)
        keys = jnp.concatenate([far[0, :, at] for far in fars], axis=0)
        values = jnp.concatenate([far[1, :, at] for far in fars], axis=0)
        weights = jnp.exp2(dot(keys, query_ref[at, :]))
        high, rest = split(den_ref[h : h + 1, :] + jnp.sum(weights, axis=0, keepdims=True))
        tail = jnp.where(rows == h, high.astype(F32), tail)
        tail = jnp.where(rows == heads + h, rest.astype(F32), tail)
        part = num_ref[at, :] + dot(values, weights.astype(BF), ((0,), (0,)))
        for d, out in enumerate(outs):
            out[at, :] = part[:, 128 * d : 128 * d + 128].astype(out.dtype)
    for d, out in enumerate(outs):
        out[HEAD_DIM * heads :, :] = tail[:, 128 * d : 128 * d + 128].astype(out.dtype)


def attend_history(fars, queries, numerator, denominator):
    columns = queries.shape[0]
    return pl.pallas_call(
        history_kernel,
        out_shape=tuple(jax.ShapeDtypeStruct((columns + 16, 128), t) for t in (F32, BF, BF, BF)),
        in_specs=[VMEM] * 7,
        out_specs=tuple([VMEM] * 4),
        compiler_params=params(),
        cost_estimate=cost(2e9, 4e6, 1e6),
        name="history",
    )(*fars, queries, numerator, denominator)


def combine_kernel(part0, part1, part2, part3, out_ref):
    columns = out_ref.shape[1]
    heads = columns // HEAD_DIM
    total = sum(part[...].astype(F32) for part in (part0, part1, part2, part3))
    for h in range(heads):
        at = slice(HEAD_DIM * h, HEAD_DIM * (h + 1))
        low = columns + heads + h
        denominator = total[columns + h : columns + h + 1] + total[low : low + 1]
        out_ref[:, at] = jnp.transpose(total[at] / denominator).astype(BF)


def combine(parts):
    return pl.pallas_call(
        combine_kernel,
        out_shape=jax.ShapeDtypeStruct((128, parts[0].shape[0] - 16), BF),
        in_specs=[VMEM] * 4,
        out_specs=VMEM,
        compiler_params=params(),
        cost_estimate=cost(1e7, 2e6),
        name="combine",
    )(*parts)


def per_device(
    history, section, slab_kernel, patch_fine, patch_mid, patch_coarse, modulation, w_qkv
):
    frames = lax.axis_size("frame")
    cos_table, sin_table = section_tables(frames, section.shape[0])
    cosine, sine = jnp.asarray(cos_table), jnp.asarray(sin_table)
    perm = jnp.asarray(head_permutation(), BF)
    lane_table = lane_frequencies()
    freqs = jnp.asarray(lane_table)
    times = jnp.asarray(np.repeat(lane_table[0, 0:8, None], 128, axis=1))

    sent, patch_fine = prepare(slab_kernel, history, section, patch_fine)
    received = lax.all_to_all(sent, "frame", 0, 0, tiled=True)
    fine = along_head(patch_fine)
    table = make_table(slab_kernel, freqs, sent)
    features = embed(slab_kernel, received, patch_mid, patch_coarse, (*fine[1:], table))
    mine = along_head(features)
    gathered = mine, tuple(other_core(block) for block in mine)
    far = make_far(gathered, modulation, w_qkv, perm, table)
    far2, far1, far3 = (along_x(far, d) for d in (2, 1, 3))
    fine_same = stack(fine, features)
    folded, gram = fold(fine_same, other_core(fine_same), modulation, w_qkv, perm, far)
    queries, keys, values = make_tokens(
        slab_kernel, gathered, folded, gram, cosine, sine, times
    )
    numerator, denominator = attend_near(queries, keys, values)
    fars = [far, far2, far3, far1]
    parts = attend_history(fars, queries, numerator, denominator)
    part2 = along_y(parts[2], 2)
    return combine([parts[0], along_y(parts[1], 1), part2, along_y(parts[3], 3)])


def solution(mesh):
    in_specs = (
        P("frame", None, None, None),
        P("frame", None),
        P(),
        P(None, ("head", "fsdp")),
        P(None, ("head", "fsdp")),
        P(None, ("head", "fsdp")),
        P(),
        P(None, None, ("head", "fsdp")),
    )
    out_specs = P("frame", ("head", "fsdp"))
    return jax.shard_map(
        per_device, mesh=mesh, in_specs=in_specs, out_specs=out_specs, check_vma=False
    )
```

```python
import functools

import jax
import jax.numpy as jnp
import numpy as np
from jax import lax
from jax.experimental import pallas as pl
from jax.experimental.pallas import tpu as pltpu
from jax.sharding import PartitionSpec as P

HEAD_DIM = 128
PARTS = (16, 56, 56)
THETA = 256.0
EPS = 1e-06
QUERY_SCALE = float(np.log2(np.e) * HEAD_DIM**-0.5)
EMBED = 52
BF = jnp.bfloat16
F32 = jnp.float32
VMEM = pl.BlockSpec(memory_space=pltpu.VMEM)
ANY = pl.BlockSpec(memory_space=pl.ANY)
SMEM = pl.BlockSpec(memory_space=pltpu.SMEM)


def params(mib=10):
    return pltpu.CompilerParams(vmem_limit_bytes=mib * 2**20)


def cost(flops, bytes_accessed, transcendentals=0):
    return pl.CostEstimate(
        flops=int(flops), bytes_accessed=int(bytes_accessed), transcendentals=int(transcendentals)
    )


def pair_tables():
    freqs = np.zeros((3, 64), np.float64)
    first, second = [], []
    pair, offset = 0, 0
    for axis, width in enumerate(PARTS):
        half = width // 2
        for i in range(half):
            freqs[axis, pair] = THETA ** (-2.0 * i / width)
            first.append(offset + i)
            second.append(offset + i + half)
            pair += 1
        offset += width
    return freqs, np.array(first + second)


def section_tables(frames, per_frame):
    freqs, _ = pair_tables()
    rows = np.arange(frames * per_frame)
    pos = np.stack(
        [4.0 * frames + rows // 512, 2.0 * (rows // 128 % 4) + 0.5, 2.0 * (rows % 128) + 0.5]
    )
    angles = freqs.T @ pos
    return np.cos(angles).astype(np.float32), np.sin(angles).astype(np.float32)


def head_permutation():
    _, order = pair_tables()
    perm = np.zeros((HEAD_DIM, HEAD_DIM), np.float32)
    perm[order, np.arange(HEAD_DIM)] = 1.0
    return perm


def lane_frequencies():
    freqs, _ = pair_tables()
    table = np.zeros((8, HEAD_DIM), np.float32)
    table[:3] = np.concatenate([freqs, freqs], axis=1)
    table[3] = np.concatenate([-np.ones(64), np.ones(64)])
    return table


def dot(a, b, dims=((1,), (0,))):
    return lax.dot_general(a, b, (dims, ((), ())), preferred_element_type=F32)


def select_columns(rows, columns, source):
    j = lax.broadcasted_iota(jnp.int32, (8, columns), 1)[0:1]
    i = lax.broadcasted_iota(jnp.int32, (rows, columns), 0)
    return jnp.where(i == source(j), 1.0, 0.0).astype(BF)


def select_rows(rows, columns, source):
    j = lax.broadcasted_iota(jnp.int32, (rows, columns), 1)
    i = lax.broadcasted_iota(jnp.int32, (rows, 128), 0)[:, 0:1]
    return jnp.where(j == source(i), 1.0, 0.0).astype(BF)


def split(value):
    high = value.astype(BF)
    return high, (value - high.astype(F32)).astype(BF)


def prepare_kernel(
    kinds_hbm,
    hist_hbm,
    sec_hbm,
    fine_hbm,
    out_ref,
    fine_ref,
    kinds_ref,
    hist_ref,
    sec_ref,
    kinds_sem,
    hist_sem,
    sec_sem,
    fine_sem,
):
    staged = [pltpu.make_async_copy(fine_hbm, fine_ref, fine_sem)]
    copies = [
        pltpu.make_async_copy(kinds_hbm, kinds_ref, kinds_sem),
        pltpu.make_async_copy(sec_hbm, sec_ref, sec_sem),
        pltpu.make_async_copy(hist_hbm, hist_ref, hist_sem),
    ]
    for copy in copies + staged:
        copy.start()
    kinds_copy, sec_copy, hist_copy = copies
    first = (lax.axis_index("head") * 2 + lax.axis_index("fsdp")) * 8
    own = select_rows(
        16, 64, lambda i: ((first + (i & 7)) & 31) * 2 + ((first + (i & 7)) >> 5)
    )
    kinds_copy.wait()
    kind = kinds_ref[lax.axis_index("frame")]
    sec_copy.wait()
    section = dot(own, sec_ref[...]).astype(BF)
    for d in range(16):
        out_ref[d, 64:80, :] = section

    @pl.when(kind == 0)
    def _():
        z, core = lax.axis_index("head"), lax.axis_index("fsdp")
        cols = select_columns(256, 128, lambda j: (64 * core + (j & 63)) * 2 + (j >> 6))
        rows = select_rows(
            128, 512, lambda i: (i >> 5) * 128 + ((i >> 1) & 15) * 8 + z * 2 + (i & 1)
        )
        hist_copy.wait()
        out = dot(rows, dot(hist_ref[...], cols).astype(BF)).astype(BF)
        blank = jnp.zeros((32, 128), BF)
        for d in range(16):
            t = d // 4
            out_ref[d, 0:64, :] = jnp.concatenate([out[32 * t : 32 * t + 32], blank], axis=0)

    @pl.when(kind == 1)
    def _():
        cols = select_rows(256, 256, lambda i: (i & 63) * 4 + (i >> 6))
        lanes = select_columns(
            512,
            512,
            lambda j: ((j >> 8) * 2 + ((j >> 2) & 1)) * 128
            + ((j >> 3) & 15) * 8
            + ((j >> 7) & 1) * 4
            + (j & 3),
        )
        hist_copy.wait()
        out = dot(dot(cols, hist_ref[...], ((1,), (1,))).astype(BF), lanes).astype(BF)
        for d in range(16):
            g, q = d // 4, d % 4
            for w in range(4):
                out_ref[d, 16 * w : 16 * w + 16, :] = out[
                    64 * w + 16 * q : 64 * w + 16 * q + 16, 128 * g : 128 * g + 128
                ]

    @pl.when(kind == 2)
    def _():
        lanes = select_columns(
            512, 512, lambda j: ((j >> 3) & 3) * 128 + (j >> 5) * 8 + (j & 7)
        )
        cols = select_rows(256, 256, lambda i: i)
        hist_copy.wait()
        out = dot(dot(cols, hist_ref[...], ((1,), (1,))).astype(BF), lanes).astype(BF)
        for d in range(16):
            for g in range(4):
                out_ref[d, 16 * g : 16 * g + 16, :] = out[
                    16 * d : 16 * d + 16, 128 * g : 128 * g + 128
                ]

    for copy in staged:
        copy.wait()


def prepare(kinds, history, section, patch_fine):
    return pl.pallas_call(
        prepare_kernel,
        out_shape=(
            jax.ShapeDtypeStruct((16, 80, 128), BF),
            jax.ShapeDtypeStruct(patch_fine.shape, BF),
        ),
        in_specs=[ANY] * 4,
        out_specs=(VMEM,) * 2,
        scratch_shapes=[
            pltpu.SMEM((16,), jnp.int32),
            pltpu.VMEM((512, 256), BF),
            pltpu.VMEM((64, 128), BF),
        ]
        + [pltpu.SemaphoreType.DMA] * 4,
        compiler_params=params(60),
        cost_estimate=cost(2e10, 1e6),
        name="prepare",
    )(kinds, history.reshape(512, 256), section.T, patch_fine)


def embed_kernel(
    kinds_ref,
    recv_ref,
    mid_ref,
    coarse_hbm,
    fine1,
    fine2,
    fine3,
    table_ref,
    out_ref,
    coarse_ref,
    mid_buf,
    coarse_buf,
    coarse_sems,
):
    del fine1, fine2, fine3, table_ref
    coarse_copies = []
    for g in range(4):
        part = pl.ds(1024 * g, 1024)
        coarse_copies.append(
            pltpu.make_async_copy(coarse_hbm.at[part], coarse_ref.at[part], coarse_sems.at[g])
        )
        coarse_copies[g].start()
    mid_count = jnp.int32(0)
    coarse_count = jnp.int32(0)
    for s in range(16):
        kind = kinds_ref[s]
        block = recv_ref[s, 0:64, :]
        mid_buf[jnp.where(kind == 1, jnp.minimum(mid_count, 6), 7)] = block
        coarse_buf[jnp.where(kind == 2, jnp.minimum(coarse_count, 7), 8)] = block
        mid_count += jnp.where(kind == 1, 1, 0)
        coarse_count += jnp.where(kind == 2, 1, 0)

        @pl.when(kind == 0)
        def _(block=block):
            out_ref[128:144, 0:128] = block[0:16]
            out_ref[128:144, 128:256] = block[16:32]

    me = lax.axis_index("frame")
    x, y = me & 3, me >> 2
    frames = [((y + d) & 3) * 4 + x for d in range(4)] + [4 * y + i for i in range(4)]
    upper = lax.broadcasted_iota(jnp.int32, (16, 128), 0) < 8
    for i, (row, lane) in enumerate(((128, 256), (144, 0), (144, 128), (144, 256))):
        first, second = (
            recv_ref[f, 64:80, :].astype(F32) for f in (frames[2 * i], frames[2 * i + 1])
        )
        out_ref[row : row + 16, lane : lane + 128] = jnp.where(upper, first, second).astype(BF)
    tokens = jnp.concatenate(
        [mid_buf[0:7, 16 * w : 16 * w + 16, :].reshape(112, 128) for w in range(4)], axis=1
    )
    order = select_columns(512, 512, lambda j: (j & 3) * 128 + (j >> 2))
    tokens = dot(tokens, order).astype(BF)
    out_ref[0:112, :] = dot(tokens, mid_ref[...]).astype(BF)
    cells = coarse_buf[0:8].reshape(512, 128)
    order = select_rows(
        512,
        512,
        lambda i: ((i >> 1) & 7) * 64 + (i >> 7) * 16 + (i & 1) * 8 + ((i >> 4) & 7),
    )
    cells = dot(order, cells).astype(BF)
    tokens = jnp.concatenate(
        [
            jnp.concatenate(
                [cells[128 * g + 16 * w : 128 * g + 16 * w + 16] for w in range(8)], axis=1
            )
            for g in range(4)
        ],
        axis=0,
    )
    order = select_columns(1024, 1024, lambda j: (j & 7) * 128 + (j >> 3))
    tokens = dot(tokens, order).astype(BF)
    total = jnp.zeros((16, out_ref.shape[1]), F32)
    for g in range(4):
        coarse_copies[g].wait()
        total += dot(tokens[16 * g : 16 * g + 16], coarse_ref[1024 * g : 1024 * g + 1024, :])
    out_ref[112:128, :] = total.astype(BF)


def embed(kinds, received, patch_mid, patch_coarse, fine):
    return pl.pallas_call(
        embed_kernel,
        out_shape=jax.ShapeDtypeStruct((160, patch_mid.shape[1]), BF),
        in_specs=[SMEM, VMEM, VMEM] + [ANY] * 5,
        out_specs=VMEM,
        scratch_shapes=[
            pltpu.VMEM(patch_coarse.shape, BF),
            pltpu.VMEM((8, 64, 128), BF),
            pltpu.VMEM((9, 64, 128), BF),
            pltpu.SemaphoreType.DMA((4,)),
        ],
        compiler_params=params(EMBED),
        cost_estimate=cost(2e9, 5e6),
        name="embed",
    )(kinds, received, patch_mid, patch_coarse, *fine)


def along_head(block):
    ring1, ring3, ring2 = (
        lax.ppermute(block, "head", [(i, (i + d) % 4) for i in range(4)]) for d in (1, 3, 2)
    )
    return block, ring1, ring2, ring3


def other_core(block):
    return lax.ppermute(block, "fsdp", [(0, 1), (1, 0)])


def stack_kernel(ref0, ref1, ref2, ref3, after_ref, out_ref):
    del after_ref
    for d, ref in enumerate((ref0, ref1, ref2, ref3)):
        out_ref[d] = ref[...]


def stack(blocks, after):
    return pl.pallas_call(
        stack_kernel,
        out_shape=jax.ShapeDtypeStruct((4, *blocks[0].shape), BF),
        in_specs=[VMEM] * 4 + [ANY],
        out_specs=VMEM,
        compiler_params=params(),
        cost_estimate=cost(2e10, 1e6),
        name="stack",
    )(*blocks, after)


def place_columns(gathered, full_ref):
    z, core = lax.axis_index("head"), lax.axis_index("fsdp")
    rows = full_ref.shape[0]
    for d, (mine, theirs) in enumerate(zip(*gathered)):
        at = ((z + 4 - d) & 3) * 2
        width = mine.shape[1]
        for ref, column in ((mine, at + core), (theirs, at + 1 - core)):
            full_ref[:, pl.ds(pl.multiple_of(column * width, 128), width)] = ref[0:rows]


def fold_kernel(
    same_ref,
    other_ref,
    mod_ref,
    w_ref,
    perm_ref,
    after_ref,
    fold_ref,
    gram_ref,
    full_ref,
):
    del after_ref
    place_columns([[ref.at[d] for d in range(4)] for ref in (same_ref, other_ref)], full_ref)
    order = select_rows(64, 64, lambda i: (i & 31) * 2 + (i >> 5))
    raw = full_ref[...]
    width = raw.shape[1]
    weight = dot(order, raw)
    low = weight.astype(BF)
    mean = jnp.sum(weight, axis=1, keepdims=True) / width
    mean_row = dot(jnp.ones((8, width), BF), low, ((1,), (1,)))[0:1] / width
    gram_ref[...] = dot(low, low, ((1,), (1,))) / width - mean * mean_row
    scaled = (weight - mean) * (1.0 + mod_ref[1:2, :])
    shift_high, shift_low = split(mod_ref[0:1, :])
    pad = jnp.zeros((14, width), BF)
    high, rest = split(scaled)
    left = jnp.concatenate(
        [high, rest, jnp.concatenate([shift_high, shift_low, pad], axis=0)], axis=0
    )
    for part in range(3):
        product = dot(left, w_ref[part])
        matrix = product[0:64] + product[64:128]
        bias = product[128:129] + product[129:130]
        columns = matrix.shape[1]
        high, rest = split(matrix)
        bias_high, bias_low = split(bias)
        rows = jnp.concatenate(
            [
                high.astype(F32),
                rest.astype(F32),
                bias_high.astype(F32),
                bias_high.astype(F32),
                bias_low.astype(F32),
                jnp.zeros((13, columns), F32),
            ],
            axis=0,
        ).astype(BF)
        if part < 2:
            rows = jnp.concatenate(
                [
                    dot(rows[:, HEAD_DIM * h : HEAD_DIM * (h + 1)], perm_ref[...]).astype(BF)
                    for h in range(columns // HEAD_DIM)
                ],
                axis=1,
            )
        fold_ref[part] = rows


def fold(same, other, modulation, w_qkv, perm, after):
    width, columns = w_qkv.shape[1], w_qkv.shape[2]
    return pl.pallas_call(
        fold_kernel,
        out_shape=(
            jax.ShapeDtypeStruct((3, 144, columns), BF),
            jax.ShapeDtypeStruct((64, 64), F32),
        ),
        in_specs=[VMEM] * 5 + [ANY],
        out_specs=(VMEM, VMEM),
        scratch_shapes=[pltpu.VMEM((64, width), BF)],
        compiler_params=params(),
        cost_estimate=cost(1e6, 1e4),
        name="fold",
    )(same, other, modulation, w_qkv, perm, after)


def along_x(value, d):
    return lax.ppermute(value, "frame", [(i, i // 4 * 4 + (i + d) % 4) for i in range(16)])


def along_y(value, d):
    return lax.ppermute(value, "frame", [(i, (i + 4 * d) % 16) for i in range(16)])


def spread_of(patches, gram):
    one, rest = split(gram)
    two, three = split(gram - one.astype(F32))
    parts = jnp.concatenate([one, two, three], axis=1)
    spread = dot(parts, jnp.concatenate([patches, patches, patches], axis=0))
    variance = jnp.sum(spread * patches.astype(F32), axis=0, keepdims=True)
    return jnp.maximum(variance, 0.0) + EPS


def extended(patches, variance):
    high, low = split(jnp.sqrt(variance))
    rows = lax.broadcasted_iota(jnp.int32, (16, patches.shape[1]), 0)
    extra = jnp.where(
        rows == 1,
        low.astype(F32),
        jnp.where((rows == 0) | (rows == 2), high.astype(F32), 0.0),
    ).astype(BF)
    return jnp.concatenate([patches, patches, extra], axis=0)


def turned_columns(raw, variance, cosine, sine, scale):
    square = jnp.sum(raw * raw, axis=0, keepdims=True) / HEAD_DIM
    factor = lax.rsqrt(square + EPS * variance) * scale
    a, b = raw[0:64] * factor, raw[64:128] * factor
    return jnp.concatenate([a * cosine - b * sine, b * cosine + a * sine], axis=0).astype(BF)


def token_kernel(
    kinds_ref,
    mine0,
    mine1,
    mine2,
    mine3,
    theirs0,
    theirs1,
    theirs2,
    theirs3,
    fold_ref,
    gram_ref,
    cos_ref,
    sin_ref,
    time_ref,
    query_ref,
    key_ref,
    value_ref,
    fine_buf,
    sec_buf,
):
    me = lax.axis_index("frame")
    x, y = me & 3, me >> 2
    heads = query_ref.shape[0] // HEAD_DIM
    columns = [((y + d) & 3) * 4 + x for d in range(4)]

    def block(ref, f):
        return ref[:, pl.ds(pl.multiple_of(f * 128, 128), 128)]

    z, core = lax.axis_index("head"), lax.axis_index("fsdp")
    mine_refs, theirs_refs = (mine0, mine1, mine2, mine3), (theirs0, theirs1, theirs2, theirs3)
    for d, (mine_ref, theirs_ref) in enumerate(zip(mine_refs, theirs_refs)):
        at = (z + 4 - d) & 3
        for i, (row, lane) in enumerate(((128, 256), (144, 0), (144, 128), (144, 256))):
            mine, theirs = (
                ref[row : row + 16, lane : lane + 128].astype(F32) for ref in (mine_ref, theirs_ref)
            )
            first, second = jnp.where(core == 0, mine, theirs), jnp.where(core == 0, theirs, mine)
            for k, part in enumerate((slice(0, 8), slice(8, 16))):
                sec_buf[
                    pl.ds(pl.multiple_of(16 * at, 16), 16), 128 * (2 * i + k) : 128 * (2 * i + k + 1)
                ] = jnp.concatenate([first[part], second[part]], axis=0).astype(BF)
        mine, theirs = (
            jnp.concatenate([ref[128:144, 0:128], ref[128:144, 128:256]], axis=0).astype(F32)
            for ref in (mine_ref, theirs_ref)
        )
        first, second = jnp.where(core == 0, mine, theirs), jnp.where(core == 0, theirs, mine)
        fine_buf[:, pl.ds(pl.multiple_of(at * 128, 128), 128)] = jnp.concatenate(
            [
                jnp.concatenate([first[:, 0:64], second[:, 0:64]], axis=1),
                jnp.concatenate([first[:, 64:128], second[:, 64:128]], axis=1),
            ],
            axis=0,
        ).astype(BF)
    patches = jnp.concatenate([sec_buf[...], fine_buf[...]], axis=1)
    variance = spread_of(patches, gram_ref[...])
    inverse = lax.rsqrt(variance)
    patches = extended(patches, variance)
    cosine = jnp.concatenate([block(cos_ref, f) for f in columns], axis=1)
    sine = jnp.concatenate([block(sin_ref, f) for f in columns], axis=1)
    row = pl.ds(pl.multiple_of(y * 512, 128), 512)
    key_cos, key_sin = cos_ref[:, row], sin_ref[:, row]
    slab = jnp.int32(0)
    for s in range(16):
        slab += jnp.where(kinds_ref[s] == 0, s, 0)
    angles = time_ref[...] * (4 * slab + y).astype(F32)
    fine_cos = jnp.concatenate([jnp.concatenate([jnp.cos(angles)] * 4, axis=1), key_cos[8:]], axis=0)
    fine_sin = jnp.concatenate([jnp.concatenate([jnp.sin(angles)] * 4, axis=1), key_sin[8:]], axis=0)
    key_cos = jnp.concatenate([key_cos, fine_cos], axis=1)
    key_sin = jnp.concatenate([key_sin, fine_sin], axis=1)
    for h in range(heads):
        at = slice(HEAD_DIM * h, HEAD_DIM * (h + 1))
        raw = dot(fold_ref[0][:, at], patches[:, 0:512], ((0,), (0,)))
        query_ref[at, :] = turned_columns(raw, variance[:, 0:512], cosine, sine, QUERY_SCALE)
        raw = dot(fold_ref[1][:, at], patches[:, 512:], ((0,), (0,)))
        key_ref[at, :] = turned_columns(raw, variance[:, 512:], key_cos, key_sin, 1.0)
        raw = dot(fold_ref[2][:, at], patches[:, 512:], ((0,), (0,)))
        value_ref[at, :] = (raw * inverse[:, 512:]).astype(BF)


def make_tokens(kinds, gathered, folded, gram, cosine, sine, times):
    columns = folded.shape[2]
    return pl.pallas_call(
        token_kernel,
        out_shape=(
            jax.ShapeDtypeStruct((columns, 512), BF),
            jax.ShapeDtypeStruct((columns, 1024), BF),
            jax.ShapeDtypeStruct((columns, 1024), BF),
        ),
        in_specs=[SMEM] + [VMEM] * 13,
        out_specs=tuple([VMEM] * 3),
        scratch_shapes=[pltpu.VMEM((64, 512), BF), pltpu.VMEM((64, 1024), BF)],
        compiler_params=params(),
        cost_estimate=cost(2e9, 8e6),
        name="tokens",
    )(kinds, *gathered[0], *gathered[1], folded, gram, cosine, sine, times)


def near_kernel(query_ref, key_ref, value_ref, far_ref, num_ref, den_ref):
    heads = query_ref.shape[0] // HEAD_DIM
    for h in range(heads):
        at = slice(HEAD_DIM * h, HEAD_DIM * (h + 1))
        weights = jnp.exp2(dot(key_ref[at, :], query_ref[at, :], ((0,), (0,))))
        own_weights = jnp.exp2(dot(far_ref[0, :, at], query_ref[at, :]))
        den_ref[h : h + 1, :] = jnp.sum(weights, axis=0, keepdims=True) + jnp.sum(
            own_weights, axis=0, keepdims=True
        )
        num_ref[at, :] = dot(value_ref[at, :], weights.astype(BF)) + dot(
            far_ref[1, :, at], own_weights.astype(BF), ((0,), (0,))
        )


def attend_near(queries, keys, values, far):
    columns, count = queries.shape
    return pl.pallas_call(
        near_kernel,
        out_shape=(
            jax.ShapeDtypeStruct((columns, count), F32),
            jax.ShapeDtypeStruct((8, count), F32),
        ),
        in_specs=[VMEM] * 4,
        out_specs=(VMEM, VMEM),
        compiler_params=params(),
        cost_estimate=cost(4e9, 1e7, 2e6),
        name="near",
    )(queries, keys, values, far)


def row_angles(kinds_ref, freq_ref):
    me = lax.axis_index("frame")
    row = lax.broadcasted_iota(jnp.int32, (128, 128), 0)
    slot = row >> 4
    slab = jnp.zeros((128, 128), F32)
    mid_count = jnp.int32(0)
    coarse_count = jnp.int32(0)
    coarse_slot = jnp.where(slot == 7, (row >> 1) & 7, -1)
    for s in range(16):
        kind = kinds_ref[s]
        is_mid, is_coarse = kind == 1, kind == 2
        slab = jnp.where(slot == jnp.where(is_mid, mid_count, 99), float(s), slab)
        slab = jnp.where(coarse_slot == jnp.where(is_coarse, coarse_count, 99), float(s), slab)
        mid_count += jnp.where(is_mid, 1, 0)
        coarse_count += jnp.where(is_coarse, 1, 0)
    coarse = slot == 7
    whole = me.astype(F32)
    quarter = (me & 3).astype(F32)
    frame_half = (me >> 3).astype(F32)
    row_half = ((me >> 2) & 1).astype(F32)
    t = 4.0 * slab + jnp.where(coarse, 1.5, 2.0 * frame_half + 0.5)
    h = jnp.where(coarse, 3.5, 4.0 * row_half + 1.5)
    w = jnp.where(
        coarse,
        8.0 * (2.0 * whole + (row & 1).astype(F32)) + 3.5,
        4.0 * (16.0 * quarter + (row & 15).astype(F32)) + 1.5,
    )
    freq_t, freq_h, freq_w, sign = (freq_ref[i : i + 1, :] for i in range(4))
    angles = t * freq_t + h * freq_h + w * freq_w
    return jnp.cos(angles), jnp.sin(angles) * sign


def table_kernel(kinds_ref, freq_ref, after_ref, table_ref):
    del after_ref
    table_ref[0], table_ref[1] = row_angles(kinds_ref, freq_ref)


def make_table(kinds, freqs, after):
    return pl.pallas_call(
        table_kernel,
        out_shape=jax.ShapeDtypeStruct((2, 128, HEAD_DIM), F32),
        in_specs=[SMEM, VMEM, ANY],
        out_specs=VMEM,
        compiler_params=params(),
        cost_estimate=cost(1e5, 1e3),
        name="table",
    )(kinds, freqs, after)


def far_kernel(
    mine0,
    mine1,
    mine2,
    mine3,
    theirs0,
    theirs1,
    theirs2,
    theirs3,
    mod_ref,
    w_ref,
    perm_ref,
    table_ref,
    out_ref,
    full_ref,
):
    place_columns(((mine0, mine1, mine2, mine3), (theirs0, theirs1, theirs2, theirs3)), full_ref)
    heads = out_ref.shape[2] // HEAD_DIM
    x = full_ref[...].astype(F32)
    x = x - jnp.mean(x, axis=1, keepdims=True)
    x = x * lax.rsqrt(jnp.mean(x * x, axis=1, keepdims=True) + EPS)
    x = (x * (1.0 + mod_ref[1:2, :]) + mod_ref[0:1, :]).astype(BF)
    raw_keys = dot(x, w_ref[1])
    out_ref[1] = dot(x, w_ref[2]).astype(BF)
    cosine, sine = table_ref[0], table_ref[1]
    for h in range(heads):
        at = slice(HEAD_DIM * h, HEAD_DIM * (h + 1))
        raw = raw_keys[:, at]
        raw = raw * lax.rsqrt(jnp.mean(raw * raw, axis=1, keepdims=True) + EPS)
        high, rest = split(raw)
        raw = dot(high, perm_ref[...]) + dot(rest, perm_ref[...])
        out_ref[0, :, at] = (raw * cosine + pltpu.roll(raw, 64, 1) * sine).astype(BF)


def make_far(gathered, modulation, w_qkv, perm, table):
    columns = w_qkv.shape[2]
    return pl.pallas_call(
        far_kernel,
        out_shape=jax.ShapeDtypeStruct((2, 128, columns), BF),
        in_specs=[VMEM] * 12,
        out_specs=VMEM,
        scratch_shapes=[pltpu.VMEM((128, w_qkv.shape[1]), BF)],
        compiler_params=params(),
        cost_estimate=cost(2e9, 1e7),
        name="far",
    )(*gathered[0], *gathered[1], modulation, w_qkv, perm, table)


def history_kernel(far1, far2, far3, query_ref, num_ref, den_ref, out0, out1, out2, out3):
    heads = query_ref.shape[0] // HEAD_DIM
    count = query_ref.shape[1]
    outs = (out0, out1, out2, out3)
    rows = lax.broadcasted_iota(jnp.int32, (16, count), 0)
    tail = jnp.zeros((16, count), F32)
    for h in range(heads):
        at = slice(HEAD_DIM * h, HEAD_DIM * (h + 1))
        fars = (far1, far2, far3)
        keys = jnp.concatenate([far[0, :, at] for far in fars], axis=0)
        values = jnp.concatenate([far[1, :, at] for far in fars], axis=0)
        weights = jnp.exp2(dot(keys, query_ref[at, :]))
        high, rest = split(den_ref[h : h + 1, :] + jnp.sum(weights, axis=0, keepdims=True))
        tail = jnp.where(rows == h, high.astype(F32), tail)
        tail = jnp.where(rows == heads + h, rest.astype(F32), tail)
        part = num_ref[at, :] + dot(values, weights.astype(BF), ((0,), (0,)))
        for d, out in enumerate(outs):
            out[at, :] = part[:, 128 * d : 128 * d + 128].astype(out.dtype)
    for d, out in enumerate(outs):
        out[HEAD_DIM * heads :, :] = tail[:, 128 * d : 128 * d + 128].astype(out.dtype)


def attend_history(fars, queries, numerator, denominator):
    columns = queries.shape[0]
    return pl.pallas_call(
        history_kernel,
        out_shape=tuple(jax.ShapeDtypeStruct((columns + 16, 128), t) for t in (F32, BF, BF, BF)),
        in_specs=[VMEM] * 6,
        out_specs=tuple([VMEM] * 4),
        compiler_params=params(),
        cost_estimate=cost(2e9, 4e6, 1e6),
        name="history",
    )(*fars, queries, numerator, denominator)


def combine_kernel(part0, part1, part2, part3, out_ref):
    columns = out_ref.shape[1]
    heads = columns // HEAD_DIM
    total = sum(part[...].astype(F32) for part in (part0, part1, part2, part3))
    for h in range(heads):
        at = slice(HEAD_DIM * h, HEAD_DIM * (h + 1))
        low = columns + heads + h
        denominator = total[columns + h : columns + h + 1] + total[low : low + 1]
        out_ref[:, at] = jnp.transpose(total[at] / denominator).astype(BF)


def combine(parts):
    return pl.pallas_call(
        combine_kernel,
        out_shape=jax.ShapeDtypeStruct((128, parts[0].shape[0] - 16), BF),
        in_specs=[VMEM] * 4,
        out_specs=VMEM,
        compiler_params=params(),
        cost_estimate=cost(1e7, 2e6),
        name="combine",
    )(*parts)


def per_device(
    history, section, slab_kernel, patch_fine, patch_mid, patch_coarse, modulation, w_qkv
):
    frames = lax.axis_size("frame")
    cos_table, sin_table = section_tables(frames, section.shape[0])
    cosine, sine = jnp.asarray(cos_table), jnp.asarray(sin_table)
    perm = jnp.asarray(head_permutation(), BF)
    lane_table = lane_frequencies()
    freqs = jnp.asarray(lane_table)
    times = jnp.asarray(np.repeat(lane_table[0, 0:8, None], 128, axis=1))

    sent, patch_fine = prepare(slab_kernel, history, section, patch_fine)
    received = lax.all_to_all(sent, "frame", 0, 0, tiled=True)
    fine = along_head(patch_fine)
    table = make_table(slab_kernel, freqs, sent)
    features = embed(slab_kernel, received, patch_mid, patch_coarse, (*fine[1:], table))
    mine = along_head(features)
    gathered = mine, tuple(other_core(block) for block in mine)
    far = make_far(gathered, modulation, w_qkv, perm, table)
    far2, far1, far3 = (along_x(far, d) for d in (2, 1, 3))
    fine_same = stack(fine, features)
    folded, gram = fold(fine_same, other_core(fine_same), modulation, w_qkv, perm, far)
    queries, keys, values = make_tokens(
        slab_kernel, gathered, folded, gram, cosine, sine, times
    )
    numerator, denominator = attend_near(queries, keys, values, far)
    fars = [far2, far3, far1]
    parts = attend_history(fars, queries, numerator, denominator)
    part2 = along_y(parts[2], 2)
    return combine([parts[0], along_y(parts[1], 1), part2, along_y(parts[3], 3)])


def solution(mesh):
    in_specs = (
        P("frame", None, None, None),
        P("frame", None),
        P(),
        P(None, ("head", "fsdp")),
        P(None, ("head", "fsdp")),
        P(None, ("head", "fsdp")),
        P(),
        P(None, None, ("head", "fsdp")),
    )
    out_specs = P("frame", ("head", "fsdp"))
    return jax.shard_map(
        per_device, mesh=mesh, in_specs=in_specs, out_specs=out_specs, check_vma=False
    )
```

```python
import functools

import jax
import jax.numpy as jnp
import numpy as np
from jax import lax
from jax.experimental import pallas as pl
from jax.experimental.pallas import tpu as pltpu
from jax.sharding import PartitionSpec as P

HEAD_DIM = 128
PARTS = (16, 56, 56)
THETA = 256.0
EPS = 1e-06
QUERY_SCALE = float(np.log2(np.e) * HEAD_DIM**-0.5)
EMBED = 52
BF = jnp.bfloat16
F32 = jnp.float32
VMEM = pl.BlockSpec(memory_space=pltpu.VMEM)
ANY = pl.BlockSpec(memory_space=pl.ANY)
SMEM = pl.BlockSpec(memory_space=pltpu.SMEM)


def params(mib=10):
    return pltpu.CompilerParams(vmem_limit_bytes=mib * 2**20)


def cost(flops, bytes_accessed, transcendentals=0):
    return pl.CostEstimate(
        flops=int(flops), bytes_accessed=int(bytes_accessed), transcendentals=int(transcendentals)
    )


def pair_tables():
    freqs = np.zeros((3, 64), np.float64)
    first, second = [], []
    pair, offset = 0, 0
    for axis, width in enumerate(PARTS):
        half = width // 2
        for i in range(half):
            freqs[axis, pair] = THETA ** (-2.0 * i / width)
            first.append(offset + i)
            second.append(offset + i + half)
            pair += 1
        offset += width
    return freqs, np.array(first + second)


def section_tables(frames, per_frame):
    freqs, _ = pair_tables()
    rows = np.arange(frames * per_frame)
    pos = np.stack(
        [4.0 * frames + rows // 512, 2.0 * (rows // 128 % 4) + 0.5, 2.0 * (rows % 128) + 0.5]
    )
    angles = freqs.T @ pos
    return np.cos(angles).astype(np.float32), np.sin(angles).astype(np.float32)


def head_permutation():
    _, order = pair_tables()
    perm = np.zeros((HEAD_DIM, HEAD_DIM), np.float32)
    perm[order, np.arange(HEAD_DIM)] = 1.0
    return perm


def lane_frequencies():
    freqs, _ = pair_tables()
    table = np.zeros((8, HEAD_DIM), np.float32)
    table[:3] = np.concatenate([freqs, freqs], axis=1)
    table[3] = np.concatenate([-np.ones(64), np.ones(64)])
    return table


def dot(a, b, dims=((1,), (0,))):
    return lax.dot_general(a, b, (dims, ((), ())), preferred_element_type=F32)


def select_columns(rows, columns, source):
    j = lax.broadcasted_iota(jnp.int32, (8, columns), 1)[0:1]
    i = lax.broadcasted_iota(jnp.int32, (rows, columns), 0)
    return jnp.where(i == source(j), 1.0, 0.0).astype(BF)


def select_rows(rows, columns, source):
    j = lax.broadcasted_iota(jnp.int32, (rows, columns), 1)
    i = lax.broadcasted_iota(jnp.int32, (rows, 128), 0)[:, 0:1]
    return jnp.where(j == source(i), 1.0, 0.0).astype(BF)


def split(value):
    high = value.astype(BF)
    return high, (value - high.astype(F32)).astype(BF)


def prepare_kernel(
    kinds_hbm,
    hist_hbm,
    sec_hbm,
    fine_hbm,
    out_ref,
    fine_ref,
    kinds_ref,
    hist_ref,
    sec_ref,
    kinds_sem,
    hist_sem,
    sec_sem,
    fine_sem,
):
    staged = [pltpu.make_async_copy(fine_hbm, fine_ref, fine_sem)]
    copies = [
        pltpu.make_async_copy(kinds_hbm, kinds_ref, kinds_sem),
        pltpu.make_async_copy(sec_hbm, sec_ref, sec_sem),
        pltpu.make_async_copy(hist_hbm, hist_ref, hist_sem),
    ]
    for copy in copies + staged:
        copy.start()
    kinds_copy, sec_copy, hist_copy = copies
    first = (lax.axis_index("head") * 2 + lax.axis_index("fsdp")) * 8
    own = select_rows(
        16, 64, lambda i: ((first + (i & 7)) & 31) * 2 + ((first + (i & 7)) >> 5)
    )
    mid_cols = select_rows(256, 256, lambda i: (i & 63) * 4 + (i >> 6))
    mid_lanes = select_columns(
        512,
        512,
        lambda j: ((j >> 8) * 2 + ((j >> 2) & 1)) * 128
        + ((j >> 3) & 15) * 8
        + ((j >> 7) & 1) * 4
        + (j & 3),
    )
    kinds_copy.wait()
    kind = kinds_ref[lax.axis_index("frame")]
    sec_copy.wait()
    section = dot(own, sec_ref[...]).astype(BF)
    for d in range(16):
        out_ref[d, 64:80, :] = section

    @pl.when(kind == 0)
    def _():
        z, core = lax.axis_index("head"), lax.axis_index("fsdp")
        cols = select_columns(256, 128, lambda j: (64 * core + (j & 63)) * 2 + (j >> 6))
        rows = select_rows(
            128, 512, lambda i: (i >> 5) * 128 + ((i >> 1) & 15) * 8 + z * 2 + (i & 1)
        )
        hist_copy.wait()
        out = dot(rows, dot(hist_ref[...], cols).astype(BF)).astype(BF)
        blank = jnp.zeros((32, 128), BF)
        for d in range(16):
            t = d // 4
            out_ref[d, 0:64, :] = jnp.concatenate([out[32 * t : 32 * t + 32], blank], axis=0)

    @pl.when(kind == 1)
    def _():
        hist_copy.wait()
        out = dot(dot(mid_cols, hist_ref[...], ((1,), (1,))).astype(BF), mid_lanes).astype(BF)
        for d in range(16):
            g, q = d // 4, d % 4
            for w in range(4):
                out_ref[d, 16 * w : 16 * w + 16, :] = out[
                    64 * w + 16 * q : 64 * w + 16 * q + 16, 128 * g : 128 * g + 128
                ]

    @pl.when(kind == 2)
    def _():
        lanes = select_columns(
            512, 512, lambda j: ((j >> 3) & 3) * 128 + (j >> 5) * 8 + (j & 7)
        )
        cols = select_rows(256, 256, lambda i: i)
        hist_copy.wait()
        out = dot(dot(cols, hist_ref[...], ((1,), (1,))).astype(BF), lanes).astype(BF)
        for d in range(16):
            for g in range(4):
                out_ref[d, 16 * g : 16 * g + 16, :] = out[
                    16 * d : 16 * d + 16, 128 * g : 128 * g + 128
                ]

    for copy in staged:
        copy.wait()


def prepare(kinds, history, section, patch_fine):
    return pl.pallas_call(
        prepare_kernel,
        out_shape=(
            jax.ShapeDtypeStruct((16, 80, 128), BF),
            jax.ShapeDtypeStruct(patch_fine.shape, BF),
        ),
        in_specs=[ANY] * 4,
        out_specs=(VMEM,) * 2,
        scratch_shapes=[
            pltpu.SMEM((16,), jnp.int32),
            pltpu.VMEM((512, 256), BF),
            pltpu.VMEM((64, 128), BF),
        ]
        + [pltpu.SemaphoreType.DMA] * 4,
        compiler_params=params(60),
        cost_estimate=cost(2e10, 1e6),
        name="prepare",
    )(kinds, history.reshape(512, 256), section.T, patch_fine)


def embed_kernel(
    kinds_ref,
    recv_ref,
    mid_ref,
    coarse_hbm,
    fine1,
    fine2,
    fine3,
    table_ref,
    out_ref,
    coarse_ref,
    mid_buf,
    coarse_buf,
    coarse_sems,
):
    del fine1, fine2, fine3, table_ref
    coarse_copies = []
    for g in range(4):
        part = pl.ds(1024 * g, 1024)
        coarse_copies.append(
            pltpu.make_async_copy(coarse_hbm.at[part], coarse_ref.at[part], coarse_sems.at[g])
        )
        coarse_copies[g].start()
    mid_count = jnp.int32(0)
    coarse_count = jnp.int32(0)
    fine_slab = jnp.int32(0)
    for s in range(16):
        kind = kinds_ref[s]
        block = recv_ref[s, 0:64, :]
        mid_buf[jnp.where(kind == 1, jnp.minimum(mid_count, 6), 7)] = block
        coarse_buf[jnp.where(kind == 2, jnp.minimum(coarse_count, 7), 8)] = block
        mid_count += jnp.where(kind == 1, 1, 0)
        coarse_count += jnp.where(kind == 2, 1, 0)
        fine_slab += jnp.where(kind == 0, s, 0)
    fine = recv_ref[fine_slab, 0:32, :]
    out_ref[128:144, 0:128] = fine[0:16]
    out_ref[128:144, 128:256] = fine[16:32]
    me = lax.axis_index("frame")
    x, y = me & 3, me >> 2
    frames = [((y + d) & 3) * 4 + x for d in range(4)] + [4 * y + i for i in range(4)]
    upper = lax.broadcasted_iota(jnp.int32, (16, 128), 0) < 8
    for i, (row, lane) in enumerate(((128, 256), (144, 0), (144, 128), (144, 256))):
        first, second = (
            recv_ref[f, 64:80, :].astype(F32) for f in (frames[2 * i], frames[2 * i + 1])
        )
        out_ref[row : row + 16, lane : lane + 128] = jnp.where(upper, first, second).astype(BF)
    tokens = jnp.concatenate(
        [mid_buf[0:7, 16 * w : 16 * w + 16, :].reshape(112, 128) for w in range(4)], axis=1
    )
    order = select_columns(512, 512, lambda j: (j & 3) * 128 + (j >> 2))
    tokens = dot(tokens, order).astype(BF)
    out_ref[0:112, :] = dot(tokens, mid_ref[...]).astype(BF)
    cells = coarse_buf[0:8].reshape(512, 128)
    order = select_rows(
        512,
        512,
        lambda i: ((i >> 1) & 7) * 64 + (i >> 7) * 16 + (i & 1) * 8 + ((i >> 4) & 7),
    )
    cells = dot(order, cells).astype(BF)
    tokens = jnp.concatenate(
        [
            jnp.concatenate(
                [cells[128 * g + 16 * w : 128 * g + 16 * w + 16] for w in range(8)], axis=1
            )
            for g in range(4)
        ],
        axis=0,
    )
    order = select_columns(1024, 1024, lambda j: (j & 7) * 128 + (j >> 3))
    tokens = dot(tokens, order).astype(BF)
    total = jnp.zeros((16, out_ref.shape[1]), F32)
    for g in range(4):
        coarse_copies[g].wait()
        total += dot(tokens[16 * g : 16 * g + 16], coarse_ref[1024 * g : 1024 * g + 1024, :])
    out_ref[112:128, :] = total.astype(BF)


def embed(kinds, received, patch_mid, patch_coarse, fine):
    return pl.pallas_call(
        embed_kernel,
        out_shape=jax.ShapeDtypeStruct((160, patch_mid.shape[1]), BF),
        in_specs=[SMEM, VMEM, VMEM] + [ANY] * 5,
        out_specs=VMEM,
        scratch_shapes=[
            pltpu.VMEM(patch_coarse.shape, BF),
            pltpu.VMEM((8, 64, 128), BF),
            pltpu.VMEM((9, 64, 128), BF),
            pltpu.SemaphoreType.DMA((4,)),
        ],
        compiler_params=params(EMBED),
        cost_estimate=cost(2e9, 5e6),
        name="embed",
    )(kinds, received, patch_mid, patch_coarse, *fine)


def along_head(block):
    ring1, ring3, ring2 = (
        lax.ppermute(block, "head", [(i, (i + d) % 4) for i in range(4)]) for d in (1, 3, 2)
    )
    return block, ring1, ring2, ring3


def other_core(block):
    return lax.ppermute(block, "fsdp", [(0, 1), (1, 0)])


def stack_kernel(ref0, ref1, ref2, ref3, after_ref, out_ref):
    del after_ref
    for d, ref in enumerate((ref0, ref1, ref2, ref3)):
        out_ref[d] = ref[...]


def stack(blocks, after):
    return pl.pallas_call(
        stack_kernel,
        out_shape=jax.ShapeDtypeStruct((4, *blocks[0].shape), BF),
        in_specs=[VMEM] * 4 + [ANY],
        out_specs=VMEM,
        compiler_params=params(),
        cost_estimate=cost(2e10, 1e6),
        name="stack",
    )(*blocks, after)


def place_columns(gathered, full_ref):
    z, core = lax.axis_index("head"), lax.axis_index("fsdp")
    rows = full_ref.shape[0]
    for d, (mine, theirs) in enumerate(zip(*gathered)):
        at = ((z + 4 - d) & 3) * 2
        width = mine.shape[1]
        for ref, column in ((mine, at + core), (theirs, at + 1 - core)):
            full_ref[:, pl.ds(pl.multiple_of(column * width, 128), width)] = ref[0:rows]


def fold_kernel(
    same_ref,
    other_ref,
    mod_ref,
    w_ref,
    perm_ref,
    after_ref,
    fold_ref,
    gram_ref,
    full_ref,
):
    del after_ref
    place_columns([[ref.at[d] for d in range(4)] for ref in (same_ref, other_ref)], full_ref)
    order = select_rows(64, 64, lambda i: (i & 31) * 2 + (i >> 5))
    raw = full_ref[...]
    width = raw.shape[1]
    weight = dot(order, raw)
    low = weight.astype(BF)
    mean = jnp.sum(weight, axis=1, keepdims=True) / width
    mean_row = dot(jnp.ones((8, width), BF), low, ((1,), (1,)))[0:1] / width
    gram_ref[...] = dot(low, low, ((1,), (1,))) / width - mean * mean_row
    scaled = (weight - mean) * (1.0 + mod_ref[1:2, :])
    shift_high, shift_low = split(mod_ref[0:1, :])
    pad = jnp.zeros((14, width), BF)
    high, rest = split(scaled)
    left = jnp.concatenate(
        [high, rest, jnp.concatenate([shift_high, shift_low, pad], axis=0)], axis=0
    )
    for part in range(3):
        product = dot(left, w_ref[part])
        matrix = product[0:64] + product[64:128]
        bias = product[128:129] + product[129:130]
        columns = matrix.shape[1]
        high, rest = split(matrix)
        bias_high, bias_low = split(bias)
        rows = jnp.concatenate(
            [
                high.astype(F32),
                rest.astype(F32),
                bias_high.astype(F32),
                bias_high.astype(F32),
                bias_low.astype(F32),
                jnp.zeros((13, columns), F32),
            ],
            axis=0,
        ).astype(BF)
        if part < 2:
            rows = jnp.concatenate(
                [
                    dot(rows[:, HEAD_DIM * h : HEAD_DIM * (h + 1)], perm_ref[...]).astype(BF)
                    for h in range(columns // HEAD_DIM)
                ],
                axis=1,
            )
        fold_ref[part] = rows


def fold(same, other, modulation, w_qkv, perm, after):
    width, columns = w_qkv.shape[1], w_qkv.shape[2]
    return pl.pallas_call(
        fold_kernel,
        out_shape=(
            jax.ShapeDtypeStruct((3, 144, columns), BF),
            jax.ShapeDtypeStruct((64, 64), F32),
        ),
        in_specs=[VMEM] * 5 + [ANY],
        out_specs=(VMEM, VMEM),
        scratch_shapes=[pltpu.VMEM((64, width), BF)],
        compiler_params=params(),
        cost_estimate=cost(1e6, 1e4),
        name="fold",
    )(same, other, modulation, w_qkv, perm, after)


def along_x(value, d):
    return lax.ppermute(value, "frame", [(i, i // 4 * 4 + (i + d) % 4) for i in range(16)])


def along_y(value, d):
    return lax.ppermute(value, "frame", [(i, (i + 4 * d) % 16) for i in range(16)])


def spread_of(patches, gram):
    one, rest = split(gram)
    two, three = split(gram - one.astype(F32))
    parts = jnp.concatenate([one, two, three], axis=1)
    spread = dot(parts, jnp.concatenate([patches, patches, patches], axis=0))
    variance = jnp.sum(spread * patches.astype(F32), axis=0, keepdims=True)
    return jnp.maximum(variance, 0.0) + EPS


def extended(patches, variance):
    high, low = split(jnp.sqrt(variance))
    rows = lax.broadcasted_iota(jnp.int32, (16, patches.shape[1]), 0)
    extra = jnp.where(
        rows == 1,
        low.astype(F32),
        jnp.where((rows == 0) | (rows == 2), high.astype(F32), 0.0),
    ).astype(BF)
    return jnp.concatenate([patches, patches, extra], axis=0)


def turned_columns(raw, variance, cosine, sine, scale):
    square = jnp.sum(raw * raw, axis=0, keepdims=True) / HEAD_DIM
    factor = lax.rsqrt(square + EPS * variance) * scale
    a, b = raw[0:64] * factor, raw[64:128] * factor
    return jnp.concatenate([a * cosine - b * sine, b * cosine + a * sine], axis=0).astype(BF)


def token_kernel(
    kinds_ref,
    mine0,
    mine1,
    mine2,
    mine3,
    theirs0,
    theirs1,
    theirs2,
    theirs3,
    fold_ref,
    gram_ref,
    cos_ref,
    sin_ref,
    time_ref,
    query_ref,
    key_ref,
    value_ref,
    fine_buf,
    sec_buf,
):
    me = lax.axis_index("frame")
    x, y = me & 3, me >> 2
    heads = query_ref.shape[0] // HEAD_DIM
    columns = [((y + d) & 3) * 4 + x for d in range(4)]

    def block(ref, f):
        return ref[:, pl.ds(pl.multiple_of(f * 128, 128), 128)]

    z, core = lax.axis_index("head"), lax.axis_index("fsdp")
    mine_refs, theirs_refs = (mine0, mine1, mine2, mine3), (theirs0, theirs1, theirs2, theirs3)
    for d, (mine_ref, theirs_ref) in enumerate(zip(mine_refs, theirs_refs)):
        at = (z + 4 - d) & 3
        for i, (row, lane) in enumerate(((128, 256), (144, 0), (144, 128), (144, 256))):
            mine, theirs = (
                ref[row : row + 16, lane : lane + 128].astype(F32) for ref in (mine_ref, theirs_ref)
            )
            first, second = jnp.where(core == 0, mine, theirs), jnp.where(core == 0, theirs, mine)
            for k, part in enumerate((slice(0, 8), slice(8, 16))):
                sec_buf[
                    pl.ds(pl.multiple_of(16 * at, 16), 16), 128 * (2 * i + k) : 128 * (2 * i + k + 1)
                ] = jnp.concatenate([first[part], second[part]], axis=0).astype(BF)
        mine, theirs = (
            jnp.concatenate([ref[128:144, 0:128], ref[128:144, 128:256]], axis=0).astype(F32)
            for ref in (mine_ref, theirs_ref)
        )
        first, second = jnp.where(core == 0, mine, theirs), jnp.where(core == 0, theirs, mine)
        fine_buf[:, pl.ds(pl.multiple_of(at * 128, 128), 128)] = jnp.concatenate(
            [
                jnp.concatenate([first[:, 0:64], second[:, 0:64]], axis=1),
                jnp.concatenate([first[:, 64:128], second[:, 64:128]], axis=1),
            ],
            axis=0,
        ).astype(BF)
    patches = jnp.concatenate([sec_buf[...], fine_buf[...]], axis=1)
    variance = spread_of(patches, gram_ref[...])
    inverse = lax.rsqrt(variance)
    patches = extended(patches, variance)
    cosine = jnp.concatenate([block(cos_ref, f) for f in columns], axis=1)
    sine = jnp.concatenate([block(sin_ref, f) for f in columns], axis=1)
    row = pl.ds(pl.multiple_of(y * 512, 128), 512)
    key_cos, key_sin = cos_ref[:, row], sin_ref[:, row]
    slab = jnp.int32(0)
    for s in range(16):
        slab += jnp.where(kinds_ref[s] == 0, s, 0)
    angles = time_ref[...] * (4 * slab + y).astype(F32)
    fine_cos = jnp.concatenate([jnp.concatenate([jnp.cos(angles)] * 4, axis=1), key_cos[8:]], axis=0)
    fine_sin = jnp.concatenate([jnp.concatenate([jnp.sin(angles)] * 4, axis=1), key_sin[8:]], axis=0)
    key_cos = jnp.concatenate([key_cos, fine_cos], axis=1)
    key_sin = jnp.concatenate([key_sin, fine_sin], axis=1)
    for h in range(heads):
        at = slice(HEAD_DIM * h, HEAD_DIM * (h + 1))
        raw = dot(fold_ref[0][:, at], patches[:, 0:512], ((0,), (0,)))
        query_ref[at, :] = turned_columns(raw, variance[:, 0:512], cosine, sine, QUERY_SCALE)
        raw = dot(fold_ref[1][:, at], patches[:, 512:], ((0,), (0,)))
        key_ref[at, :] = turned_columns(raw, variance[:, 512:], key_cos, key_sin, 1.0)
        raw = dot(fold_ref[2][:, at], patches[:, 512:], ((0,), (0,)))
        value_ref[at, :] = (raw * inverse[:, 512:]).astype(BF)


def make_tokens(kinds, gathered, folded, gram, cosine, sine, times):
    columns = folded.shape[2]
    return pl.pallas_call(
        token_kernel,
        out_shape=(
            jax.ShapeDtypeStruct((columns, 512), BF),
            jax.ShapeDtypeStruct((columns, 1024), BF),
            jax.ShapeDtypeStruct((columns, 1024), BF),
        ),
        in_specs=[SMEM] + [VMEM] * 13,
        out_specs=tuple([VMEM] * 3),
        scratch_shapes=[pltpu.VMEM((64, 512), BF), pltpu.VMEM((64, 1024), BF)],
        compiler_params=params(),
        cost_estimate=cost(2e9, 8e6),
        name="tokens",
    )(kinds, *gathered[0], *gathered[1], folded, gram, cosine, sine, times)


def near_kernel(query_ref, key_ref, value_ref, far_ref, num_ref, den_ref):
    heads = query_ref.shape[0] // HEAD_DIM
    for h in range(heads):
        at = slice(HEAD_DIM * h, HEAD_DIM * (h + 1))
        weights = jnp.exp2(dot(key_ref[at, :], query_ref[at, :], ((0,), (0,))))
        own_weights = jnp.exp2(dot(far_ref[0, :, at], query_ref[at, :]))
        den_ref[h : h + 1, :] = jnp.sum(weights, axis=0, keepdims=True) + jnp.sum(
            own_weights, axis=0, keepdims=True
        )
        num_ref[at, :] = dot(value_ref[at, :], weights.astype(BF)) + dot(
            far_ref[1, :, at], own_weights.astype(BF), ((0,), (0,))
        )


def attend_near(queries, keys, values, far):
    columns, count = queries.shape
    return pl.pallas_call(
        near_kernel,
        out_shape=(
            jax.ShapeDtypeStruct((columns, count), F32),
            jax.ShapeDtypeStruct((8, count), F32),
        ),
        in_specs=[VMEM] * 4,
        out_specs=(VMEM, VMEM),
        compiler_params=params(),
        cost_estimate=cost(4e9, 1e7, 2e6),
        name="near",
    )(queries, keys, values, far)


def row_angles(kinds_ref, freq_ref):
    me = lax.axis_index("frame")
    row = lax.broadcasted_iota(jnp.int32, (128, 128), 0)
    slot = row >> 4
    slab = jnp.zeros((128, 128), F32)
    mid_count = jnp.int32(0)
    coarse_count = jnp.int32(0)
    coarse_slot = jnp.where(slot == 7, (row >> 1) & 7, -1)
    for s in range(16):
        kind = kinds_ref[s]
        is_mid, is_coarse = kind == 1, kind == 2
        slab = jnp.where(slot == jnp.where(is_mid, mid_count, 99), float(s), slab)
        slab = jnp.where(coarse_slot == jnp.where(is_coarse, coarse_count, 99), float(s), slab)
        mid_count += jnp.where(is_mid, 1, 0)
        coarse_count += jnp.where(is_coarse, 1, 0)
    coarse = slot == 7
    whole = me.astype(F32)
    quarter = (me & 3).astype(F32)
    frame_half = (me >> 3).astype(F32)
    row_half = ((me >> 2) & 1).astype(F32)
    t = 4.0 * slab + jnp.where(coarse, 1.5, 2.0 * frame_half + 0.5)
    h = jnp.where(coarse, 3.5, 4.0 * row_half + 1.5)
    w = jnp.where(
        coarse,
        8.0 * (2.0 * whole + (row & 1).astype(F32)) + 3.5,
        4.0 * (16.0 * quarter + (row & 15).astype(F32)) + 1.5,
    )
    freq_t, freq_h, freq_w, sign = (freq_ref[i : i + 1, :] for i in range(4))
    angles = t * freq_t + h * freq_h + w * freq_w
    return jnp.cos(angles), jnp.sin(angles) * sign


def table_kernel(kinds_ref, freq_ref, after_ref, table_ref):
    del after_ref
    table_ref[0], table_ref[1] = row_angles(kinds_ref, freq_ref)


def make_table(kinds, freqs, after):
    return pl.pallas_call(
        table_kernel,
        out_shape=jax.ShapeDtypeStruct((2, 128, HEAD_DIM), F32),
        in_specs=[SMEM, VMEM, ANY],
        out_specs=VMEM,
        compiler_params=params(),
        cost_estimate=cost(1e5, 1e3),
        name="table",
    )(kinds, freqs, after)


def far_kernel(
    mine0,
    mine1,
    mine2,
    mine3,
    theirs0,
    theirs1,
    theirs2,
    theirs3,
    mod_ref,
    w_ref,
    perm_ref,
    table_ref,
    out_ref,
    full_ref,
):
    place_columns(((mine0, mine1, mine2, mine3), (theirs0, theirs1, theirs2, theirs3)), full_ref)
    heads = out_ref.shape[2] // HEAD_DIM
    x = full_ref[...].astype(F32)
    x = x - jnp.mean(x, axis=1, keepdims=True)
    x = x * lax.rsqrt(jnp.mean(x * x, axis=1, keepdims=True) + EPS)
    x = (x * (1.0 + mod_ref[1:2, :]) + mod_ref[0:1, :]).astype(BF)
    raw_keys = dot(x, w_ref[1])
    out_ref[1] = dot(x, w_ref[2]).astype(BF)
    cosine, sine = table_ref[0], table_ref[1]
    for h in range(heads):
        at = slice(HEAD_DIM * h, HEAD_DIM * (h + 1))
        raw = raw_keys[:, at]
        raw = raw * lax.rsqrt(jnp.mean(raw * raw, axis=1, keepdims=True) + EPS)
        high, rest = split(raw)
        raw = dot(high, perm_ref[...]) + dot(rest, perm_ref[...])
        out_ref[0, :, at] = (raw * cosine + pltpu.roll(raw, 64, 1) * sine).astype(BF)


def make_far(gathered, modulation, w_qkv, perm, table):
    columns = w_qkv.shape[2]
    return pl.pallas_call(
        far_kernel,
        out_shape=jax.ShapeDtypeStruct((2, 128, columns), BF),
        in_specs=[VMEM] * 12,
        out_specs=VMEM,
        scratch_shapes=[pltpu.VMEM((128, w_qkv.shape[1]), BF)],
        compiler_params=params(),
        cost_estimate=cost(2e9, 1e7),
        name="far",
    )(*gathered[0], *gathered[1], modulation, w_qkv, perm, table)


def middle_kernel(far_ref, query_ref, num_ref, den_ref, out_ref, sum_ref):
    heads = query_ref.shape[0] // HEAD_DIM
    for h in range(heads):
        at = slice(HEAD_DIM * h, HEAD_DIM * (h + 1))
        weights = jnp.exp2(dot(far_ref[0, :, at], query_ref[at, :]))
        sum_ref[h : h + 1, :] = den_ref[h : h + 1, :] + jnp.sum(weights, axis=0, keepdims=True)
        out_ref[at, :] = num_ref[at, :] + dot(
            far_ref[1, :, at], weights.astype(BF), ((0,), (0,))
        )


def attend_first(far, queries, numerator, denominator):
    return pl.pallas_call(
        middle_kernel,
        out_shape=(
            jax.ShapeDtypeStruct(numerator.shape, F32),
            jax.ShapeDtypeStruct(denominator.shape, F32),
        ),
        in_specs=[VMEM] * 4,
        out_specs=(VMEM, VMEM),
        compiler_params=params(),
        cost_estimate=cost(2e9, 1e6, 1e6),
        name="first",
    )(far, queries, numerator, denominator)


def history_kernel(far1, far3, query_ref, num_ref, den_ref, out0, out1, out2, out3):
    heads = query_ref.shape[0] // HEAD_DIM
    count = query_ref.shape[1]
    outs = (out0, out1, out2, out3)
    rows = lax.broadcasted_iota(jnp.int32, (16, count), 0)
    tail = jnp.zeros((16, count), F32)
    for h in range(heads):
        at = slice(HEAD_DIM * h, HEAD_DIM * (h + 1))
        fars = (far1, far3)
        keys = jnp.concatenate([far[0, :, at] for far in fars], axis=0)
        values = jnp.concatenate([far[1, :, at] for far in fars], axis=0)
        weights = jnp.exp2(dot(keys, query_ref[at, :]))
        high, rest = split(den_ref[h : h + 1, :] + jnp.sum(weights, axis=0, keepdims=True))
        tail = jnp.where(rows == h, high.astype(F32), tail)
        tail = jnp.where(rows == heads + h, rest.astype(F32), tail)
        part = num_ref[at, :] + dot(values, weights.astype(BF), ((0,), (0,)))
        for d, out in enumerate(outs):
            out[at, :] = part[:, 128 * d : 128 * d + 128].astype(out.dtype)
    for d, out in enumerate(outs):
        out[HEAD_DIM * heads :, :] = tail[:, 128 * d : 128 * d + 128].astype(out.dtype)


def attend_history(fars, queries, numerator, denominator):
    columns = queries.shape[0]
    return pl.pallas_call(
        history_kernel,
        out_shape=tuple(jax.ShapeDtypeStruct((columns + 16, 128), t) for t in (F32, BF, BF, BF)),
        in_specs=[VMEM] * 5,
        out_specs=tuple([VMEM] * 4),
        compiler_params=params(),
        cost_estimate=cost(2e9, 4e6, 1e6),
        name="history",
    )(*fars, queries, numerator, denominator)


def combine_kernel(part0, part1, part2, part3, out_ref):
    columns = out_ref.shape[1]
    heads = columns // HEAD_DIM
    total = sum(part[...].astype(F32) for part in (part0, part1, part2, part3))
    for h in range(heads):
        at = slice(HEAD_DIM * h, HEAD_DIM * (h + 1))
        low = columns + heads + h
        denominator = total[columns + h : columns + h + 1] + total[low : low + 1]
        out_ref[:, at] = jnp.transpose(total[at] / denominator).astype(BF)


def combine(parts):
    return pl.pallas_call(
        combine_kernel,
        out_shape=jax.ShapeDtypeStruct((128, parts[0].shape[0] - 16), BF),
        in_specs=[VMEM] * 4,
        out_specs=VMEM,
        compiler_params=params(),
        cost_estimate=cost(1e7, 2e6),
        name="combine",
    )(*parts)


def per_device(
    history, section, slab_kernel, patch_fine, patch_mid, patch_coarse, modulation, w_qkv
):
    frames = lax.axis_size("frame")
    cos_table, sin_table = section_tables(frames, section.shape[0])
    cosine, sine = jnp.asarray(cos_table), jnp.asarray(sin_table)
    perm = jnp.asarray(head_permutation(), BF)
    lane_table = lane_frequencies()
    freqs = jnp.asarray(lane_table)
    times = jnp.asarray(np.repeat(lane_table[0, 0:8, None], 128, axis=1))

    sent, patch_fine = prepare(slab_kernel, history, section, patch_fine)
    received = lax.all_to_all(sent, "frame", 0, 0, tiled=True)
    fine = along_head(patch_fine)
    table = make_table(slab_kernel, freqs, sent)
    features = embed(slab_kernel, received, patch_mid, patch_coarse, (*fine[1:], table))
    mine = along_head(features)
    gathered = mine, tuple(other_core(block) for block in mine)
    far = make_far(gathered, modulation, w_qkv, perm, table)
    far2, far1, far3 = (along_x(far, d) for d in (2, 1, 3))
    fine_same = stack(fine, features)
    folded, gram = fold(fine_same, other_core(fine_same), modulation, w_qkv, perm, far)
    queries, keys, values = make_tokens(
        slab_kernel, gathered, folded, gram, cosine, sine, times
    )
    numerator, denominator = attend_near(queries, keys, values, far)
    numerator, denominator = attend_first(far2, queries, numerator, denominator)
    fars = [far3, far1]
    parts = attend_history(fars, queries, numerator, denominator)
    part2 = along_y(parts[2], 2)
    return combine([parts[0], along_y(parts[1], 1), part2, along_y(parts[3], 3)])


def solution(mesh):
    in_specs = (
        P("frame", None, None, None),
        P("frame", None),
        P(),
        P(None, ("head", "fsdp")),
        P(None, ("head", "fsdp")),
        P(None, ("head", "fsdp")),
        P(),
        P(None, None, ("head", "fsdp")),
    )
    out_specs = P("frame", ("head", "fsdp"))
    return jax.shard_map(
        per_device, mesh=mesh, in_specs=in_specs, out_specs=out_specs, check_vma=False
    )
```

```python
import functools

import jax
import jax.numpy as jnp
import numpy as np
from jax import lax
from jax.experimental import pallas as pl
from jax.experimental.pallas import tpu as pltpu
from jax.sharding import PartitionSpec as P

HEAD_DIM = 128
PARTS = (16, 56, 56)
THETA = 256.0
EPS = 1e-06
QUERY_SCALE = float(np.log2(np.e) * HEAD_DIM**-0.5)
EMBED = 52
BF = jnp.bfloat16
F32 = jnp.float32
VMEM = pl.BlockSpec(memory_space=pltpu.VMEM)
ANY = pl.BlockSpec(memory_space=pl.ANY)
SMEM = pl.BlockSpec(memory_space=pltpu.SMEM)


def params(mib=10):
    return pltpu.CompilerParams(vmem_limit_bytes=mib * 2**20)


def cost(flops, bytes_accessed, transcendentals=0):
    return pl.CostEstimate(
        flops=int(flops), bytes_accessed=int(bytes_accessed), transcendentals=int(transcendentals)
    )


def pair_tables():
    freqs = np.zeros((3, 64), np.float64)
    first, second = [], []
    pair, offset = 0, 0
    for axis, width in enumerate(PARTS):
        half = width // 2
        for i in range(half):
            freqs[axis, pair] = THETA ** (-2.0 * i / width)
            first.append(offset + i)
            second.append(offset + i + half)
            pair += 1
        offset += width
    return freqs, np.array(first + second)


def section_tables(frames, per_frame):
    freqs, _ = pair_tables()
    rows = np.arange(frames * per_frame)
    pos = np.stack(
        [4.0 * frames + rows // 512, 2.0 * (rows // 128 % 4) + 0.5, 2.0 * (rows % 128) + 0.5]
    )
    angles = freqs.T @ pos
    return np.cos(angles).astype(np.float32), np.sin(angles).astype(np.float32)


def head_permutation():
    _, order = pair_tables()
    perm = np.zeros((HEAD_DIM, HEAD_DIM), np.float32)
    perm[order, np.arange(HEAD_DIM)] = 1.0
    return perm


def lane_frequencies():
    freqs, _ = pair_tables()
    table = np.zeros((8, HEAD_DIM), np.float32)
    table[:3] = np.concatenate([freqs, freqs], axis=1)
    table[3] = np.concatenate([-np.ones(64), np.ones(64)])
    return table


def dot(a, b, dims=((1,), (0,))):
    return lax.dot_general(a, b, (dims, ((), ())), preferred_element_type=F32)


def select_columns(rows, columns, source):
    j = lax.broadcasted_iota(jnp.int32, (8, columns), 1)[0:1]
    i = lax.broadcasted_iota(jnp.int32, (rows, columns), 0)
    return jnp.where(i == source(j), 1.0, 0.0).astype(BF)


def select_rows(rows, columns, source):
    j = lax.broadcasted_iota(jnp.int32, (rows, columns), 1)
    i = lax.broadcasted_iota(jnp.int32, (rows, 128), 0)[:, 0:1]
    return jnp.where(j == source(i), 1.0, 0.0).astype(BF)


def split(value):
    high = value.astype(BF)
    return high, (value - high.astype(F32)).astype(BF)


def prepare_kernel(
    kinds_hbm,
    hist_hbm,
    sec_hbm,
    fine_hbm,
    out_ref,
    fine_ref,
    kinds_ref,
    hist_ref,
    sec_ref,
    kinds_sem,
    hist_sem,
    sec_sem,
    fine_sem,
):
    staged = [pltpu.make_async_copy(fine_hbm, fine_ref, fine_sem)]
    copies = [
        pltpu.make_async_copy(kinds_hbm, kinds_ref, kinds_sem),
        pltpu.make_async_copy(sec_hbm, sec_ref, sec_sem),
        pltpu.make_async_copy(hist_hbm, hist_ref, hist_sem),
    ]
    for copy in copies + staged:
        copy.start()
    kinds_copy, sec_copy, hist_copy = copies
    first = (lax.axis_index("head") * 2 + lax.axis_index("fsdp")) * 8
    own = select_rows(
        16, 64, lambda i: ((first + (i & 7)) & 31) * 2 + ((first + (i & 7)) >> 5)
    )
    mid_cols = select_rows(256, 256, lambda i: (i & 63) * 4 + (i >> 6))
    mid_lanes = select_columns(
        512,
        512,
        lambda j: ((j >> 8) * 2 + ((j >> 2) & 1)) * 128
        + ((j >> 3) & 15) * 8
        + ((j >> 7) & 1) * 4
        + (j & 3),
    )
    kinds_copy.wait()
    kind = kinds_ref[lax.axis_index("frame")]
    sec_copy.wait()
    section = dot(own, sec_ref[...]).astype(BF)
    for d in range(16):
        out_ref[d, 64:80, :] = section

    @pl.when(kind == 0)
    def _():
        z, core = lax.axis_index("head"), lax.axis_index("fsdp")
        cols = select_columns(256, 128, lambda j: (64 * core + (j & 63)) * 2 + (j >> 6))
        rows = select_rows(
            128, 512, lambda i: (i >> 5) * 128 + ((i >> 1) & 15) * 8 + z * 2 + (i & 1)
        )
        hist_copy.wait()
        out = dot(rows, dot(hist_ref[...], cols).astype(BF)).astype(BF)
        blank = jnp.zeros((32, 128), BF)
        for d in range(16):
            t = d // 4
            out_ref[d, 0:64, :] = jnp.concatenate([out[32 * t : 32 * t + 32], blank], axis=0)

    @pl.when(kind == 1)
    def _():
        hist_copy.wait()
        out = dot(dot(mid_cols, hist_ref[...], ((1,), (1,))).astype(BF), mid_lanes).astype(BF)
        for d in range(16):
            g, q = d // 4, d % 4
            for w in range(4):
                out_ref[d, 16 * w : 16 * w + 16, :] = out[
                    64 * w + 16 * q : 64 * w + 16 * q + 16, 128 * g : 128 * g + 128
                ]

    @pl.when(kind == 2)
    def _():
        lanes = select_columns(
            512, 512, lambda j: ((j >> 3) & 3) * 128 + (j >> 5) * 8 + (j & 7)
        )
        cols = select_rows(256, 256, lambda i: i)
        hist_copy.wait()
        out = dot(dot(cols, hist_ref[...], ((1,), (1,))).astype(BF), lanes).astype(BF)
        for d in range(16):
            for g in range(4):
                out_ref[d, 16 * g : 16 * g + 16, :] = out[
                    16 * d : 16 * d + 16, 128 * g : 128 * g + 128
                ]

    for copy in staged:
        copy.wait()


def prepare(kinds, history, section, patch_fine):
    return pl.pallas_call(
        prepare_kernel,
        out_shape=(
            jax.ShapeDtypeStruct((16, 80, 128), BF),
            jax.ShapeDtypeStruct(patch_fine.shape, BF),
        ),
        in_specs=[ANY] * 4,
        out_specs=(VMEM,) * 2,
        scratch_shapes=[
            pltpu.SMEM((16,), jnp.int32),
            pltpu.VMEM((512, 256), BF),
            pltpu.VMEM((64, 128), BF),
        ]
        + [pltpu.SemaphoreType.DMA] * 4,
        compiler_params=params(60),
        cost_estimate=cost(2e10, 1e6),
        name="prepare",
    )(kinds, history.reshape(512, 256), section.T, patch_fine)


def embed_kernel(
    kinds_ref,
    recv_ref,
    mid_ref,
    coarse_hbm,
    fine1,
    fine2,
    fine3,
    table_ref,
    out_ref,
    coarse_ref,
    mid_buf,
    coarse_buf,
    coarse_sems,
):
    del fine1, fine2, fine3, table_ref
    coarse_copies = []
    for g in range(4):
        part = pl.ds(1024 * g, 1024)
        coarse_copies.append(
            pltpu.make_async_copy(coarse_hbm.at[part], coarse_ref.at[part], coarse_sems.at[g])
        )
        coarse_copies[g].start()
    mid_count = jnp.int32(0)
    coarse_count = jnp.int32(0)
    fine_slab = jnp.int32(0)
    for s in range(16):
        kind = kinds_ref[s]
        block = recv_ref[s, 0:64, :]
        mid_buf[jnp.where(kind == 1, jnp.minimum(mid_count, 6), 7)] = block
        coarse_buf[jnp.where(kind == 2, jnp.minimum(coarse_count, 7), 8)] = block
        mid_count += jnp.where(kind == 1, 1, 0)
        coarse_count += jnp.where(kind == 2, 1, 0)
        fine_slab += jnp.where(kind == 0, s, 0)
    fine = recv_ref[fine_slab, 0:32, :]
    out_ref[128:144, 0:128] = fine[0:16]
    out_ref[128:144, 128:256] = fine[16:32]
    me = lax.axis_index("frame")
    x, y = me & 3, me >> 2
    frames = [((y + d) & 3) * 4 + x for d in range(4)] + [4 * y + i for i in range(4)]
    upper = lax.broadcasted_iota(jnp.int32, (16, 128), 0) < 8
    for i, (row, lane) in enumerate(((128, 256), (144, 0), (144, 128), (144, 256))):
        first, second = (
            recv_ref[f, 64:80, :].astype(F32) for f in (frames[2 * i], frames[2 * i + 1])
        )
        out_ref[row : row + 16, lane : lane + 128] = jnp.where(upper, first, second).astype(BF)
    tokens = jnp.concatenate(
        [mid_buf[0:7, 16 * w : 16 * w + 16, :].reshape(112, 128) for w in range(4)], axis=1
    )
    order = select_columns(512, 512, lambda j: (j & 3) * 128 + (j >> 2))
    tokens = dot(tokens, order).astype(BF)
    out_ref[0:112, :] = dot(tokens, mid_ref[...]).astype(BF)
    cells = coarse_buf[0:8].reshape(512, 128)
    order = select_rows(
        512,
        512,
        lambda i: ((i >> 1) & 7) * 64 + (i >> 7) * 16 + (i & 1) * 8 + ((i >> 4) & 7),
    )
    cells = dot(order, cells).astype(BF)
    tokens = jnp.concatenate(
        [
            jnp.concatenate(
                [cells[128 * g + 16 * w : 128 * g + 16 * w + 16] for w in range(8)], axis=1
            )
            for g in range(4)
        ],
        axis=0,
    )
    order = select_columns(1024, 1024, lambda j: (j & 7) * 128 + (j >> 3))
    tokens = dot(tokens, order).astype(BF)
    total = jnp.zeros((16, out_ref.shape[1]), F32)
    for g in range(4):
        coarse_copies[g].wait()
        total += dot(tokens[16 * g : 16 * g + 16], coarse_ref[1024 * g : 1024 * g + 1024, :])
    out_ref[112:128, :] = total.astype(BF)


def embed(kinds, received, patch_mid, patch_coarse, fine):
    return pl.pallas_call(
        embed_kernel,
        out_shape=jax.ShapeDtypeStruct((160, patch_mid.shape[1]), BF),
        in_specs=[SMEM, VMEM, VMEM] + [ANY] * 5,
        out_specs=VMEM,
        scratch_shapes=[
            pltpu.VMEM(patch_coarse.shape, BF),
            pltpu.VMEM((8, 64, 128), BF),
            pltpu.VMEM((9, 64, 128), BF),
            pltpu.SemaphoreType.DMA((4,)),
        ],
        compiler_params=params(EMBED),
        cost_estimate=cost(2e9, 5e6),
        name="embed",
    )(kinds, received, patch_mid, patch_coarse, *fine)


def along_head(block):
    ring1, ring3, ring2 = (
        lax.ppermute(block, "head", [(i, (i + d) % 4) for i in range(4)]) for d in (1, 3, 2)
    )
    return block, ring1, ring2, ring3


def other_core(block):
    return lax.ppermute(block, "fsdp", [(0, 1), (1, 0)])


def stack_kernel(ref0, ref1, ref2, ref3, after_ref, out_ref):
    del after_ref
    for d, ref in enumerate((ref0, ref1, ref2, ref3)):
        out_ref[d] = ref[...]


def stack(blocks, after):
    return pl.pallas_call(
        stack_kernel,
        out_shape=jax.ShapeDtypeStruct((4, *blocks[0].shape), BF),
        in_specs=[VMEM] * 4 + [ANY],
        out_specs=VMEM,
        compiler_params=params(),
        cost_estimate=cost(2e10, 1e6),
        name="stack",
    )(*blocks, after)


def place_columns(gathered, full_ref):
    z, core = lax.axis_index("head"), lax.axis_index("fsdp")
    rows = full_ref.shape[0]
    for d, (mine, theirs) in enumerate(zip(*gathered)):
        at = ((z + 4 - d) & 3) * 2
        width = mine.shape[1]
        for ref, column in ((mine, at + core), (theirs, at + 1 - core)):
            full_ref[:, pl.ds(pl.multiple_of(column * width, 128), width)] = ref[0:rows]


def fold_kernel(
    same_ref,
    other_ref,
    mod_ref,
    w_ref,
    perm_ref,
    after_ref,
    fold_ref,
    gram_ref,
    full_ref,
):
    del after_ref
    place_columns([[ref.at[d] for d in range(4)] for ref in (same_ref, other_ref)], full_ref)
    order = select_rows(64, 64, lambda i: (i & 31) * 2 + (i >> 5))
    raw = full_ref[...]
    width = raw.shape[1]
    weight = dot(order, raw)
    low = weight.astype(BF)
    mean = jnp.sum(weight, axis=1, keepdims=True) / width
    mean_row = dot(jnp.ones((8, width), BF), low, ((1,), (1,)))[0:1] / width
    gram_ref[...] = dot(low, low, ((1,), (1,))) / width - mean * mean_row
    scaled = (weight - mean) * (1.0 + mod_ref[1:2, :])
    shift_high, shift_low = split(mod_ref[0:1, :])
    pad = jnp.zeros((14, width), BF)
    high, rest = split(scaled)
    left = jnp.concatenate(
        [high, rest, jnp.concatenate([shift_high, shift_low, pad], axis=0)], axis=0
    )
    for part in range(3):
        product = dot(left, w_ref[part])
        matrix = product[0:64] + product[64:128]
        bias = product[128:129] + product[129:130]
        columns = matrix.shape[1]
        high, rest = split(matrix)
        bias_high, bias_low = split(bias)
        rows = jnp.concatenate(
            [
                high.astype(F32),
                rest.astype(F32),
                bias_high.astype(F32),
                bias_high.astype(F32),
                bias_low.astype(F32),
                jnp.zeros((13, columns), F32),
            ],
            axis=0,
        ).astype(BF)
        if part < 2:
            rows = jnp.concatenate(
                [
                    dot(rows[:, HEAD_DIM * h : HEAD_DIM * (h + 1)], perm_ref[...]).astype(BF)
                    for h in range(columns // HEAD_DIM)
                ],
                axis=1,
            )
        fold_ref[part] = rows


def fold(same, other, modulation, w_qkv, perm, after):
    width, columns = w_qkv.shape[1], w_qkv.shape[2]
    return pl.pallas_call(
        fold_kernel,
        out_shape=(
            jax.ShapeDtypeStruct((3, 144, columns), BF),
            jax.ShapeDtypeStruct((64, 64), F32),
        ),
        in_specs=[VMEM] * 5 + [ANY],
        out_specs=(VMEM, VMEM),
        scratch_shapes=[pltpu.VMEM((64, width), BF)],
        compiler_params=params(),
        cost_estimate=cost(1e6, 1e4),
        name="fold",
    )(same, other, modulation, w_qkv, perm, after)


def along_x(value, d):
    return lax.ppermute(value, "frame", [(i, i // 4 * 4 + (i + d) % 4) for i in range(16)])


def along_y(value, d):
    return lax.ppermute(value, "frame", [(i, (i + 4 * d) % 16) for i in range(16)])


def spread_of(patches, gram):
    one, rest = split(gram)
    two, three = split(gram - one.astype(F32))
    parts = jnp.concatenate([one, two, three], axis=1)
    spread = dot(parts, jnp.concatenate([patches, patches, patches], axis=0))
    variance = jnp.sum(spread * patches.astype(F32), axis=0, keepdims=True)
    return jnp.maximum(variance, 0.0) + EPS


def extended(patches, variance):
    high, low = split(jnp.sqrt(variance))
    rows = lax.broadcasted_iota(jnp.int32, (16, patches.shape[1]), 0)
    extra = jnp.where(
        rows == 1,
        low.astype(F32),
        jnp.where((rows == 0) | (rows == 2), high.astype(F32), 0.0),
    ).astype(BF)
    return jnp.concatenate([patches, patches, extra], axis=0)


def turned_columns(raw, variance, cosine, sine, scale):
    square = jnp.sum(raw * raw, axis=0, keepdims=True) / HEAD_DIM
    factor = lax.rsqrt(square + EPS * variance) * scale
    a, b = raw[0:64] * factor, raw[64:128] * factor
    return jnp.concatenate([a * cosine - b * sine, b * cosine + a * sine], axis=0).astype(BF)


def token_kernel(
    kinds_ref,
    mine0,
    mine1,
    mine2,
    mine3,
    theirs0,
    theirs1,
    theirs2,
    theirs3,
    fold_ref,
    gram_ref,
    cos_ref,
    sin_ref,
    time_ref,
    query_ref,
    key_ref,
    value_ref,
    fine_buf,
    sec_buf,
):
    me = lax.axis_index("frame")
    x, y = me & 3, me >> 2
    heads = query_ref.shape[0] // HEAD_DIM
    columns = [((y + d) & 3) * 4 + x for d in range(4)]

    def block(ref, f):
        return ref[:, pl.ds(pl.multiple_of(f * 128, 128), 128)]

    z, core = lax.axis_index("head"), lax.axis_index("fsdp")
    mine_refs, theirs_refs = (mine0, mine1, mine2, mine3), (theirs0, theirs1, theirs2, theirs3)
    for d, (mine_ref, theirs_ref) in enumerate(zip(mine_refs, theirs_refs)):
        at = (z + 4 - d) & 3
        for i, (row, lane) in enumerate(((128, 256), (144, 0), (144, 128), (144, 256))):
            mine, theirs = (
                ref[row : row + 16, lane : lane + 128].astype(F32) for ref in (mine_ref, theirs_ref)
            )
            first, second = jnp.where(core == 0, mine, theirs), jnp.where(core == 0, theirs, mine)
            for k, part in enumerate((slice(0, 8), slice(8, 16))):
                sec_buf[
                    pl.ds(pl.multiple_of(16 * at, 16), 16), 128 * (2 * i + k) : 128 * (2 * i + k + 1)
                ] = jnp.concatenate([first[part], second[part]], axis=0).astype(BF)
        mine, theirs = (
            jnp.concatenate([ref[128:144, 0:128], ref[128:144, 128:256]], axis=0).astype(F32)
            for ref in (mine_ref, theirs_ref)
        )
        first, second = jnp.where(core == 0, mine, theirs), jnp.where(core == 0, theirs, mine)
        fine_buf[:, pl.ds(pl.multiple_of(at * 128, 128), 128)] = jnp.concatenate(
            [
                jnp.concatenate([first[:, 0:64], second[:, 0:64]], axis=1),
                jnp.concatenate([first[:, 64:128], second[:, 64:128]], axis=1),
            ],
            axis=0,
        ).astype(BF)
    patches = jnp.concatenate([sec_buf[...], fine_buf[...]], axis=1)
    variance = spread_of(patches, gram_ref[...])
    inverse = lax.rsqrt(variance)
    patches = extended(patches, variance)
    cosine = jnp.concatenate([block(cos_ref, f) for f in columns], axis=1)
    sine = jnp.concatenate([block(sin_ref, f) for f in columns], axis=1)
    row = pl.ds(pl.multiple_of(y * 512, 128), 512)
    key_cos, key_sin = cos_ref[:, row], sin_ref[:, row]
    slab = jnp.int32(0)
    for s in range(16):
        slab += jnp.where(kinds_ref[s] == 0, s, 0)
    angles = time_ref[...] * (4 * slab + y).astype(F32)
    fine_cos = jnp.concatenate([jnp.concatenate([jnp.cos(angles)] * 4, axis=1), key_cos[8:]], axis=0)
    fine_sin = jnp.concatenate([jnp.concatenate([jnp.sin(angles)] * 4, axis=1), key_sin[8:]], axis=0)
    key_cos = jnp.concatenate([key_cos, fine_cos], axis=1)
    key_sin = jnp.concatenate([key_sin, fine_sin], axis=1)
    for h in range(heads):
        at = slice(HEAD_DIM * h, HEAD_DIM * (h + 1))
        raw = dot(fold_ref[0][:, at], patches[:, 0:512], ((0,), (0,)))
        query_ref[at, :] = turned_columns(raw, variance[:, 0:512], cosine, sine, QUERY_SCALE)
        raw = dot(fold_ref[1][:, at], patches[:, 512:], ((0,), (0,)))
        key_ref[at, :] = turned_columns(raw, variance[:, 512:], key_cos, key_sin, 1.0)
        raw = dot(fold_ref[2][:, at], patches[:, 512:], ((0,), (0,)))
        value_ref[at, :] = (raw * inverse[:, 512:]).astype(BF)


def make_tokens(kinds, gathered, folded, gram, cosine, sine, times):
    columns = folded.shape[2]
    return pl.pallas_call(
        token_kernel,
        out_shape=(
            jax.ShapeDtypeStruct((columns, 512), BF),
            jax.ShapeDtypeStruct((columns, 1024), BF),
            jax.ShapeDtypeStruct((columns, 1024), BF),
        ),
        in_specs=[SMEM] + [VMEM] * 13,
        out_specs=tuple([VMEM] * 3),
        scratch_shapes=[pltpu.VMEM((64, 512), BF), pltpu.VMEM((64, 1024), BF)],
        compiler_params=params(),
        cost_estimate=cost(2e9, 8e6),
        name="tokens",
    )(kinds, *gathered[0], *gathered[1], folded, gram, cosine, sine, times)


def near_kernel(query_ref, key_ref, value_ref, far_ref, num_ref, den_ref):
    heads = query_ref.shape[0] // HEAD_DIM
    for h in range(heads):
        at = slice(HEAD_DIM * h, HEAD_DIM * (h + 1))
        weights = jnp.exp2(dot(key_ref[at, :], query_ref[at, :], ((0,), (0,))))
        own_weights = jnp.exp2(dot(far_ref[0, :, at], query_ref[at, :]))
        den_ref[h : h + 1, :] = jnp.sum(weights, axis=0, keepdims=True) + jnp.sum(
            own_weights, axis=0, keepdims=True
        )
        num_ref[at, :] = dot(value_ref[at, :], weights.astype(BF)) + dot(
            far_ref[1, :, at], own_weights.astype(BF), ((0,), (0,))
        )


def attend_near(queries, keys, values, far):
    columns, count = queries.shape
    return pl.pallas_call(
        near_kernel,
        out_shape=(
            jax.ShapeDtypeStruct((columns, count), F32),
            jax.ShapeDtypeStruct((8, count), F32),
        ),
        in_specs=[VMEM] * 4,
        out_specs=(VMEM, VMEM),
        compiler_params=params(),
        cost_estimate=cost(4e9, 1e7, 2e6),
        name="near",
    )(queries, keys, values, far)


def row_angles(kinds_ref, freq_ref):
    me = lax.axis_index("frame")
    row = lax.broadcasted_iota(jnp.int32, (128, 128), 0)
    slot = row >> 4
    slab = jnp.zeros((128, 128), F32)
    mid_count = jnp.int32(0)
    coarse_count = jnp.int32(0)
    coarse_slot = jnp.where(slot == 7, (row >> 1) & 7, -1)
    for s in range(16):
        kind = kinds_ref[s]
        is_mid, is_coarse = kind == 1, kind == 2
        slab = jnp.where(slot == jnp.where(is_mid, mid_count, 99), float(s), slab)
        slab = jnp.where(coarse_slot == jnp.where(is_coarse, coarse_count, 99), float(s), slab)
        mid_count += jnp.where(is_mid, 1, 0)
        coarse_count += jnp.where(is_coarse, 1, 0)
    coarse = slot == 7
    whole = me.astype(F32)
    quarter = (me & 3).astype(F32)
    frame_half = (me >> 3).astype(F32)
    row_half = ((me >> 2) & 1).astype(F32)
    t = 4.0 * slab + jnp.where(coarse, 1.5, 2.0 * frame_half + 0.5)
    h = jnp.where(coarse, 3.5, 4.0 * row_half + 1.5)
    w = jnp.where(
        coarse,
        8.0 * (2.0 * whole + (row & 1).astype(F32)) + 3.5,
        4.0 * (16.0 * quarter + (row & 15).astype(F32)) + 1.5,
    )
    freq_t, freq_h, freq_w, sign = (freq_ref[i : i + 1, :] for i in range(4))
    angles = t * freq_t + h * freq_h + w * freq_w
    return jnp.cos(angles), jnp.sin(angles) * sign


def table_kernel(kinds_ref, freq_ref, after_ref, table_ref):
    del after_ref
    table_ref[0], table_ref[1] = row_angles(kinds_ref, freq_ref)


def make_table(kinds, freqs, after):
    return pl.pallas_call(
        table_kernel,
        out_shape=jax.ShapeDtypeStruct((2, 128, HEAD_DIM), F32),
        in_specs=[SMEM, VMEM, ANY],
        out_specs=VMEM,
        compiler_params=params(),
        cost_estimate=cost(1e5, 1e3),
        name="table",
    )(kinds, freqs, after)


def far_kernel(
    mine0,
    mine1,
    mine2,
    mine3,
    theirs0,
    theirs1,
    theirs2,
    theirs3,
    mod_ref,
    w_ref,
    perm_ref,
    table_ref,
    out_ref,
    full_ref,
):
    place_columns(((mine0, mine1, mine2, mine3), (theirs0, theirs1, theirs2, theirs3)), full_ref)
    heads = out_ref.shape[2] // HEAD_DIM
    x = full_ref[...].astype(F32)
    x = x - jnp.mean(x, axis=1, keepdims=True)
    x = x * lax.rsqrt(jnp.mean(x * x, axis=1, keepdims=True) + EPS)
    x = (x * (1.0 + mod_ref[1:2, :]) + mod_ref[0:1, :]).astype(BF)
    raw_keys = dot(x, w_ref[1])
    out_ref[1] = dot(x, w_ref[2]).astype(BF)
    cosine, sine = table_ref[0], table_ref[1]
    for h in range(heads):
        at = slice(HEAD_DIM * h, HEAD_DIM * (h + 1))
        raw = raw_keys[:, at]
        raw = raw * lax.rsqrt(jnp.mean(raw * raw, axis=1, keepdims=True) + EPS)
        high, rest = split(raw)
        raw = dot(high, perm_ref[...]) + dot(rest, perm_ref[...])
        out_ref[0, :, at] = (raw * cosine + pltpu.roll(raw, 64, 1) * sine).astype(BF)


def make_far(gathered, modulation, w_qkv, perm, table):
    columns = w_qkv.shape[2]
    return pl.pallas_call(
        far_kernel,
        out_shape=jax.ShapeDtypeStruct((2, 128, columns), BF),
        in_specs=[VMEM] * 12,
        out_specs=VMEM,
        scratch_shapes=[pltpu.VMEM((128, w_qkv.shape[1]), BF)],
        compiler_params=params(),
        cost_estimate=cost(2e9, 1e7),
        name="far",
    )(*gathered[0], *gathered[1], modulation, w_qkv, perm, table)


def middle_kernel(far_ref, query_ref, num_ref, den_ref, out_ref, sum_ref):
    heads = query_ref.shape[0] // HEAD_DIM
    for h in range(heads):
        at = slice(HEAD_DIM * h, HEAD_DIM * (h + 1))
        weights = jnp.exp2(dot(far_ref[0, :, at], query_ref[at, :]))
        sum_ref[h : h + 1, :] = den_ref[h : h + 1, :] + jnp.sum(weights, axis=0, keepdims=True)
        out_ref[at, :] = num_ref[at, :] + dot(
            far_ref[1, :, at], weights.astype(BF), ((0,), (0,))
        )


def attend_first(far, queries, numerator, denominator):
    return pl.pallas_call(
        middle_kernel,
        out_shape=(
            jax.ShapeDtypeStruct(numerator.shape, F32),
            jax.ShapeDtypeStruct(denominator.shape, F32),
        ),
        in_specs=[VMEM] * 4,
        out_specs=(VMEM, VMEM),
        compiler_params=params(),
        cost_estimate=cost(2e9, 1e6, 1e6),
        name="first",
    )(far, queries, numerator, denominator)


def history_kernel(far1, query_ref, num_ref, den_ref, out0, out1, out2, out3):
    heads = query_ref.shape[0] // HEAD_DIM
    count = query_ref.shape[1]
    outs = (out0, out1, out2, out3)
    rows = lax.broadcasted_iota(jnp.int32, (16, count), 0)
    tail = jnp.zeros((16, count), F32)
    for h in range(heads):
        at = slice(HEAD_DIM * h, HEAD_DIM * (h + 1))
        fars = (far1,)
        keys = jnp.concatenate([far[0, :, at] for far in fars], axis=0)
        values = jnp.concatenate([far[1, :, at] for far in fars], axis=0)
        weights = jnp.exp2(dot(keys, query_ref[at, :]))
        high, rest = split(den_ref[h : h + 1, :] + jnp.sum(weights, axis=0, keepdims=True))
        tail = jnp.where(rows == h, high.astype(F32), tail)
        tail = jnp.where(rows == heads + h, rest.astype(F32), tail)
        part = num_ref[at, :] + dot(values, weights.astype(BF), ((0,), (0,)))
        for d, out in enumerate(outs):
            out[at, :] = part[:, 128 * d : 128 * d + 128].astype(out.dtype)
    for d, out in enumerate(outs):
        out[HEAD_DIM * heads :, :] = tail[:, 128 * d : 128 * d + 128].astype(out.dtype)


def attend_history(fars, queries, numerator, denominator):
    columns = queries.shape[0]
    return pl.pallas_call(
        history_kernel,
        out_shape=tuple(jax.ShapeDtypeStruct((columns + 16, 128), t) for t in (F32, BF, BF, BF)),
        in_specs=[VMEM] * 4,
        out_specs=tuple([VMEM] * 4),
        compiler_params=params(),
        cost_estimate=cost(2e9, 4e6, 1e6),
        name="history",
    )(*fars, queries, numerator, denominator)


def combine_kernel(part0, part1, part2, part3, out_ref):
    columns = out_ref.shape[1]
    heads = columns // HEAD_DIM
    total = sum(part[...].astype(F32) for part in (part0, part1, part2, part3))
    for h in range(heads):
        at = slice(HEAD_DIM * h, HEAD_DIM * (h + 1))
        low = columns + heads + h
        denominator = total[columns + h : columns + h + 1] + total[low : low + 1]
        out_ref[:, at] = jnp.transpose(total[at] / denominator).astype(BF)


def combine(parts):
    return pl.pallas_call(
        combine_kernel,
        out_shape=jax.ShapeDtypeStruct((128, parts[0].shape[0] - 16), BF),
        in_specs=[VMEM] * 4,
        out_specs=VMEM,
        compiler_params=params(),
        cost_estimate=cost(1e7, 2e6),
        name="combine",
    )(*parts)


def per_device(
    history, section, slab_kernel, patch_fine, patch_mid, patch_coarse, modulation, w_qkv
):
    frames = lax.axis_size("frame")
    cos_table, sin_table = section_tables(frames, section.shape[0])
    cosine, sine = jnp.asarray(cos_table), jnp.asarray(sin_table)
    perm = jnp.asarray(head_permutation(), BF)
    lane_table = lane_frequencies()
    freqs = jnp.asarray(lane_table)
    times = jnp.asarray(np.repeat(lane_table[0, 0:8, None], 128, axis=1))

    sent, patch_fine = prepare(slab_kernel, history, section, patch_fine)
    received = lax.all_to_all(sent, "frame", 0, 0, tiled=True)
    fine = along_head(patch_fine)
    table = make_table(slab_kernel, freqs, sent)
    features = embed(slab_kernel, received, patch_mid, patch_coarse, (*fine[1:], table))
    mine = along_head(features)
    gathered = mine, tuple(other_core(block) for block in mine)
    far = make_far(gathered, modulation, w_qkv, perm, table)
    far2, far1, far3 = (along_x(far, d) for d in (2, 1, 3))
    fine_same = stack(fine, features)
    folded, gram = fold(fine_same, other_core(fine_same), modulation, w_qkv, perm, far)
    queries, keys, values = make_tokens(
        slab_kernel, gathered, folded, gram, cosine, sine, times
    )
    numerator, denominator = attend_near(queries, keys, values, far)
    numerator, denominator = attend_first(far2, queries, numerator, denominator)
    numerator, denominator = attend_first(far3, queries, numerator, denominator)
    fars = [far1]
    parts = attend_history(fars, queries, numerator, denominator)
    part2 = along_y(parts[2], 2)
    return combine([parts[0], along_y(parts[1], 1), part2, along_y(parts[3], 3)])


def solution(mesh):
    in_specs = (
        P("frame", None, None, None),
        P("frame", None),
        P(),
        P(None, ("head", "fsdp")),
        P(None, ("head", "fsdp")),
        P(None, ("head", "fsdp")),
        P(),
        P(None, None, ("head", "fsdp")),
    )
    out_specs = P("frame", ("head", "fsdp"))
    return jax.shard_map(
        per_device, mesh=mesh, in_specs=in_specs, out_specs=out_specs, check_vma=False
    )
```
